128 devices in a mesh: grp: 4 (over z_lo, core), dp: 32 (over z_hi, x, y).
Axes of the slice: x: 4, y: 4, z: 4 (z_hi: 2, z_lo: 2; z = z_hi * 2 + z_lo), core: 2. Of those that a mesh axis runs over, the one named last changes fastest.
Arguments:
- hidden: bfloat16 [49152, 4096], P(('grp', 'dp')), may hold values from -120 to 120
- w_proj: bfloat16 [4096, 1024], replicated, may hold values from -0.09375 to 0.09375
- pairing: int32 [49152], P(('grp', 'dp')), may hold values from 0 to 12287, as said below
- loss_scale: float32 [], replicated, may hold values from 32 to 128
Outputs:
- grad_hidden: bfloat16 [49152, 4096], P(('grp', 'dp'))
- grad_proj: bfloat16 [4096, 1024], P(('grp', 'dp'))
The draws below stay inside these ranges and needn't reach their ends.
Inputs may be any that keep to these rules, and one draw needn't show every extreme that they name: `pairing`: the partner of row i of group g lies in the group whose index differs in the lowest bit, within the same aligned block of 384 rows as i; the partner's partner is row i again.
All inputs are finite; a program needn't handle non-finite values.
Results may differ from the reference program's by a relative error of at most 0.0072.
Values sent between devices are 32-bit elements; how exact they have to be, the bound alone decides.
A program may use at most 192 MiB of HBM per device.

```python
import math
import jax
import jax.numpy as jnp
import numpy as np
from jax import lax

FF = 4096
EMB = 1024
ROW_DEV = 384
ROWS = 12288
TOTAL = 49152
N_GRP = 4
N_DP = 32


def draw_hidden(key, part):
    key = jax.random.fold_in(key, 11)
    key_rows = jax.random.fold_in(key, 1)
    key_cols = jax.random.fold_in(key, 2)
    key_body = jax.random.fold_in(key, 3)
    position = (jnp.arange(TOTAL) % ROWS).astype(jnp.float32) / ROWS
    row_scale = jnp.power(10.0, 0.5 * position + 0.5 * jax.random.uniform(key_rows, (TOTAL,)))
    col_scale = jnp.power(10.0, jax.random.uniform(key_cols, (FF,)))
    sample = jax.random.normal(key_body, (TOTAL, FF))
    sample = jnp.clip(sample, -4.0, 4.0)
    return (0.3 * sample * row_scale[:, None] * col_scale[None, :]).astype(jnp.bfloat16)


def draw_pairing(key, part):
    key = jax.random.fold_in(key, 23)
    scores = jax.random.randint(key, (N_GRP // 2, N_DP, ROW_DEV), 0, 2 ** 19) * ROW_DEV + jnp.arange(ROW_DEV)
    forward = jnp.argsort(scores, axis=-1, stable=True).astype(jnp.int32)
    backward = jnp.argsort(forward, axis=-1, stable=True).astype(jnp.int32)
    offsets = (jnp.arange(N_DP) * ROW_DEV).astype(jnp.int32)[None, :, None]
    stacked = jnp.stack([forward + offsets, backward + offsets], axis=1)
    return stacked.reshape(TOTAL).astype(jnp.int32)


def normal_values(rng, extent, deviation, most, kind=jnp.bfloat16):
    drawn = deviation * jax.random.normal(rng, extent, jnp.float32)
    return jnp.clip(drawn, min=-most, max=most).astype(kind)


def setup_inputs(seed: int = 0) -> dict:
    seeds = jax.random.split(jax.random.key(seed), 5)
    return {
        "hidden": draw_hidden(jax.random.fold_in(seeds[4], 71), 0),
        "w_proj": normal_values(seeds[1], (FF, EMB), FF ** -0.5, 0.09375),
        "pairing": draw_pairing(jax.random.fold_in(seeds[4], 71), 0),
        "loss_scale": jnp.clip(jnp.exp(jax.random.uniform(seeds[3], (), jnp.float32, math.log(32.0), math.log(128.0))), 32.0, 128.0),
    }


precise = lax.Precision.HIGHEST

def whitening_map(covariance):
    factor = jnp.linalg.cholesky(covariance)
    identity = jnp.eye(covariance.shape[0], dtype=covariance.dtype)
    return lax.linalg.triangular_solve(factor, identity, left_side=True, lower=True)

def group_normals(projected):
    column_mean = lax.optimization_barrier(jnp.sum(projected, axis=0)) / ROWS
    centered = projected - column_mean
    covariance = jnp.matmul(centered.T, centered, precision=precise) / ROWS
    inverse = whitening_map(covariance)
    whitened = jnp.matmul(centered, inverse.T, precision=precise)
    radius = jnp.sqrt(lax.optimization_barrier(jnp.sum(whitened * whitened, axis=1, keepdims=True)) + 1e-06)
    return whitened / radius

def pair_loss(projected, pairing, loss_scale):
    grouped = projected.reshape(N_GRP, ROWS, EMB)
    normals = jax.vmap(group_normals)(grouped)
    partner_group = normals[np.arange(N_GRP) ^ 1]
    row_index = pairing.reshape(N_GRP, ROWS)
    partner = jax.vmap(lambda block, which: block[which])(partner_group, row_index)
    difference = normals - partner
    return loss_scale * jnp.sum(difference * difference)

def reference(hidden, w_proj, pairing, loss_scale):
    active = jax.nn.relu(hidden)
    projected = jnp.dot(active.astype(jnp.float32), w_proj.astype(jnp.float32), preferred_element_type=jnp.float32)
    loss_value, pull_back = jax.vjp(lambda rows: pair_loss(rows, pairing, loss_scale), projected)
    grad_float, = pull_back(jnp.ones_like(loss_value))
    grad_rounded = grad_float.astype(jnp.bfloat16)
    grad_active = lax.dot_general(grad_rounded.astype(jnp.float32), w_proj.astype(jnp.float32), (((1,), (1,)), ((), ())), preferred_element_type=jnp.float32)
    grad_hidden = jnp.where(hidden > 0, grad_active, 0.0).astype(jnp.bfloat16)
    grad_proj = lax.dot_general(active.astype(jnp.float32), grad_rounded.astype(jnp.float32), (((0,), (0,)), ((), ())), preferred_element_type=jnp.float32)
    return (grad_hidden, grad_proj.astype(jnp.bfloat16))
```

```python
import functools

import jax
import jax.numpy as jnp
from jax import lax
from jax.experimental import pallas as pl
from jax.experimental.pallas import tpu as pltpu
from jax.sharding import PartitionSpec as P

MESH = pl.DeviceIdType.MESH
VMEM = pl.BlockSpec(memory_space=pltpu.VMEM)


class Place:
    def __init__(self):
        grp, dp = lax.axis_index("grp"), lax.axis_index("dp")
        self.core = lax.rem(grp, 2)
        self.z = (dp // 16) * 2 + grp // 2
        self.x = lax.rem(dp // 4, 4)
        self.y = lax.rem(dp, 4)

    def device(self, axis=None, step=0, core=None):
        where = {"x": self.x, "y": self.y, "z": self.z}
        if axis is not None:
            where[axis] = lax.rem(where[axis] + step, 4)
        core = self.core if core is None else core
        z = where["z"]
        return (lax.rem(z, 2) * 2 + core, (z // 2) * 16 + where["x"] * 4 + where["y"])

    def greet(self, devices):
        barrier = pltpu.get_barrier_semaphore()
        for device in devices:
            pl.semaphore_signal(barrier, inc=1, device_id=device, device_id_type=MESH)
        pl.semaphore_wait(barrier, len(devices))


def remote(src, dst, send, recv, device):
    copy = pltpu.make_async_remote_copy(
        src_ref=src, dst_ref=dst, send_sem=send, recv_sem=recv, device_id=device, device_id_type=MESH
    )
    copy.start()
    return copy


class RingSum:
    def __init__(self, place, axis, part, relay, final, send, recv):
        self.me = getattr(place, axis)
        self.right, self.left = place.device(axis, 1), place.device(axis, 3)
        self.next, self.far, self.prev = (lax.rem(self.me + s, 4) for s in (1, 2, 3))
        self.part, self.relay, self.final, self.send, self.recv = part, relay, final, send, recv
        self.copies = []

    def copy(self, src, dst, device):
        i = len(self.copies)
        self.copies.append(remote(src, dst, self.send.at[i], self.recv.at[i], device))

    def start_far(self):
        self.copy(self.part(self.far, 0), self.relay.at[0], self.right)
        self.copy(self.part(self.far, 1), self.relay.at[1], self.left)

    def start_near(self):
        self.copy(self.part(self.next, 1), self.final.at[0, 1], self.right)
        self.copy(self.part(self.prev, 0), self.final.at[1, 0], self.left)

    def pass_on(self):
        self.copies[0].wait_recv()
        self.relay[0] += self.part(self.next, 0)[...]
        self.copy(self.relay.at[0], self.final.at[0, 0], self.right)
        self.copies[1].wait_recv()
        self.relay[1] += self.part(self.prev, 1)[...]
        self.copy(self.relay.at[1], self.final.at[1, 1], self.left)

    def finish(self):
        for copy in self.copies[2:]:
            copy.wait_recv()
        for h in (0, 1):
            yield self.part(self.me, h)[...] + self.final[0, h] + self.final[1, h]

    def drain(self):
        for copy in self.copies:
            copy.wait_send()


class RingShare(RingSum):
    def __init__(self, place, axis, part, send, recv):
        super().__init__(place, axis, part, None, None, send, recv)

    def start(self):
        for h, device in ((0, self.right), (1, self.left), (1, self.right), (0, self.left)):
            part = self.part(self.me, h)
            self.copy(part, part, device)

    def pass_on(self):
        self.copies[0].wait_recv()
        part = self.part(self.prev, 0)
        self.copy(part, part, self.right)
        self.copies[1].wait_recv()
        part = self.part(self.next, 1)
        self.copy(part, part, self.left)

    def finish(self):
        for copy in self.copies[2:]:
            copy.wait_recv()


def small_sum_kernel(value, out, total, got_x, got_y, got_z, send, recv):
    place = Place()
    across = {axis: [place.device(axis, step) for step in (1, 2, 3)] for axis in "xy"}
    opposite = place.device("z", 2)
    place.greet(across["x"] + across["y"] + [opposite])
    copies = []

    def exchange(src, got, devices):
        mine = []
        for i, device in enumerate(devices):
            k = len(copies)
            mine.append(remote(src, got.at[i], send.at[k], recv.at[k], device))
            copies.append(mine[-1])
        for copy in mine:
            copy.wait_recv()
        return src[...] + sum(got[i] for i in range(len(devices)))

    total[0] = exchange(value, got_x, across["x"])
    total[1] = exchange(total.at[0], got_y, across["y"])
    out[...] = exchange(total.at[1], got_z, [opposite])
    for copy in copies:
        copy.wait_send()


def small_sum(value, collective_id):
    shape = value.shape
    return pl.pallas_call(
        small_sum_kernel,
        out_shape=jax.ShapeDtypeStruct(shape, jnp.float32),
        in_specs=[VMEM],
        out_specs=VMEM,
        scratch_shapes=[
            pltpu.VMEM((2, *shape), jnp.float32),
            pltpu.VMEM((3, *shape), jnp.float32),
            pltpu.VMEM((3, *shape), jnp.float32),
            pltpu.VMEM((1, *shape), jnp.float32),
            pltpu.SemaphoreType.DMA((7,)),
            pltpu.SemaphoreType.DMA((7,)),
        ],
        compiler_params=pltpu.CompilerParams(collective_id=collective_id, has_side_effects=True),
    )(value)


def all_sum_kernel(value, out, relay1, final1, sum1, relay2, final2, sum2, got, send, recv):
    place = Place()
    plans = (("x", "y"), ("y", "x"))
    opposite = place.device("z", 2)
    place.greet([place.device(axis, step) for axis in "xy" for step in (1, 3)] + [opposite])

    def lane(p, stage):
        i = p * 5 + stage
        return send.at[i], recv.at[i]

    first = [
        RingSum(place, axes[0], lambda k, h, p=p: value.at[p, k, h], relay1.at[p], final1.at[p], *lane(p, 0))
        for p, axes in enumerate(plans)
    ]
    for ring in first:
        ring.start_far()
    for ring in first:
        ring.start_near()
    for ring in first:
        ring.pass_on()
    second = []
    for p, axes in enumerate(plans):
        for h, half in enumerate(first[p].finish()):
            sum1[p, h] = half
        second.append(
            RingSum(
                place,
                axes[1],
                lambda k, h, p=p: sum1.at[p, k // 2, lax.rem(k, 2), h],
                relay2.at[p],
                final2.at[p],
                *lane(p, 1),
            )
        )
        second[p].start_far()
        second[p].start_near()
    for ring in second:
        ring.pass_on()
    across = []
    for p in range(2):
        for h, half in enumerate(second[p].finish()):
            sum2[p, h] = half
        across.append(remote(sum2.at[p], got.at[p], send.at[p * 5 + 2, 0], recv.at[p * 5 + 2, 0], opposite))
    third = []
    for p, axes in enumerate(plans):
        across[p].wait_recv()
        outer, inner = getattr(place, axes[0]), getattr(place, axes[1])
        out[p, outer, inner // 2, lax.rem(inner, 2)] = sum2[p] + got[p]
        third.append(
            RingShare(
                place,
                axes[1],
                lambda k, h, p=p, outer=outer: out.at[p, outer, k // 2, lax.rem(k, 2), h],
                *lane(p, 3),
            )
        )
        third[p].start()
    for ring in third:
        ring.pass_on()
    fourth = []
    for p, axes in enumerate(plans):
        third[p].finish()
        fourth.append(RingShare(place, axes[0], lambda k, h, p=p: out.at[p, k, h], *lane(p, 4)))
        fourth[p].start()
    for ring in fourth:
        ring.pass_on()
    for ring in fourth:
        ring.finish()
    for ring in first + second + third + fourth:
        ring.drain()
    for copy in across:
        copy.wait_send()


def all_sum(value, collective_id):
    shape = value.shape
    piece = value.size // (2 * 4 * 4 * 2 * 128)
    cut = (2, 4, 2, 2, 2, piece, 128)
    total = pl.pallas_call(
        all_sum_kernel,
        out_shape=jax.ShapeDtypeStruct(cut, jnp.float32),
        in_specs=[VMEM],
        out_specs=VMEM,
        scratch_shapes=[
            pltpu.VMEM((2, 2, 2, 2, piece, 128), jnp.float32),
            pltpu.VMEM((2, 2, 2, 2, 2, piece, 128), jnp.float32),
            pltpu.VMEM((2, 2, 2, 2, piece, 128), jnp.float32),
            pltpu.VMEM((2, 2, piece, 128), jnp.float32),
            pltpu.VMEM((2, 2, 2, piece, 128), jnp.float32),
            pltpu.VMEM((2, 2, piece, 128), jnp.float32),
            pltpu.VMEM((2, 2, piece, 128), jnp.float32),
            pltpu.SemaphoreType.DMA((10, 6)),
            pltpu.SemaphoreType.DMA((10, 6)),
        ],
        compiler_params=pltpu.CompilerParams(collective_id=collective_id, has_side_effects=True),
    )(value.reshape(cut))
    return total.reshape(shape)


ORDERS = (("x", "y", "z"), ("y", "z", "x"), ("z", "x", "y"))
WIDTHS = (384, 384, 256)


def weight_kernel(active_here, active_there, grad_here, grad_there, out, active, grad, *scratch):
    send, recv = scratch[-2:]
    place = Place()
    rows = grad_here.shape[0]
    active[:rows] = active_here[...]
    active[rows:] = active_there[...].astype(active.dtype)
    grad[:rows] = grad_here[...].astype(grad.dtype)
    grad[rows:] = grad_there[...].astype(grad.dtype)
    place.greet([place.device(axis, step) for axis in "xyz" for step in (1, 3)])
    parts, relays, finals, sums = [], [], [], []
    for p in range(3):
        parts.append(scratch[9 * p])
        relays.append(scratch[9 * p + 1 : 9 * p + 4])
        finals.append(scratch[9 * p + 4 : 9 * p + 7])
        sums.append(scratch[9 * p + 7 : 9 * p + 9])

    @pl.loop(0, 4)
    def _(z):
        start = lax.rem(z, 2) * 1024 + (z // 2) * 512
        columns = active[:, pl.ds(pl.multiple_of(start, 512), 512)]
        begin = 0
        for p, width in enumerate(WIDTHS):
            product = lax.dot_general(
                columns,
                grad[:, begin : begin + width],
                (((0,), (0,)), ((), ())),
                preferred_element_type=jnp.float32,
            )
            begin += width
            for x in range(4):
                for y in range(4):
                    row = x * 128 + y * 32
                    block = product[row : row + 32].reshape(2, 16, width)
                    if p == 0:
                        parts[p][x, y // 2, y % 2, z // 2, lax.rem(z, 2)] = block
                    elif p == 1:
                        parts[p][y, z // 2, lax.rem(z, 2), x // 2, x % 2] = block
                    else:
                        parts[p][z, x // 2, x % 2, y // 2, y % 2] = block

    rings = []
    for stage in range(3):
        now = []
        for p, axes in enumerate(ORDERS):
            if stage == 0:
                part = lambda k, h, p=p: parts[p].at[k, h]
            else:
                for h, half in enumerate(rings[-1][p].finish()):
                    sums[p][stage - 1][h] = half
                part = lambda k, h, p=p, s=stage: sums[p][s - 1].at[k // 2, lax.rem(k, 2), h]
            i = p * 3 + stage
            ring = RingSum(place, axes[stage], part, relays[p][stage], finals[p][stage], send.at[i], recv.at[i])
            ring.start_far()
            ring.start_near()
            now.append(ring)
        for ring in now:
            ring.pass_on()
        rings.append(now)
    begin = 0
    for p, width in enumerate(WIDTHS):
        for h, half in enumerate(rings[2][p].finish()):
            out[16 * h : 16 * h + 16, begin : begin + width] = half.astype(out.dtype)
        begin += width
    for now in rings:
        for ring in now:
            ring.drain()


def weight_sum(active_here, active_there, grad_here, grad_there, collective_id):
    scratch = []
    inputs = (active_here, active_there, grad_here, grad_there)
    rows = 2 * grad_here.shape[0]
    whole = [pltpu.VMEM((rows, 2048), jnp.bfloat16), pltpu.VMEM((rows, 1024), jnp.bfloat16)]
    for width in WIDTHS:
        tail = (2, 16, width)
        scratch += [
            pltpu.VMEM(shape + tail, jnp.float32)
            for shape in [
                (4, 2, 2, 2, 2),
                (2, 2, 2, 2),
                (2, 2),
                (2,),
                (2, 2, 2, 2, 2),
                (2, 2, 2),
                (2,),
                (2, 2, 2, 2),
                (2, 2),
            ]
        ]
    for p in range(3):
        scratch[9 * p + 3] = pltpu.VMEM((2, 16, WIDTHS[p]), jnp.float32)
        scratch[9 * p + 6] = pltpu.VMEM((2, 2, 16, WIDTHS[p]), jnp.float32)
    return pl.pallas_call(
        weight_kernel,
        out_shape=jax.ShapeDtypeStruct((32, 1024), jnp.bfloat16),
        in_specs=[VMEM] * 4,
        out_specs=VMEM,
        scratch_shapes=whole + scratch + [pltpu.SemaphoreType.DMA((9, 6)), pltpu.SemaphoreType.DMA((9, 6))],
        compiler_params=pltpu.CompilerParams(
            collective_id=collective_id, has_side_effects=True, vmem_limit_bytes=56 * 2**20
        ),
    )(*inputs)


precise = lax.Precision.HIGHEST
N, B = 1024, 128


def spread_row(tile, row):
    return jnp.broadcast_to(tile[row : row + 1, :], (8, B))


def spread_column(tile, column):
    return jnp.broadcast_to(tile[:, column : column + 1], (8, B))


def leaf_inverse(block, pivots=4):
    sub = lax.broadcasted_iota(jnp.int32, (8, B), 0)
    lane = lax.broadcasted_iota(jnp.int32, (8, B), 1)
    a = [block[8 * g : 8 * g + 8, :] for g in range(16)]
    w = [jnp.where(lane == sub + 8 * g, 1.0, 0.0) for g in range(16)]
    done = []
    for g in range(16):
        finished = jnp.zeros((8, B), jnp.float32)
        for r in range(0, 8, pivots):
            j = 8 * g + r
            span = range(pivots)
            here = [spread_column(a[g], j + k) for k in span]
            rows = [spread_row(a[g], r + k) for k in span]
            wrows = [spread_row(w[g], r + k) for k in span]
            d = {(l, k): spread_row(here[k], r + l) for k in span for l in span if l >= k}
            low, inv = {}, []
            for k in span:
                inv.append(1.0 / d[k, k])
                for l in range(k + 1, pivots):
                    low[l, k] = d[l, k] * inv[k]
                for l in range(k + 1, pivots):
                    for m in range(k + 1, l + 1):
                        d[l, m] = d[l, m] - low[l, k] * d[m, k]
            for k in span:
                for l in range(k):
                    rows[k] = rows[k] - low[k, l] * rows[l]
                    wrows[k] = wrows[k] - low[k, l] * wrows[l]
            q = [rows[k] * inv[k] for k in span]
            qw = [wrows[k] * inv[k] for k in span]
            for k in reversed(span):
                for l in range(k + 1, pivots):
                    q[k] = q[k] - low[l, k] * q[l]
                    qw[k] = qw[k] - low[l, k] * qw[l]
            for k in span:
                finished = jnp.where(sub == r + k, wrows[k] * lax.rsqrt(d[k, k]), finished)
            if r + pivots < 8:
                mult = [jnp.where(sub >= r + pivots, here[k], 0.0) for k in span]
                for k in span:
                    a[g] = a[g] - mult[k] * q[k]
                    w[g] = w[g] - mult[k] * qw[k]
            for t in range(g + 1, 16):
                mult = [spread_column(a[t], j + k) for k in span]
                for k in span:
                    a[t] = a[t] - mult[k] * q[k]
                    w[t] = w[t] - mult[k] * qw[k]
        done.append(finished)
    return done


def dot(a, b, over):
    return lax.dot_general(a, b, (over, ((), ())), precision=precise, preferred_element_type=jnp.float32)


def inverse_kernel(packed, out, top, work):
    for i in range(8):
        for j in range(i + 1):
            block = packed[i * (i + 1) // 2 + j]
            out[B * i : B * i + B, B * j : B * j + B] = block
            if j < i:
                out[B * j : B * j + B, B * i : B * i + B] = block.T
    lane = lax.broadcasted_iota(jnp.int32, (B, B), 1)
    sub = lax.broadcasted_iota(jnp.int32, (B, B), 0)
    unit = jnp.where(lane == sub, 1.0, 0.0)

    @pl.loop(0, 8)
    def _(k):
        here = pl.ds(pl.multiple_of(k * B, B), B)
        for g, tile in enumerate(leaf_inverse(out[here, here])):
            work[8 * g : 8 * g + 8, :] = tile
        out[here, here] = unit
        top[...] = dot(work[...], out[here, :], ((1,), (0,)))
        out[here, :] = top[...]

        @pl.loop(k + 1, 8)
        def _(i):
            there = pl.ds(pl.multiple_of(i * B, B), B)
            out[there, here] = jnp.zeros((B, B), jnp.float32)
            out[there, :] -= dot(top[:, there], top[...], ((0,), (0,)))

    for i in range(7):
        out[B * i : B * i + B, B * (i + 1) :] = jnp.zeros((B, N - B * (i + 1)), jnp.float32)


def factor_inverse(packed):
    return pl.pallas_call(
        inverse_kernel,
        out_shape=jax.ShapeDtypeStruct((N, N), jnp.float32),
        in_specs=[VMEM],
        out_specs=VMEM,
        scratch_shapes=[pltpu.VMEM((B, N), jnp.float32), pltpu.VMEM((B, B), jnp.float32)],
        compiler_params=pltpu.CompilerParams(vmem_limit_bytes=32 * 2**20),
    )(packed)


def blocks_kernel(left, right, extra, out):
    row = lax.broadcasted_iota(jnp.int32, (B, B), 0)
    lane = lax.broadcasted_iota(jnp.int32, (B, B), 1)
    for i in range(8):
        width = B * (i + 1)
        wide = dot(left[:, B * i : B * i + B], right[:, :width], ((0,), (0,)))
        for j in range(i + 1):
            block = wide[:, B * j : B * j + B]
            if extra is not None and j == i:
                line = jnp.broadcast_to(extra[i : i + 1, :], (B, B))
                first = jnp.broadcast_to(line[:, :1], (B, B))
                block = jnp.where((row == 0) & (lane > 0), line, block)
                block = jnp.where((row == 1) & (lane == B - 1), first, block)
            out[i * (i + 1) // 2 + j] = block


def lower_blocks(left, right, extra=None):
    operands = (left, right) if extra is None else (left, right, extra)
    kernel = blocks_kernel if extra is not None else lambda a, b, out: blocks_kernel(a, b, None, out)
    return pl.pallas_call(
        kernel,
        out_shape=jax.ShapeDtypeStruct((36, B, B), jnp.float32),
        in_specs=[VMEM] * len(operands),
        out_specs=VMEM,
        compiler_params=pltpu.CompilerParams(vmem_limit_bytes=40 * 2**20),
    )(*operands)


def whiten_kernel(centered, inverse, out):
    for i in range(4):
        width = 256 * (i + 1)
        out[:, width - 256 : width] = dot(centered[:, :width], inverse[width - 256 : width, :width], ((1,), (1,)))


def whiten(centered, inverse):
    return pl.pallas_call(
        whiten_kernel,
        out_shape=jax.ShapeDtypeStruct(centered.shape, jnp.float32),
        in_specs=[VMEM, VMEM],
        out_specs=VMEM,
        compiler_params=pltpu.CompilerParams(vmem_limit_bytes=40 * 2**20),
    )(centered, inverse)


def rows_kernel(count, grad_white, whitened, packed, inverse, out, sym, mixed):
    row = lax.broadcasted_iota(jnp.int32, (B, B), 0)
    lane = lax.broadcasted_iota(jnp.int32, (B, B), 1)
    for i in range(8):
        for j in range(i + 1):
            block = packed[i * (i + 1) // 2 + j]
            if j < i:
                sym[B * i : B * i + B, B * j : B * j + B] = block
                sym[B * j : B * j + B, B * i : B * i + B] = block.T
            else:
                low = jnp.where(row >= lane, block, 0.0)
                sym[B * i : B * i + B, B * i : B * i + B] = low + jnp.where(row > lane, block, 0.0).T
                total = jnp.where(lane[:1] > 0, block[:1, :], block[1:2, B - 1 :])
                mixed[:, B * i : B * i + B] = grad_white[:, B * i : B * i + B] - total / count
    for i in range(4):
        columns = slice(256 * i, 256 * i + 256)
        mixed[:, columns] -= dot(whitened[...], sym[:, columns], ((1,), (0,))) / count
    for i in range(4):
        columns = slice(256 * i, 256 * i + 256)
        out[:, columns] = dot(mixed[:, 256 * i :], inverse[256 * i :, columns], ((1,), (0,)))


def gradient_rows(count, grad_white, whitened, packed, inverse):
    return pl.pallas_call(
        functools.partial(rows_kernel, count),
        out_shape=jax.ShapeDtypeStruct(whitened.shape, jnp.float32),
        in_specs=[VMEM] * 4,
        out_specs=VMEM,
        scratch_shapes=[pltpu.VMEM((N, N), jnp.float32), pltpu.VMEM(whitened.shape, jnp.float32)],
        compiler_params=pltpu.CompilerParams(vmem_limit_bytes=48 * 2**20),
    )(grad_white, whitened, packed, inverse)


def from_other_core(value):
    pairs = [(source, source ^ 1) for source in range(lax.axis_size("grp"))]
    return lax.ppermute(value, "grp", pairs)


def local(hidden, w_proj, pairing, loss_scale):
    rows, hidden_width = hidden.shape
    count = rows * lax.axis_size("dp")
    core = lax.rem(lax.axis_index("grp"), 2)
    active = jax.nn.relu(hidden)
    by_core = active.reshape(rows, 2, 2, hidden_width // 4)
    mine = lax.dynamic_index_in_dim(by_core, core, 2, keepdims=False).reshape(rows, hidden_width // 2)
    other = lax.dynamic_index_in_dim(by_core, 1 - core, 2, keepdims=False).reshape(rows, hidden_width // 2)
    arrived = from_other_core(other.astype(jnp.float32))

    projected = jnp.dot(active, w_proj, preferred_element_type=jnp.float32)
    column_sum = small_sum(jnp.sum(projected, axis=0).reshape(8, B), 0)
    centered = projected - column_sum.reshape(N) / count
    covariance = all_sum(lower_blocks(centered, centered).reshape(36 * B, B), 1) / count
    inverse = factor_inverse(covariance.reshape(36, B, B))
    whitened = whiten(centered, inverse)
    radius = jnp.sqrt(jnp.sum(whitened * whitened, axis=1, keepdims=True) + 1e-06)
    normals = whitened / radius
    partner_block = from_other_core(normals)
    partner = jnp.take(partner_block, pairing - lax.axis_index("dp") * rows, axis=0)
    grad_normals = 4.0 * loss_scale * (normals - partner)
    grad_white = (
        grad_normals - normals * jnp.sum(normals * grad_normals, axis=1, keepdims=True)
    ) / radius
    white_total = jnp.sum(grad_white, axis=0).reshape(8, B)
    mixed = all_sum(lower_blocks(grad_white, whitened, white_total).reshape(36 * B, B), 2)
    grad_float = gradient_rows(count, grad_white, whitened, mixed.reshape(36, B, B), inverse)
    grad_rounded = grad_float.astype(jnp.bfloat16)
    grad_weight = weight_sum(mine, arrived, grad_float, from_other_core(grad_float), 3)
    grad_active = lax.dot_general(
        grad_rounded, w_proj, (((1,), (1,)), ((), ())), preferred_element_type=jnp.float32
    )
    grad_hidden = jnp.where(hidden > 0, grad_active, 0.0).astype(jnp.bfloat16)
    return (grad_hidden, grad_weight)


def solution(mesh):
    return jax.shard_map(
        local,
        mesh=mesh,
        in_specs=(P(("grp", "dp"), None), P(), P(("grp", "dp")), P()),
        out_specs=(P(("grp", "dp"), None), P(("grp", "dp"), None)),
        check_vma=False,
    )
```

```python
import functools

import jax
import jax.numpy as jnp
from jax import lax
from jax.experimental import pallas as pl
from jax.experimental.pallas import tpu as pltpu
from jax.sharding import PartitionSpec as P

MESH = pl.DeviceIdType.MESH
VMEM = pl.BlockSpec(memory_space=pltpu.VMEM)


class Place:
    def __init__(self):
        grp, dp = lax.axis_index("grp"), lax.axis_index("dp")
        self.core = lax.rem(grp, 2)
        self.z = (dp // 16) * 2 + grp // 2
        self.x = lax.rem(dp // 4, 4)
        self.y = lax.rem(dp, 4)

    def device(self, axis=None, step=0, core=None):
        where = {"x": self.x, "y": self.y, "z": self.z}
        if axis is not None:
            where[axis] = lax.rem(where[axis] + step, 4)
        core = self.core if core is None else core
        z = where["z"]
        return (lax.rem(z, 2) * 2 + core, (z // 2) * 16 + where["x"] * 4 + where["y"])

    def greet(self, devices):
        barrier = pltpu.get_barrier_semaphore()
        for device in devices:
            pl.semaphore_signal(barrier, inc=1, device_id=device, device_id_type=MESH)
        pl.semaphore_wait(barrier, len(devices))


def remote(src, dst, send, recv, device):
    copy = pltpu.make_async_remote_copy(
        src_ref=src, dst_ref=dst, send_sem=send, recv_sem=recv, device_id=device, device_id_type=MESH
    )
    copy.start()
    return copy


class RingSum:
    def __init__(self, place, axis, part, relay, final, send, recv):
        self.me = getattr(place, axis)
        self.right, self.left = place.device(axis, 1), place.device(axis, 3)
        self.next, self.far, self.prev = (lax.rem(self.me + s, 4) for s in (1, 2, 3))
        self.part, self.relay, self.final, self.send, self.recv = part, relay, final, send, recv
        self.copies = []

    def copy(self, src, dst, device):
        i = len(self.copies)
        self.copies.append(remote(src, dst, self.send.at[i], self.recv.at[i], device))

    def start_far(self):
        self.copy(self.part(self.far, 0), self.relay.at[0], self.right)
        self.copy(self.part(self.far, 1), self.relay.at[1], self.left)

    def start_near(self):
        self.copy(self.part(self.next, 1), self.final.at[0, 1], self.right)
        self.copy(self.part(self.prev, 0), self.final.at[1, 0], self.left)

    def pass_on(self):
        self.copies[0].wait_recv()
        self.relay[0] += self.part(self.next, 0)[...]
        self.copy(self.relay.at[0], self.final.at[0, 0], self.right)
        self.copies[1].wait_recv()
        self.relay[1] += self.part(self.prev, 1)[...]
        self.copy(self.relay.at[1], self.final.at[1, 1], self.left)

    def finish(self):
        for copy in self.copies[2:]:
            copy.wait_recv()
        for h in (0, 1):
            yield self.part(self.me, h)[...] + self.final[0, h] + self.final[1, h]

    def drain(self):
        for copy in self.copies:
            copy.wait_send()


class RingShare(RingSum):
    def __init__(self, place, axis, part, send, recv):
        super().__init__(place, axis, part, None, None, send, recv)

    def start(self):
        for h, device in ((0, self.right), (1, self.left), (1, self.right), (0, self.left)):
            part = self.part(self.me, h)
            self.copy(part, part, device)

    def pass_on(self):
        self.copies[0].wait_recv()
        part = self.part(self.prev, 0)
        self.copy(part, part, self.right)
        self.copies[1].wait_recv()
        part = self.part(self.next, 1)
        self.copy(part, part, self.left)

    def finish(self):
        for copy in self.copies[2:]:
            copy.wait_recv()


def small_sum_kernel(value, out, total, got_x, got_y, got_z, send, recv):
    place = Place()
    across = {axis: [place.device(axis, step) for step in (1, 2, 3)] for axis in "xy"}
    opposite = place.device("z", 2)
    place.greet(across["x"] + across["y"] + [opposite])
    copies = []

    def exchange(src, got, devices):
        mine = []
        for i, device in enumerate(devices):
            k = len(copies)
            mine.append(remote(src, got.at[i], send.at[k], recv.at[k], device))
            copies.append(mine[-1])
        for copy in mine:
            copy.wait_recv()
        return src[...] + sum(got[i] for i in range(len(devices)))

    total[0] = exchange(value, got_x, across["x"])
    total[1] = exchange(total.at[0], got_y, across["y"])
    out[...] = exchange(total.at[1], got_z, [opposite])
    for copy in copies:
        copy.wait_send()


def small_sum(value, collective_id):
    shape = value.shape
    return pl.pallas_call(
        small_sum_kernel,
        out_shape=jax.ShapeDtypeStruct(shape, jnp.float32),
        in_specs=[VMEM],
        out_specs=VMEM,
        scratch_shapes=[
            pltpu.VMEM((2, *shape), jnp.float32),
            pltpu.VMEM((3, *shape), jnp.float32),
            pltpu.VMEM((3, *shape), jnp.float32),
            pltpu.VMEM((1, *shape), jnp.float32),
            pltpu.SemaphoreType.DMA((7,)),
            pltpu.SemaphoreType.DMA((7,)),
        ],
        compiler_params=pltpu.CompilerParams(collective_id=collective_id, has_side_effects=True),
    )(value)


class DirectSum:
    def __init__(self, place, axis, part, got, send, recv):
        self.me = getattr(place, axis)
        self.part, self.got, self.copies = part, got, []
        for step in (2, 1, 3):
            chunk = part(lax.rem(self.me + step, 4))
            i = step - 1
            self.copies.append(remote(chunk, got.at[i], send.at[i], recv.at[i], place.device(axis, step)))

    def finish(self):
        for copy in self.copies:
            copy.wait_recv()
        return self.part(self.me)[...] + self.got[0] + self.got[1] + self.got[2]

    def drain(self):
        for copy in self.copies:
            copy.wait_send()


class DirectShare(DirectSum):
    def __init__(self, place, axis, part, send, recv):
        self.copies = []
        mine = part(getattr(place, axis))
        for step in (2, 1, 3):
            i = step - 1
            self.copies.append(remote(mine, mine, send.at[i], recv.at[i], place.device(axis, step)))

    def finish(self):
        for copy in self.copies:
            copy.wait_recv()


PLANS = (("x", "y"), ("y", "x"))


def all_sum_steps(place, scale, value, out, relay1, final1, sum1, got2, sum2, got3, send, recv):
    portions = [(s, p) for s in range(2) for p in range(2)]

    def lane(s, p, stage):
        i = (s * 2 + p) * 5 + stage
        return send.at[i], recv.at[i]

    opposite = place.device("z", 2)
    first, second, across, third, fourth = {}, {}, {}, {}, {}
    for s, p in portions:
        first[s, p] = RingSum(
            place,
            PLANS[p][0],
            lambda k, h, s=s, p=p: value.at[s, p, k, h],
            relay1.at[s, p],
            final1.at[s, p],
            *lane(s, p, 0),
        )
    for s in range(2):
        for p in range(2):
            first[s, p].start_far()
        for p in range(2):
            first[s, p].start_near()
    yield
    for ring in first.values():
        ring.pass_on()
    yield
    for s, p in portions:
        for h, half in enumerate(first[s, p].finish()):
            sum1[s, p, h] = half
        second[s, p] = DirectSum(
            place,
            PLANS[p][1],
            lambda k, s=s, p=p: sum1.at[s, p, k // 2, lax.rem(k, 2)],
            got2.at[s, p],
            *lane(s, p, 1),
        )
    for s, p in portions:
        sum2[s, p] = second[s, p].finish()
        i = (s * 2 + p) * 5 + 2
        across[s, p] = remote(sum2.at[s, p], got3.at[s, p], send.at[i, 0], recv.at[i, 0], opposite)
    for s, p in portions:
        across[s, p].wait_recv()
        outer, inner = (getattr(place, axis) for axis in PLANS[p])
        out[s, p, outer, inner // 2, lax.rem(inner, 2)] = (sum2[s, p] + got3[s, p]) * scale
        third[s, p] = DirectShare(
            place,
            PLANS[p][1],
            lambda k, s=s, p=p, outer=outer: out.at[s, p, outer, k // 2, lax.rem(k, 2)],
            *lane(s, p, 3),
        )
    for s, p in portions:
        third[s, p].finish()
        fourth[s, p] = RingShare(
            place, PLANS[p][0], lambda k, h, s=s, p=p: out.at[s, p, k, h], *lane(s, p, 4)
        )
        fourth[s, p].start()
    for ring in fourth.values():
        ring.pass_on()
    for ring in fourth.values():
        ring.finish()
    for group in (first, second, third, fourth):
        for ring in group.values():
            ring.drain()
    for copy in across.values():
        copy.wait_send()
    yield


def all_sum_greet(place, core):
    others = [place.device(axis, step) for axis in "xy" for step in (1, 2, 3)]
    place.greet(others + [place.device("z", 2)] + ([place.device(core=1 - place.core)] if core else []))


def all_sum_kernel(scale, value, out, *scratch):
    place = Place()
    all_sum_greet(place, False)
    for _ in all_sum_steps(place, scale, value, out, *scratch):
        pass


def all_sum_share_kernel(scale, value, hidden, out, arrived, outgoing, core_send, core_recv, *scratch):
    place = Place()
    all_sum_greet(place, True)
    steps = all_sum_steps(place, scale, value, out, *scratch)
    next(steps)
    half = outgoing.shape[1] // 2
    for part in range(2):
        start = pl.multiple_of(part * 2 * half + (1 - place.core) * half, half)
        rows = jnp.maximum(hidden[:, pl.ds(start, half)].astype(jnp.float32), 0.0)
        outgoing[:, part * half : part * half + half] = rows
    copy = remote(outgoing, arrived, core_send.at[0], core_recv.at[0], place.device(core=1 - place.core))
    for _ in steps:
        pass
    copy.wait()


def all_sum(value, scale, collective_id, hidden=None):
    shape = value.shape
    piece = value.size // (2 * 2 * 4 * 4 * 128)
    cut = (2, 2, 4, 2, 2, piece, 128)
    floats = lambda *lead: pltpu.VMEM((2, 2, *lead, piece, 128), jnp.float32)
    scratch = [
        floats(2, 2),
        floats(2, 2, 2),
        floats(2, 2),
        floats(3),
        floats(),
        floats(),
        pltpu.SemaphoreType.DMA((20, 6)),
        pltpu.SemaphoreType.DMA((20, 6)),
    ]
    out = jax.ShapeDtypeStruct(cut, jnp.float32)
    params = pltpu.CompilerParams(
        collective_id=collective_id, has_side_effects=True, vmem_limit_bytes=48 * 2**20
    )
    if hidden is None:
        total = pl.pallas_call(
            functools.partial(all_sum_kernel, scale),
            out_shape=out,
            in_specs=[VMEM],
            out_specs=VMEM,
            scratch_shapes=scratch,
            compiler_params=params,
        )(value.reshape(cut))
        return total.reshape(shape)
    wide = (hidden.shape[0], hidden.shape[1] // 2)
    extra = [pltpu.VMEM(wide, jnp.float32), pltpu.SemaphoreType.DMA((1,)), pltpu.SemaphoreType.DMA((1,))]
    total, arrived = pl.pallas_call(
        functools.partial(all_sum_share_kernel, scale),
        out_shape=(out, jax.ShapeDtypeStruct(wide, jnp.float32)),
        in_specs=[VMEM, VMEM],
        out_specs=(VMEM, VMEM),
        scratch_shapes=extra + scratch,
        compiler_params=params,
    )(value.reshape(cut), hidden)
    return total.reshape(shape), arrived


ORDERS = (("x", "y", "z"), ("y", "z", "x"), ("z", "x", "y"))
WIDTHS = (384, 384, 256)
ANY = pl.BlockSpec(memory_space=pl.ANY)


def weight_kernel(hidden_in, arrived_in, grad_in, proj_in, out, grad_hidden, *scratch):
    hidden, arrived, proj, grad_there, active, grad, local, core_send, core_recv = scratch[:9]
    send, recv = scratch[-2:]
    scratch = scratch[9:-2]
    place = Place()
    rows, width = grad_in.shape
    loads = []
    for i, (src, dst) in enumerate(((hidden_in, hidden), (arrived_in, arrived), (proj_in, proj))):
        loads.append(pltpu.make_async_copy(src, dst, local.at[i]))
        loads[i].start()
    across = place.device(core=1 - place.core)
    place.greet([place.device(axis, step) for axis in "xy" for step in (1, 3)] + [place.device("z", s) for s in (1, 2, 3)]
                + [place.device(axis, 2) for axis in "xy"] + [across])
    swap = remote(grad_in, grad_there, core_send.at[0], core_recv.at[0], across)
    parts, relays, finals, sums = [], [], [], []
    for p in range(3):
        parts.append(scratch[8 * p])
        relays.append(scratch[8 * p + 1 : 8 * p + 3])
        finals.append(scratch[8 * p + 3 : 8 * p + 6])
        sums.append(scratch[8 * p + 6 : 8 * p + 8])
    grad[:rows] = grad_in[...].astype(grad.dtype)
    loads[0].wait()
    for part in range(2):
        start = pl.multiple_of(part * 2048 + place.core * 1024, 1024)
        active[:rows, part * 1024 : part * 1024 + 1024] = jnp.maximum(hidden[:, pl.ds(start, 1024)], 0.0)
    loads[1].wait()
    active[rows:] = arrived[...].astype(active.dtype)
    swap.wait_recv()
    grad[rows:] = grad_there[...].astype(grad.dtype)

    def multiply(p):
        begin, width = sum(WIDTHS[:p]), WIDTHS[p]

        @pl.loop(0, 4)
        def _(z):
            start = lax.rem(z, 2) * 1024 + (z // 2) * 512
            product = lax.dot_general(
                active[:, pl.ds(pl.multiple_of(start, 512), 512)],
                grad[:, begin : begin + width],
                (((0,), (0,)), ((), ())),
                preferred_element_type=jnp.float32,
            )
            for x in range(4):
                for y in range(4):
                    row = x * 128 + y * 32
                    block = product[row : row + 32]
                    if p == 0:
                        parts[p][x, y // 2, y % 2, z // 2, lax.rem(z, 2)] = block
                    elif p == 1:
                        parts[p][y, z // 2, lax.rem(z, 2), x // 2, x % 2] = block
                    else:
                        parts[p][z, x // 2, x % 2, y // 2, y % 2] = block

    def hidden_tile(t):
        columns = pl.ds(pl.multiple_of(t * 512, 512), 512)
        product = lax.dot_general(
            grad[:rows, :], proj[columns, :], (((1,), (1,)), ((), ())), preferred_element_type=jnp.float32
        )
        kept = jnp.where(hidden[:, columns].astype(jnp.float32) > 0, product, 0.0)
        grad_hidden[:, columns] = kept.astype(grad_hidden.dtype)

    order = (2, 0, 1)
    first, second, third = {}, {}, {}
    for p in order:
        multiply(p)
        i = p * 3
        first[p] = RingSum(
            place, ORDERS[p][0], lambda k, h, p=p: parts[p].at[k, h], relays[p][0], finals[p][0], send.at[i], recv.at[i]
        )
        first[p].start_far()
        first[p].start_near()
    loads[2].wait()
    pl.loop(0, 3)(hidden_tile)
    for p in order:
        first[p].pass_on()
    pl.loop(3, 8)(hidden_tile)
    for p in order:
        for h, half in enumerate(first[p].finish()):
            sums[p][0][h] = half
        i = p * 3 + 1
        second[p] = RingSum(
            place,
            ORDERS[p][1],
            lambda k, h, p=p: sums[p][0].at[k // 2, lax.rem(k, 2), h],
            relays[p][1],
            finals[p][1],
            send.at[i],
            recv.at[i],
        )
        second[p].start_far()
        second[p].start_near()
    for p in order:
        second[p].pass_on()
    for p in order:
        for h, half in enumerate(second[p].finish()):
            sums[p][1][h] = half
        i = p * 3 + 2
        third[p] = DirectSum(
            place,
            ORDERS[p][2],
            lambda k, p=p: sums[p][1].at[k // 2, lax.rem(k, 2)],
            finals[p][2],
            send.at[i],
            recv.at[i],
        )
    for p in order:
        begin = sum(WIDTHS[:p])
        out[:, begin : begin + WIDTHS[p]] = third[p].finish().astype(out.dtype)
    for group in (first, second, third):
        for ring in group.values():
            ring.drain()
    swap.wait_send()


def weight_sum(hidden, arrived, grad, proj, collective_id):
    rows, width = grad.shape
    bf16 = jnp.bfloat16
    scratch = [
        pltpu.VMEM(hidden.shape, bf16),
        pltpu.VMEM(arrived.shape, jnp.float32),
        pltpu.VMEM(proj.shape, bf16),
        pltpu.VMEM(grad.shape, jnp.float32),
        pltpu.VMEM((2 * rows, arrived.shape[1]), bf16),
        pltpu.VMEM((2 * rows, width), bf16),
        pltpu.SemaphoreType.DMA((3,)),
        pltpu.SemaphoreType.DMA((1,)),
        pltpu.SemaphoreType.DMA((1,)),
    ]
    for columns in WIDTHS:
        scratch += [
            pltpu.VMEM((*lead, 32, columns), jnp.float32)
            for lead in [
                (4, 2, 2, 2, 2),
                (2, 2, 2, 2),
                (2, 2),
                (2, 2, 2, 2, 2),
                (2, 2, 2),
                (3,),
                (2, 2, 2, 2),
                (2, 2),
            ]
        ]
    scratch += [pltpu.SemaphoreType.DMA((9, 6)), pltpu.SemaphoreType.DMA((9, 6))]
    return pl.pallas_call(
        weight_kernel,
        out_shape=(jax.ShapeDtypeStruct((32, width), bf16), jax.ShapeDtypeStruct(hidden.shape, bf16)),
        in_specs=[ANY, ANY, VMEM, ANY],
        out_specs=(VMEM, VMEM),
        scratch_shapes=scratch,
        compiler_params=pltpu.CompilerParams(
            collective_id=collective_id, has_side_effects=True, vmem_limit_bytes=56 * 2**20
        ),
    )(hidden, arrived, grad, proj)


precise = lax.Precision.HIGHEST
N, B = 1024, 128


def spread_row(tile, row):
    return jnp.broadcast_to(tile[row : row + 1, :], (8, B))


def spread_column(tile, column):
    return jnp.broadcast_to(tile[:, column : column + 1], (8, B))


def invert_pair(a, b, c):
    det = a * c - b * b
    r = 1.0 / det
    return c * r, -b * r, a * r, det


def factor_rows(a, b, c, det, row0, row1):
    s = lax.rsqrt(a)
    first = row0 * s
    return first, (row1 - (b * s) * first) * (lax.rsqrt(det) * (a * s))


def leaf_steps(block, store):
    sub = lax.broadcasted_iota(jnp.int32, (8, B), 0)
    lane = lax.broadcasted_iota(jnp.int32, (8, B), 1)
    a = [block[8 * g : 8 * g + 8, :] for g in range(16)]
    w = [jnp.where(lane == sub + 8 * g, 1.0, 0.0) for g in range(16)]
    four = range(4)

    def entry(tile, row, column):
        return spread_row(spread_column(tile, column), row)

    d = {(l, m): entry(a[0], l, m) for l in four for m in range(l + 1)}
    finished = None
    for step in range(32):
        g, r, j = step // 2, 4 * (step % 2), 4 * step
        p, q, s, det = invert_pair(d[0, 0], d[1, 0], d[1, 1])
        k = [[p * d[n, 0] + q * d[n, 1], q * d[n, 0] + s * d[n, 1]] for n in (2, 3)]
        s00 = d[2, 2] - (d[2, 0] * k[0][0] + d[2, 1] * k[0][1])
        s10 = d[3, 2] - (d[3, 0] * k[0][0] + d[3, 1] * k[0][1])
        s11 = d[3, 3] - (d[3, 0] * k[1][0] + d[3, 1] * k[1][1])
        u, v, t, det2 = invert_pair(s00, s10, s11)
        e = {(2, 2): u, (3, 2): v, (3, 3): t}
        for i in (0, 1):
            e[2, i] = -(k[0][i] * u + k[1][i] * v)
            e[3, i] = -(k[0][i] * v + k[1][i] * t)
        e[0, 0] = p - (e[2, 0] * k[0][0] + e[3, 0] * k[1][0])
        e[1, 0] = q - (e[2, 1] * k[0][0] + e[3, 1] * k[1][0])
        e[1, 1] = s - (e[2, 1] * k[0][1] + e[3, 1] * k[1][1])
        for l in four:
            for m in range(l):
                e[m, l] = e[l, m]
        rows = [spread_row(a[g], r + n) for n in four]
        wrows = [spread_row(w[g], r + n) for n in four]
        old = d
        if step < 31:
            ng, nr = (step + 1) // 2, 4 * ((step + 1) % 2)
            tile = a[ng]
            near = [spread_column(tile, j + n) for n in four]
            far = [spread_column(tile, j + 4 + n) for n in four]
            gap = [[spread_row(near[n], nr + l) for n in four] for l in four]
            h = [[sum(e[n, m] * gap[l][m] for m in four) for n in four] for l in four]
            d = {
                (l, m): spread_row(far[m], nr + l) - sum(gap[l][n] * h[m][n] for n in four)
                for l in four
                for m in range(l + 1)
            }
        x = [sum(e[n, m] * rows[m] for m in four) for n in four]
        xw = [sum(e[n, m] * wrows[m] for m in four) for n in four]
        first, second = factor_rows(old[0, 0], old[1, 0], old[1, 1], det, wrows[0], wrows[1])
        rest = [wrows[n] - (k[n - 2][0] * wrows[0] + k[n - 2][1] * wrows[1]) for n in (2, 3)]
        third, fourth = factor_rows(s00, s10, s11, det2, *rest)
        if r == 0:
            finished = first
        for n, row in enumerate((first, second, third, fourth)):
            if r + n:
                finished = jnp.where(sub == r + n, row, finished)
        if r == 4:
            store(g, finished)
        for tile in range(g if r == 0 else g + 1, 16):
            mult = [spread_column(a[tile], j + n) for n in four]
            if tile == g:
                mult = [jnp.where(sub >= 4, m, 0.0) for m in mult]
            a[tile] = a[tile] - sum(mult[n] * x[n] for n in four)
            w[tile] = w[tile] - sum(mult[n] * xw[n] for n in four)
        yield step


def dot(a, b, over):
    return lax.dot_general(a, b, (over, ((), ())), precision=precise, preferred_element_type=jnp.float32)


def inverse_kernel(packed, out, whole, top, work):
    for i in range(8):
        for j in range(i + 1):
            block = packed[i * (i + 1) // 2 + j]
            whole[B * i : B * i + B, B * j : B * j + B] = block
            if j < i:
                whole[B * j : B * j + B, B * i : B * i + B] = block.T
    whole[N:, :] = jnp.zeros((B, N), jnp.float32)
    lane = lax.broadcasted_iota(jnp.int32, (B, B), 1)
    sub = lax.broadcasted_iota(jnp.int32, (B, B), 0)
    unit = jnp.where(lane == sub, 1.0, 0.0)

    def store(g, tile):
        work[8 * g : 8 * g + 8, :] = tile

    def rows_of(i):
        return pl.ds(pl.multiple_of(i * B, B), B)

    for _ in leaf_steps(whole[:B, :B], store):
        pass

    @pl.loop(0, 7)
    def _(k):
        here, below = rows_of(k), rows_of(k + 1)
        factor = work[...]
        first = dot(factor, whole[here, below], ((1,), (0,)))
        whole[below, below] -= dot(first, first, ((0,), (0,)))
        block = whole[below, below]
        whole[here, here] = unit
        jobs = []

        def make_top(c):
            def job():
                columns = slice(256 * c, 256 * c + 256)
                top[:, columns] = dot(factor, whole[here, columns], ((1,), (0,)))

            return job

        def update(t, c):
            def job():
                columns = slice(256 * c, 256 * c + 256)
                there = rows_of(jnp.minimum(k + 1 + t, 8))
                left = top[:, rows_of(jnp.minimum(k + 1 + t, 7))]
                whole[there, columns] -= dot(left, top[:, columns], ((0,), (0,)))

            return job

        def clear():
            for t in range(7):
                whole[rows_of(jnp.minimum(k + 1 + t, 8)), here] = jnp.zeros((B, B), jnp.float32)

        jobs += [make_top(c) for c in range(4)] + [clear]
        jobs += [update(t, c) for t in range(7) for c in range(4)]
        jobs.append(lambda: whole.__setitem__((here, slice(None)), top[...]))
        done = 0
        for step in leaf_steps(block, store):
            upto = len(jobs) * (step + 1) // 32
            for job in jobs[done:upto]:
                job()
            done = upto

    whole[7 * B : N, 7 * B :] = unit
    whole[7 * B : N, :] = dot(work[...], whole[7 * B : N, :], ((1,), (0,)))
    for i in range(8):
        width = B * (i + 1)
        out[B * i : width, :width] = whole[B * i : width, :width]
        if i < 7:
            out[B * i : width, width:] = jnp.zeros((B, N - width), jnp.float32)


def factor_inverse(packed):
    return pl.pallas_call(
        inverse_kernel,
        out_shape=jax.ShapeDtypeStruct((N, N), jnp.float32),
        in_specs=[VMEM],
        out_specs=VMEM,
        scratch_shapes=[
            pltpu.VMEM((N + B, N), jnp.float32),
            pltpu.VMEM((B, N), jnp.float32),
            pltpu.VMEM((B, B), jnp.float32),
        ],
        compiler_params=pltpu.CompilerParams(vmem_limit_bytes=32 * 2**20),
    )(packed)


def blocks_kernel(left, right, extra, out):
    row = lax.broadcasted_iota(jnp.int32, (B, B), 0)
    lane = lax.broadcasted_iota(jnp.int32, (B, B), 1)
    for i in range(8):
        width = B * (i + 1)
        wide = dot(left[:, B * i : B * i + B], right[:, :width], ((0,), (0,)))
        for j in range(i + 1):
            block = wide[:, B * j : B * j + B]
            if extra is not None and j == i:
                line = jnp.broadcast_to(extra[i : i + 1, :], (B, B))
                first = jnp.broadcast_to(line[:, :1], (B, B))
                block = jnp.where((row == 0) & (lane > 0), line, block)
                block = jnp.where((row == 1) & (lane == B - 1), first, block)
            out[i * (i + 1) // 2 + j] = block


def lower_blocks(left, right, extra=None):
    operands = (left, right) if extra is None else (left, right, extra)
    kernel = blocks_kernel if extra is not None else lambda a, b, out: blocks_kernel(a, b, None, out)
    return pl.pallas_call(
        kernel,
        out_shape=jax.ShapeDtypeStruct((36, B, B), jnp.float32),
        in_specs=[VMEM] * len(operands),
        out_specs=VMEM,
        compiler_params=pltpu.CompilerParams(vmem_limit_bytes=40 * 2**20),
    )(*operands)


def whiten_kernel(centered, inverse, out):
    for i in range(4):
        width = 256 * (i + 1)
        out[:, width - 256 : width] = dot(centered[:, :width], inverse[width - 256 : width, :width], ((1,), (1,)))


def whiten(centered, inverse):
    return pl.pallas_call(
        whiten_kernel,
        out_shape=jax.ShapeDtypeStruct(centered.shape, jnp.float32),
        in_specs=[VMEM, VMEM],
        out_specs=VMEM,
        compiler_params=pltpu.CompilerParams(vmem_limit_bytes=40 * 2**20),
    )(centered, inverse)


def rows_kernel(count, grad_white, whitened, packed, inverse, out, sym, mixed):
    row = lax.broadcasted_iota(jnp.int32, (B, B), 0)
    lane = lax.broadcasted_iota(jnp.int32, (B, B), 1)
    for i in range(8):
        for j in range(i + 1):
            block = packed[i * (i + 1) // 2 + j]
            if j < i:
                sym[B * i : B * i + B, B * j : B * j + B] = block
                sym[B * j : B * j + B, B * i : B * i + B] = block.T
            else:
                low = jnp.where(row >= lane, block, 0.0)
                sym[B * i : B * i + B, B * i : B * i + B] = low + jnp.where(row > lane, block, 0.0).T
                total = jnp.where(lane[:1] > 0, block[:1, :], block[1:2, B - 1 :])
                mixed[:, B * i : B * i + B] = grad_white[:, B * i : B * i + B] - total / count
    for i in range(4):
        columns = slice(256 * i, 256 * i + 256)
        mixed[:, columns] -= dot(whitened[...], sym[:, columns], ((1,), (0,))) / count
    for i in range(4):
        columns = slice(256 * i, 256 * i + 256)
        out[:, columns] = dot(mixed[:, 256 * i :], inverse[256 * i :, columns], ((1,), (0,)))


def gradient_rows(count, grad_white, whitened, packed, inverse):
    return pl.pallas_call(
        functools.partial(rows_kernel, count),
        out_shape=jax.ShapeDtypeStruct(whitened.shape, jnp.float32),
        in_specs=[VMEM] * 4,
        out_specs=VMEM,
        scratch_shapes=[pltpu.VMEM((N, N), jnp.float32), pltpu.VMEM(whitened.shape, jnp.float32)],
        compiler_params=pltpu.CompilerParams(vmem_limit_bytes=48 * 2**20),
    )(grad_white, whitened, packed, inverse)


def from_other_core(value):
    pairs = [(source, source ^ 1) for source in range(lax.axis_size("grp"))]
    return lax.ppermute(value, "grp", pairs)


def local(hidden, w_proj, pairing, loss_scale):
    rows = hidden.shape[0]
    count = rows * lax.axis_size("dp")
    active = jax.nn.relu(hidden)
    projected = jnp.dot(active, w_proj, preferred_element_type=jnp.float32)
    column_sum = small_sum(jnp.sum(projected, axis=0).reshape(8, B), 0)
    centered = projected - column_sum.reshape(N) / count
    products = lower_blocks(centered, centered).reshape(36 * B, B)
    covariance, arrived = all_sum(products, 1.0 / count, 1, hidden)
    inverse = factor_inverse(covariance.reshape(36, B, B))
    whitened = whiten(centered, inverse)
    radius = jnp.sqrt(jnp.sum(whitened * whitened, axis=1, keepdims=True) + 1e-06)
    normals = whitened / radius
    partner_block = from_other_core(normals)
    partner = jnp.take(partner_block, pairing - lax.axis_index("dp") * rows, axis=0)
    grad_normals = 4.0 * loss_scale * (normals - partner)
    grad_white = (
        grad_normals - normals * jnp.sum(normals * grad_normals, axis=1, keepdims=True)
    ) / radius
    white_total = jnp.sum(grad_white, axis=0).reshape(8, B)
    mixed = all_sum(lower_blocks(grad_white, whitened, white_total).reshape(36 * B, B), 1.0, 2)
    grad_float = gradient_rows(count, grad_white, whitened, mixed.reshape(36, B, B), inverse)
    grad_weight, grad_hidden = weight_sum(hidden, arrived, grad_float, w_proj, 3)
    return (grad_hidden, grad_weight)


def solution(mesh):
    return jax.shard_map(
        local,
        mesh=mesh,
        in_specs=(P(("grp", "dp"), None), P(), P(("grp", "dp")), P()),
        out_specs=(P(("grp", "dp"), None), P(("grp", "dp"), None)),
        check_vma=False,
    )
```

```python
import functools

import jax
import jax.numpy as jnp
from jax import lax
from jax.experimental import pallas as pl
from jax.experimental.pallas import tpu as pltpu
from jax.sharding import PartitionSpec as P

MESH = pl.DeviceIdType.MESH
VMEM = pl.BlockSpec(memory_space=pltpu.VMEM)
ANY = pl.BlockSpec(memory_space=pl.ANY)


class Place:
    def __init__(self):
        grp, dp = lax.axis_index("grp"), lax.axis_index("dp")
        self.core = lax.rem(grp, 2)
        self.z = (dp // 16) * 2 + grp // 2
        self.x = lax.rem(dp // 4, 4)
        self.y = lax.rem(dp, 4)

    def device(self, axis=None, step=0, core=None):
        where = {"x": self.x, "y": self.y, "z": self.z}
        if axis is not None:
            where[axis] = lax.rem(where[axis] + step, 4)
        core = self.core if core is None else core
        z = where["z"]
        return (lax.rem(z, 2) * 2 + core, (z // 2) * 16 + where["x"] * 4 + where["y"])

    def greet(self, devices):
        barrier = pltpu.get_barrier_semaphore()
        for device in devices:
            pl.semaphore_signal(barrier, inc=1, device_id=device, device_id_type=MESH)
        pl.semaphore_wait(barrier, len(devices))


def remote(src, dst, send, recv, device):
    copy = pltpu.make_async_remote_copy(
        src_ref=src, dst_ref=dst, send_sem=send, recv_sem=recv, device_id=device, device_id_type=MESH
    )
    copy.start()
    return copy


class RingSum:
    def __init__(self, place, axis, part, relay, final, send, recv):
        self.me = getattr(place, axis)
        self.right, self.left = place.device(axis, 1), place.device(axis, 3)
        self.next, self.far, self.prev = (lax.rem(self.me + s, 4) for s in (1, 2, 3))
        self.part, self.relay, self.final, self.send, self.recv = part, relay, final, send, recv
        self.copies = []

    def copy(self, src, dst, device):
        i = len(self.copies)
        self.copies.append(remote(src, dst, self.send.at[i], self.recv.at[i], device))

    def start_far(self):
        self.copy(self.part(self.far, 0), self.relay.at[0], self.right)
        self.copy(self.part(self.far, 1), self.relay.at[1], self.left)

    def start_near(self):
        self.copy(self.part(self.next, 1), self.final.at[0, 1], self.right)
        self.copy(self.part(self.prev, 0), self.final.at[1, 0], self.left)

    def pass_on(self):
        self.copies[0].wait_recv()
        self.relay[0] += self.part(self.next, 0)[...]
        self.copy(self.relay.at[0], self.final.at[0, 0], self.right)
        self.copies[1].wait_recv()
        self.relay[1] += self.part(self.prev, 1)[...]
        self.copy(self.relay.at[1], self.final.at[1, 1], self.left)

    def finish(self):
        for copy in self.copies[2:]:
            copy.wait_recv()
        for h in (0, 1):
            yield self.part(self.me, h)[...] + self.final[0, h] + self.final[1, h]

    def drain(self):
        for copy in self.copies:
            copy.wait_send()


class RingShare(RingSum):
    def __init__(self, place, axis, part, send, recv):
        super().__init__(place, axis, part, None, None, send, recv)

    def start(self):
        for h, device in ((0, self.right), (1, self.left), (1, self.right), (0, self.left)):
            part = self.part(self.me, h)
            self.copy(part, part, device)

    def pass_on(self):
        self.copies[0].wait_recv()
        part = self.part(self.prev, 0)
        self.copy(part, part, self.right)
        self.copies[1].wait_recv()
        part = self.part(self.next, 1)
        self.copy(part, part, self.left)

    def finish(self):
        for copy in self.copies[2:]:
            copy.wait_recv()


class DirectSum:
    def __init__(self, place, axis, part, got, send, recv):
        self.me = getattr(place, axis)
        self.part, self.got, self.copies = part, got, []
        for step in (2, 1, 3):
            chunk = part(lax.rem(self.me + step, 4))
            i = step - 1
            self.copies.append(remote(chunk, got.at[i], send.at[i], recv.at[i], place.device(axis, step)))

    def finish(self):
        for copy in self.copies:
            copy.wait_recv()
        return self.part(self.me)[...] + self.got[0] + self.got[1] + self.got[2]

    def drain(self):
        for copy in self.copies:
            copy.wait_send()


class DirectShare(DirectSum):
    def __init__(self, place, axis, part, send, recv):
        self.copies = []
        mine = part(getattr(place, axis))
        for step in (2, 1, 3):
            i = step - 1
            self.copies.append(remote(mine, mine, send.at[i], recv.at[i], place.device(axis, step)))

    def finish(self):
        for copy in self.copies:
            copy.wait_recv()


PLANS = (("x", "y"), ("y", "x"))


def all_sum_steps(place, scale, value, out, relay1, final1, sum1, got2, sum2, got3, send, recv):
    portions = [(s, p) for s in range(2) for p in range(2)]

    def lane(s, p, stage):
        i = (s * 2 + p) * 5 + stage
        return send.at[i], recv.at[i]

    opposite = place.device("z", 2)
    first, second, across, third, fourth = {}, {}, {}, {}, {}
    for s, p in portions:
        first[s, p] = RingSum(
            place,
            PLANS[p][0],
            lambda k, h, s=s, p=p: value.at[s, p, k, h],
            relay1.at[s, p],
            final1.at[s, p],
            *lane(s, p, 0),
        )
    for s in range(2):
        for p in range(2):
            first[s, p].start_far()
        for p in range(2):
            first[s, p].start_near()
    yield
    for ring in first.values():
        ring.pass_on()
    yield
    for s, p in portions:
        for h, half in enumerate(first[s, p].finish()):
            sum1[s, p, h] = half
        second[s, p] = DirectSum(
            place,
            PLANS[p][1],
            lambda k, s=s, p=p: sum1.at[s, p, k // 2, lax.rem(k, 2)],
            got2.at[s, p],
            *lane(s, p, 1),
        )
    yield
    for s, p in portions:
        sum2[s, p] = second[s, p].finish()
        i = (s * 2 + p) * 5 + 2
        across[s, p] = remote(sum2.at[s, p], got3.at[s, p], send.at[i, 0], recv.at[i, 0], opposite)
    yield
    for s, p in portions:
        across[s, p].wait_recv()
        outer, inner = (getattr(place, axis) for axis in PLANS[p])
        out[s, p, outer, inner // 2, lax.rem(inner, 2)] = (sum2[s, p] + got3[s, p]) * scale
        third[s, p] = DirectShare(
            place,
            PLANS[p][1],
            lambda k, s=s, p=p, outer=outer: out.at[s, p, outer, k // 2, lax.rem(k, 2)],
            *lane(s, p, 3),
        )
    yield
    for s, p in portions:
        third[s, p].finish()
        fourth[s, p] = RingShare(
            place, PLANS[p][0], lambda k, h, s=s, p=p: out.at[s, p, k, h], *lane(s, p, 4)
        )
        fourth[s, p].start()
    yield
    for ring in fourth.values():
        ring.pass_on()
    for ring in fourth.values():
        ring.finish()
    for group in (first, second, third, fourth):
        for ring in group.values():
            ring.drain()
    for copy in across.values():
        copy.wait_send()
    yield


def all_sum_greet(place, core):
    others = [place.device(axis, step) for axis in "xy" for step in (1, 2, 3)]
    place.greet(others + [place.device("z", 2)] + ([place.device(core=1 - place.core)] if core else []))


precise = lax.Precision.HIGHEST
N, B = 1024, 128


def spread_row(tile, row):
    return jnp.broadcast_to(tile[row : row + 1, :], (8, B))


def spread_column(tile, column):
    return jnp.broadcast_to(tile[:, column : column + 1], (8, B))


def invert_pair(a, b, c):
    det = a * c - b * b
    r = 1.0 / det
    return c * r, -b * r, a * r, det


def factor_rows(a, b, c, det, row0, row1):
    s = lax.rsqrt(a)
    first = row0 * s
    return first, (row1 - (b * s) * first) * (lax.rsqrt(det) * (a * s))


def leaf_steps(block, store):
    sub = lax.broadcasted_iota(jnp.int32, (8, B), 0)
    lane = lax.broadcasted_iota(jnp.int32, (8, B), 1)
    a = [block[8 * g : 8 * g + 8, :] for g in range(16)]
    w = [jnp.where(lane == sub + 8 * g, 1.0, 0.0) for g in range(16)]
    four = range(4)

    def entry(tile, row, column):
        return spread_row(spread_column(tile, column), row)

    d = {(l, m): entry(a[0], l, m) for l in four for m in range(l + 1)}
    finished = None
    for step in range(32):
        g, r, j = step // 2, 4 * (step % 2), 4 * step
        p, q, s, det = invert_pair(d[0, 0], d[1, 0], d[1, 1])
        k = [[p * d[n, 0] + q * d[n, 1], q * d[n, 0] + s * d[n, 1]] for n in (2, 3)]
        s00 = d[2, 2] - (d[2, 0] * k[0][0] + d[2, 1] * k[0][1])
        s10 = d[3, 2] - (d[3, 0] * k[0][0] + d[3, 1] * k[0][1])
        s11 = d[3, 3] - (d[3, 0] * k[1][0] + d[3, 1] * k[1][1])
        u, v, t, det2 = invert_pair(s00, s10, s11)
        e = {(2, 2): u, (3, 2): v, (3, 3): t}
        for i in (0, 1):
            e[2, i] = -(k[0][i] * u + k[1][i] * v)
            e[3, i] = -(k[0][i] * v + k[1][i] * t)
        e[0, 0] = p - (e[2, 0] * k[0][0] + e[3, 0] * k[1][0])
        e[1, 0] = q - (e[2, 1] * k[0][0] + e[3, 1] * k[1][0])
        e[1, 1] = s - (e[2, 1] * k[0][1] + e[3, 1] * k[1][1])
        for l in four:
            for m in range(l):
                e[m, l] = e[l, m]
        rows = [spread_row(a[g], r + n) for n in four]
        wrows = [spread_row(w[g], r + n) for n in four]
        old = d
        if step < 31:
            ng, nr = (step + 1) // 2, 4 * ((step + 1) % 2)
            tile = a[ng]
            near = [spread_column(tile, j + n) for n in four]
            far = [spread_column(tile, j + 4 + n) for n in four]
            gap = [[spread_row(near[n], nr + l) for n in four] for l in four]
            h = [[sum(e[n, m] * gap[l][m] for m in four) for n in four] for l in four]
            d = {
                (l, m): spread_row(far[m], nr + l) - sum(gap[l][n] * h[m][n] for n in four)
                for l in four
                for m in range(l + 1)
            }
        x = [sum(e[n, m] * rows[m] for m in four) for n in four]
        xw = [sum(e[n, m] * wrows[m] for m in four) for n in four]
        first, second = factor_rows(old[0, 0], old[1, 0], old[1, 1], det, wrows[0], wrows[1])
        rest = [wrows[n] - (k[n - 2][0] * wrows[0] + k[n - 2][1] * wrows[1]) for n in (2, 3)]
        third, fourth = factor_rows(s00, s10, s11, det2, *rest)
        if r == 0:
            finished = first
        for n, row in enumerate((first, second, third, fourth)):
            if r + n:
                finished = jnp.where(sub == r + n, row, finished)
        if r == 4:
            store(g, finished)
        for tile in range(g if r == 0 else g + 1, 16):
            mult = [spread_column(a[tile], j + n) for n in four]
            if tile == g:
                mult = [jnp.where(sub >= 4, m, 0.0) for m in mult]
            a[tile] = a[tile] - sum(mult[n] * x[n] for n in four)
            w[tile] = w[tile] - sum(mult[n] * xw[n] for n in four)
        yield step


def inverse_kernel(packed, out, whole, top, work):
    for i in range(8):
        for j in range(i + 1):
            block = packed[i * (i + 1) // 2 + j]
            whole[B * i : B * i + B, B * j : B * j + B] = block
            if j < i:
                whole[B * j : B * j + B, B * i : B * i + B] = block.T
    whole[N:, :] = jnp.zeros((B, N), jnp.float32)
    lane = lax.broadcasted_iota(jnp.int32, (B, B), 1)
    sub = lax.broadcasted_iota(jnp.int32, (B, B), 0)
    unit = jnp.where(lane == sub, 1.0, 0.0)

    def store(g, tile):
        work[8 * g : 8 * g + 8, :] = tile

    def rows_of(i):
        return pl.ds(pl.multiple_of(i * B, B), B)

    for _ in leaf_steps(whole[:B, :B], store):
        pass

    @pl.loop(0, 7)
    def _(k):
        here, below = rows_of(k), rows_of(k + 1)
        factor = work[...]
        first = dot(factor, whole[here, below], ((1,), (0,)))
        whole[below, below] -= dot(first, first, ((0,), (0,)))
        block = whole[below, below]
        whole[here, here] = unit
        jobs = []

        def make_top(c):
            def job():
                columns = slice(256 * c, 256 * c + 256)
                top[:, columns] = dot(factor, whole[here, columns], ((1,), (0,)))

            return job

        def update(t, c):
            def job():
                columns = slice(256 * c, 256 * c + 256)
                there = rows_of(jnp.minimum(k + 1 + t, 8))
                left = top[:, rows_of(jnp.minimum(k + 1 + t, 7))]
                whole[there, columns] -= dot(left, top[:, columns], ((0,), (0,)))

            return job

        def clear():
            for t in range(7):
                whole[rows_of(jnp.minimum(k + 1 + t, 8)), here] = jnp.zeros((B, B), jnp.float32)

        jobs += [make_top(c) for c in range(4)] + [clear]
        jobs += [update(t, c) for t in range(7) for c in range(4)]
        jobs.append(lambda: whole.__setitem__((here, slice(None)), top[...]))
        done = 0
        for step in leaf_steps(block, store):
            upto = len(jobs) * (step + 1) // 32
            for job in jobs[done:upto]:
                job()
            done = upto

    whole[7 * B : N, 7 * B :] = unit
    whole[7 * B : N, :] = dot(work[...], whole[7 * B : N, :], ((1,), (0,)))
    for i in range(8):
        width = B * (i + 1)
        out[B * i : width, :width] = whole[B * i : width, :width]
        if i < 7:
            out[B * i : width, width:] = jnp.zeros((B, N - width), jnp.float32)


def factor_inverse(packed):
    return pl.pallas_call(
        inverse_kernel,
        out_shape=jax.ShapeDtypeStruct((N, N), jnp.float32),
        in_specs=[VMEM],
        out_specs=VMEM,
        scratch_shapes=[
            pltpu.VMEM((N + B, N), jnp.float32),
            pltpu.VMEM((B, N), jnp.float32),
            pltpu.VMEM((B, B), jnp.float32),
        ],
        compiler_params=pltpu.CompilerParams(vmem_limit_bytes=32 * 2**20),
    )(packed)


def dot(a, b, over, precision=precise):
    return lax.dot_general(a, b, (over, ((), ())), precision=precision, preferred_element_type=jnp.float32)


def make_all_sum_scratch():
    floats = lambda *lead: pltpu.VMEM((2, 2, *lead, 72, 128), jnp.float32)
    return [
        floats(2, 2),
        floats(2, 2, 2),
        floats(2, 2),
        floats(3),
        floats(),
        floats(),
        pltpu.SemaphoreType.DMA((20, 6)),
        pltpu.SemaphoreType.DMA((20, 6)),
    ]


CUT = (2, 2, 4, 2, 2, 72, 128)


def put_block(value, i, j, block):
    begin = (i * (i + 1) // 2 + j) * B
    row = begin
    while row < begin + B:
        piece, inside = divmod(row, 72)
        count = min(72 - inside, begin + B - row)
        s, p, k, h, l = piece // 32, piece // 16 % 2, piece // 4 % 4, piece // 2 % 2, piece % 2
        value[s, p, k, h, l, inside : inside + count, :] = block[row - begin : row - begin + count, :]
        row += count


def get_block(value, i, j):
    begin = (i * (i + 1) // 2 + j) * B
    row, parts = begin, []
    while row < begin + B:
        piece, inside = divmod(row, 72)
        count = min(72 - inside, begin + B - row)
        s, p, k, h, l = piece // 32, piece // 16 % 2, piece // 4 % 4, piece // 2 % 2, piece % 2
        parts.append(value[s, p, k, h, l, inside : inside + count, :])
        row += count
    return parts[0] if len(parts) == 1 else jnp.concatenate(parts, axis=0)


FAN = [(y, z) for y in range(4) for z in range(2)][1:]


def front_kernel(
    hidden_in, proj_in, covariance, centered, active,
    hidden, proj, local_sum, row_sum, got_row, got_rest, value, outgoing, arrived,
    loads, core_send, core_recv, sum_send, sum_recv, *scratch,
):
    place = Place()
    rows, width = centered.shape
    deep = proj.shape[1]
    copies = []
    for i in range(4):
        copies.append(pltpu.make_async_copy(hidden_in.at[:, i * deep : i * deep + deep], hidden.at[i], loads.at[0, i]))
        copies.append(pltpu.make_async_copy(proj_in.at[i * deep : i * deep + deep], proj.at[i], loads.at[1, i]))
    for copy in copies:
        copy.start()
    line = [place.device("x", step) for step in (1, 2, 3)]

    def rest_of(step):
        z = lax.rem(place.z + 2 * step[1], 4)
        return (lax.rem(z, 2) * 2 + place.core, (z // 2) * 16 + place.x * 4 + lax.rem(place.y + step[0], 4))

    rest = [rest_of(step) for step in FAN]
    other = place.device(core=1 - place.core)
    barrier = pltpu.get_barrier_semaphore()
    for device in line + rest + [other]:
        pl.semaphore_signal(barrier, inc=1, device_id=device, device_id_type=MESH)
    for i in range(4):
        copies[2 * i].wait()
        copies[2 * i + 1].wait()
        rows_here = jnp.maximum(hidden[i], 0.0)
        for c in range(0, width, 256):
            product = jnp.dot(rows_here, proj[i, :, c : c + 256], preferred_element_type=jnp.float32)
            if i:
                product = product + centered[:, c : c + 256]
            centered[:, c : c + 256] = product
            if i == 3:
                total = jnp.sum(product, axis=0, keepdims=True)
                for q in (0, 128):
                    local_sum[(c + q) // 128 : (c + q) // 128 + 1, :] = total[:, q : q + 128]
                centered[:, c : c + 256] = product - total / rows
    pl.semaphore_wait(barrier, len(line + rest) + 1)
    along = [remote(local_sum, got_row.at[i], sum_send.at[i], sum_recv.at[i], line[i]) for i in range(3)]
    for i in range(8):
        wide = dot(centered[:, B * i : B * i + B], centered[:, : B * (i + 1)], ((0,), (0,)))
        for j in range(i + 1):
            put_block(value, i, j, wide[:, B * j : B * j + B])
        if i == 4:
            for copy in along:
                copy.wait_recv()
            row_sum[...] = local_sum[...] + got_row[0] + got_row[1] + got_row[2]
            along += [
                remote(row_sum, got_rest.at[n], sum_send.at[3 + n], sum_recv.at[3 + n], rest[n]) for n in range(7)
            ]
    for copy in along[3:]:
        copy.wait_recv()
    total = row_sum[...]
    for n in range(7):
        total = total + got_rest[n]
    count = rows * 32
    shift = local_sum[...] / rows - total / count
    upright = (shift * rows).T
    for i in range(8):
        column = jnp.broadcast_to(upright[:, i : i + 1], (B, B))
        for j in range(i + 1):
            put_block(value, i, j, get_block(value, i, j) + column * shift[j : j + 1, :])
    steps = all_sum_steps(place, 1.0 / count, value, covariance, *scratch)
    next(steps)
    half = deep
    for part in range(2):
        kept = jnp.maximum(hidden[2 * part + 1 - place.core].astype(jnp.float32), 0.0)
        outgoing[:, part * half : part * half + half] = kept
    swap = remote(outgoing, arrived, core_send.at[0], core_recv.at[0], other)
    for i in range(8):
        centered[:, B * i : B * i + B] += shift[i : i + 1, :]

    def turn(q):
        part, inside = divmod(q * 256, half)
        mine = hidden[2 * part + place.core, :, inside : inside + 256].astype(jnp.float32)
        active[q * 256 : q * 256 + 256, :rows] = jnp.maximum(mine, 0.0).T.astype(active.dtype)

    def turn_arrived(q):
        active[q * 256 : q * 256 + 256, rows:] = arrived[:, q * 256 : q * 256 + 256].T.astype(active.dtype)

    work = [functools.partial(turn, q) for q in range(8)]
    for job in work[:4]:
        job()
    next(steps)
    for job in work[4:]:
        job()
    swap.wait_recv()
    later = [functools.partial(turn_arrived, q) for q in range(8)]
    for _ in steps:
        for job in later[:2]:
            job()
        later = later[2:]
    for job in later:
        job()
    swap.wait_send()
    for copy in along:
        copy.wait_send()


def front(hidden, proj):
    rows, depth = hidden.shape
    width = proj.shape[1]
    f32, bf16 = jnp.float32, jnp.bfloat16
    return pl.pallas_call(
        front_kernel,
        out_shape=(
            jax.ShapeDtypeStruct(CUT, f32),
            jax.ShapeDtypeStruct((rows, width), f32),
            jax.ShapeDtypeStruct((depth // 2, 2 * rows), bf16),
        ),
        in_specs=[ANY, ANY],
        out_specs=(VMEM, VMEM, VMEM),
        scratch_shapes=[
            pltpu.VMEM((4, rows, depth // 4), bf16),
            pltpu.VMEM((4, depth // 4, width), bf16),
            pltpu.VMEM((8, B), f32),
            pltpu.VMEM((8, B), f32),
            pltpu.VMEM((3, 8, B), f32),
            pltpu.VMEM((7, 8, B), f32),
            pltpu.VMEM(CUT, f32),
            pltpu.VMEM((rows, depth // 2), f32),
            pltpu.VMEM((rows, depth // 2), f32),
            pltpu.SemaphoreType.DMA((2, 4)),
            pltpu.SemaphoreType.DMA((1,)),
            pltpu.SemaphoreType.DMA((1,)),
            pltpu.SemaphoreType.DMA((10,)),
            pltpu.SemaphoreType.DMA((10,)),
            *make_all_sum_scratch(),
        ],
        compiler_params=pltpu.CompilerParams(
            collective_id=0, has_side_effects=True, vmem_limit_bytes=58 * 2**20
        ),
    )(hidden, proj)


def middle_kernel(
    centered, inverse, pairing, scale, mixed, white, grad_white,
    there, value, core_send, core_recv, *scratch,
):
    place = Place()
    rows, width = centered.shape
    other = place.device(core=1 - place.core)
    all_sum_greet(place, True)
    swaps = []
    squares = jnp.zeros((rows, 1), jnp.float32)
    for i in range(4):
        columns = slice(256 * i, 256 * i + 256)
        tile = dot(centered[:, : 256 * i + 256], inverse[columns, : 256 * i + 256], ((1,), (1,)))
        white[:, columns] = tile
        squares = squares + jnp.sum(tile * tile, axis=1, keepdims=True)
        swaps.append(
            remote(white.at[:, columns], there.at[:, columns], core_send.at[i], core_recv.at[i], other)
        )
    over = 1.0 / jnp.sqrt(squares + 1e-06)
    lane = lax.broadcasted_iota(jnp.int32, (rows, rows), 1)
    chosen = jnp.where(pairing[...] == lane, 1.0, 0.0)
    squares = jnp.zeros((rows, 1), jnp.float32)
    for swap in swaps:
        swap.wait_recv()
    for i in range(4):
        tile = there[:, 256 * i : 256 * i + 256]
        squares = squares + jnp.sum(tile * tile, axis=1, keepdims=True)
    over_there = 1.0 / jnp.sqrt(squares + 1e-06)
    factor = 4.0 * scale[0, 0]
    along = jnp.zeros((rows, 1), jnp.float32)
    for i in range(4):
        columns = slice(256 * i, 256 * i + 256)
        partner = dot(chosen, there[:, columns] * over_there, ((1,), (0,)))
        normals = white[:, columns] * over
        grad = factor * (normals - partner)
        grad_white[:, columns] = grad
        along = along + jnp.sum(normals * grad, axis=1, keepdims=True)
    totals = []
    for i in range(4):
        columns = slice(256 * i, 256 * i + 256)
        grad = (grad_white[:, columns] - white[:, columns] * (over * along)) * over
        grad_white[:, columns] = grad
        total = jnp.sum(grad, axis=0, keepdims=True)
        totals += [total[:, :B], total[:, B:]]
    row = lax.broadcasted_iota(jnp.int32, (B, B), 0)
    lane = lax.broadcasted_iota(jnp.int32, (B, B), 1)
    for i in range(8):
        wide = dot(grad_white[:, B * i : B * i + B], white[:, : B * (i + 1)], ((0,), (0,)), lax.Precision.HIGH)
        for j in range(i + 1):
            block = wide[:, B * j : B * j + B]
            if j == i:
                line = jnp.broadcast_to(totals[i], (B, B))
                first = jnp.broadcast_to(totals[i][:, :1], (B, B))
                block = jnp.where((row == 0) & (lane > 0), line, block)
                block = jnp.where((row == 1) & (lane == B - 1), first, block)
            put_block(value, i, j, block)
    for _ in all_sum_steps(place, 1.0, value, mixed, *scratch):
        pass
    for swap in swaps:
        swap.wait_send()


def middle(centered, inverse, pairing, scale):
    shape = jax.ShapeDtypeStruct(centered.shape, jnp.float32)
    return pl.pallas_call(
        middle_kernel,
        out_shape=(jax.ShapeDtypeStruct(CUT, jnp.float32), shape, shape),
        in_specs=[VMEM, VMEM, VMEM, pl.BlockSpec(memory_space=pltpu.SMEM)],
        out_specs=(VMEM, VMEM, VMEM),
        scratch_shapes=[
            pltpu.VMEM(centered.shape, jnp.float32),
            pltpu.VMEM(CUT, jnp.float32),
            pltpu.SemaphoreType.DMA((4,)),
            pltpu.SemaphoreType.DMA((4,)),
            *make_all_sum_scratch(),
        ],
        compiler_params=pltpu.CompilerParams(
            collective_id=1, has_side_effects=True, vmem_limit_bytes=48 * 2**20
        ),
    )(centered, inverse, pairing, scale)


ORDERS = (("x", "y", "z"), ("y", "z", "x"), ("z", "x", "y"))
WIDTHS = (384, 384, 256)


def tail_kernel(
    grad_white, white, packed, inverse, hidden_in, proj_in, active_in, out, grad_hidden,
    hidden, proj, active, sym, mixed, grad_here, grad_there, grad, local, core_send, core_recv, *scratch,
):
    send, recv = scratch[-2:]
    place = Place()
    rows, width = white.shape
    count = rows * 32
    loads = []
    for i, (src, dst) in enumerate(((hidden_in, hidden), (proj_in, proj), (active_in, active))):
        loads.append(pltpu.make_async_copy(src, dst, local.at[i]))
        loads[i].start()
    across = place.device(core=1 - place.core)
    peers = [place.device(axis, step) for axis in "xyz" for step in (1, 2, 3)] + [across]
    barrier = pltpu.get_barrier_semaphore()
    for device in peers:
        pl.semaphore_signal(barrier, inc=1, device_id=device, device_id_type=MESH)

    row = lax.broadcasted_iota(jnp.int32, (B, B), 0)
    lane = lax.broadcasted_iota(jnp.int32, (B, B), 1)
    for c in range(4):
        for q in (0, 1):
            j, at = 2 * c + q, slice(B * q, B * q + B)
            for i in range(8):
                if i > j:
                    block = get_block(packed, i, j)
                elif i < j:
                    block = get_block(packed, j, i).T
                else:
                    block = get_block(packed, i, i)
                    total = jnp.where(lane[:1] > 0, block[:1, :], block[1:2, B - 1 :])
                    mixed[:, B * i : B * i + B] = grad_white[:, B * i : B * i + B] - total / count
                    block = jnp.where(row >= lane, block, 0.0) + jnp.where(row > lane, block, 0.0).T
                sym[B * i : B * i + B, at] = block
        columns = slice(256 * c, 256 * c + 256)
        mixed[:, columns] -= dot(white[...], sym[...], ((1,), (0,)), lax.Precision.HIGH) / count
    pl.semaphore_wait(barrier, len(peers))

    swaps = []

    def gradient(c):
        columns = slice(256 * c, 256 * c + 256)
        tile = dot(mixed[:, 256 * c :], inverse[256 * c :, columns], ((1,), (0,)), lax.Precision.HIGH)
        grad_here[:, columns] = tile
        grad[:rows, columns] = tile.astype(grad.dtype)
        swaps.append(
            remote(grad_here.at[:, columns], grad_there.at[:, columns], core_send.at[c], core_recv.at[c], across)
        )

    def gradient_there(c):
        columns = slice(256 * c, 256 * c + 256)
        swaps[c].wait_recv()
        grad[rows:, columns] = grad_there[:, columns].astype(grad.dtype)

    parts, relays, finals, sums = [], [], [], []
    for p in range(3):
        parts.append(scratch[8 * p])
        relays.append(scratch[8 * p + 1 : 8 * p + 3])
        finals.append(scratch[8 * p + 3 : 8 * p + 6])
        sums.append(scratch[8 * p + 6 : 8 * p + 8])

    def multiply(p, k):
        begin = sum(WIDTHS[:p])
        high, low = k // 2, lax.rem(k, 2)
        if p == 0:
            left = active[:, :, k]
        elif p == 1:
            left = active[:, :, :, k]
        else:
            left = active[low, high]
        product = jnp.dot(
            left.reshape(512, 2 * rows), grad[:, begin : begin + WIDTHS[p]], preferred_element_type=jnp.float32
        )
        for n in range(16):
            block = product[32 * n : 32 * n + 32]
            if p == 0:
                parts[p][k, n % 4 // 2, n % 2, n // 4 % 2, n // 8] = block
            elif p == 1:
                parts[p][k, n // 4 % 2, n // 8, n % 4 // 2, n % 2] = block
            else:
                parts[p][k, n // 8, n // 4 % 2, n % 4 // 2, n % 2] = block

    def hidden_tile(t):
        columns = pl.ds(pl.multiple_of(t * 512, 512), 512)
        product = lax.dot_general(
            grad[:rows, :], proj[columns, :], (((1,), (1,)), ((), ())), preferred_element_type=jnp.float32
        )
        kept = jnp.where(hidden[:, columns].astype(jnp.float32) > 0, product, 0.0)
        grad_hidden[:, columns] = kept.astype(grad_hidden.dtype)

    first, second, third = {}, {}, {}

    def begin(p):
        i = p * 3
        first[p] = ring = RingSum(
            place, ORDERS[p][0], lambda k, h: parts[p].at[k, h], relays[p][0], finals[p][0], send.at[i], recv.at[i]
        )
        multiply(p, ring.far)
        ring.start_far()
        multiply(p, ring.next)
        multiply(p, ring.prev)
        ring.start_near()

    for c in (0, 1, 2):
        gradient(c)
    loads[2].wait()
    gradient_there(0)
    gradient_there(1)
    begin(0)
    gradient(3)
    gradient_there(2)
    begin(1)
    gradient_there(3)
    begin(2)
    for p in range(3):
        multiply(p, first[p].me)
    loads[0].wait()
    loads[1].wait()
    pl.loop(0, 4)(hidden_tile)
    for p in range(3):
        first[p].pass_on()
    pl.loop(4, 8)(hidden_tile)
    for p in range(3):
        for h, half in enumerate(first[p].finish()):
            sums[p][0][h] = half
        i = p * 3 + 1
        second[p] = RingSum(
            place,
            ORDERS[p][1],
            lambda k, h, p=p: sums[p][0].at[k // 2, lax.rem(k, 2), h],
            relays[p][1],
            finals[p][1],
            send.at[i],
            recv.at[i],
        )
        second[p].start_far()
        second[p].start_near()
    for p in range(3):
        second[p].pass_on()
    for p in range(3):
        for h, half in enumerate(second[p].finish()):
            sums[p][1][h] = half
        i = p * 3 + 2
        third[p] = DirectSum(
            place,
            ORDERS[p][2],
            lambda k, p=p: sums[p][1].at[k // 2, lax.rem(k, 2)],
            finals[p][2],
            send.at[i],
            recv.at[i],
        )
    for p in range(3):
        start = sum(WIDTHS[:p])
        out[:, start : start + WIDTHS[p]] = third[p].finish().astype(out.dtype)
    for group in (first, second, third):
        for ring in group.values():
            ring.drain()
    for swap in swaps:
        swap.wait_send()


def tail(grad_white, white, mixed, inverse, hidden, proj, active):
    rows, width = white.shape
    bf16, f32 = jnp.bfloat16, jnp.float32
    cut = (2, 2, 4, 4, 32, 2 * rows)
    scratch = [
        pltpu.VMEM(hidden.shape, bf16),
        pltpu.VMEM(proj.shape, bf16),
        pltpu.VMEM(cut, bf16),
        pltpu.VMEM((width, 256), f32),
        pltpu.VMEM(white.shape, f32),
        pltpu.VMEM(white.shape, f32),
        pltpu.VMEM(white.shape, f32),
        pltpu.VMEM((2 * rows, width), bf16),
        pltpu.SemaphoreType.DMA((3,)),
        pltpu.SemaphoreType.DMA((4,)),
        pltpu.SemaphoreType.DMA((4,)),
    ]
    for columns in WIDTHS:
        scratch += [
            pltpu.VMEM((*lead, 32, columns), f32)
            for lead in [
                (4, 2, 2, 2, 2),
                (2, 2, 2, 2),
                (2, 2),
                (2, 2, 2, 2, 2),
                (2, 2, 2),
                (3,),
                (2, 2, 2, 2),
                (2, 2),
            ]
        ]
    scratch += [pltpu.SemaphoreType.DMA((9, 6)), pltpu.SemaphoreType.DMA((9, 6))]
    return pl.pallas_call(
        tail_kernel,
        out_shape=(jax.ShapeDtypeStruct((32, width), bf16), jax.ShapeDtypeStruct(hidden.shape, bf16)),
        in_specs=[VMEM, VMEM, VMEM, VMEM, ANY, ANY, ANY],
        out_specs=(VMEM, VMEM),
        scratch_shapes=scratch,
        compiler_params=pltpu.CompilerParams(
            collective_id=2, has_side_effects=True, vmem_limit_bytes=60 * 2**20
        ),
    )(grad_white, white, mixed, inverse, hidden, proj, active.reshape(cut))


def local(hidden, w_proj, pairing, loss_scale):
    rows = hidden.shape[0]
    covariance, centered, active = front(hidden, w_proj)
    inverse = factor_inverse(covariance.reshape(36, B, B))
    partner = (pairing - lax.axis_index("dp") * rows).reshape(rows, 1)
    mixed, white, grad_white = middle(centered, inverse, partner, loss_scale.reshape(1, 1))
    grad_weight, grad_hidden = tail(grad_white, white, mixed, inverse, hidden, w_proj, active)
    return (grad_hidden, grad_weight)


def solution(mesh):
    return jax.shard_map(
        local,
        mesh=mesh,
        in_specs=(P(("grp", "dp"), None), P(), P(("grp", "dp")), P()),
        out_specs=(P(("grp", "dp"), None), P(("grp", "dp"), None)),
        check_vma=False,
    )
```

```python
import functools

import jax
import jax.numpy as jnp
from jax import lax
from jax.experimental import pallas as pl
from jax.experimental.pallas import tpu as pltpu
from jax.sharding import PartitionSpec as P

MESH = pl.DeviceIdType.MESH
VMEM = pl.BlockSpec(memory_space=pltpu.VMEM)
ANY = pl.BlockSpec(memory_space=pl.ANY)


class Place:
    def __init__(self):
        grp, dp = lax.axis_index("grp"), lax.axis_index("dp")
        self.core = lax.rem(grp, 2)
        self.z = (dp // 16) * 2 + grp // 2
        self.x = lax.rem(dp // 4, 4)
        self.y = lax.rem(dp, 4)

    def device(self, axis=None, step=0, core=None):
        where = {"x": self.x, "y": self.y, "z": self.z}
        if axis is not None:
            where[axis] = lax.rem(where[axis] + step, 4)
        core = self.core if core is None else core
        z = where["z"]
        return (lax.rem(z, 2) * 2 + core, (z // 2) * 16 + where["x"] * 4 + where["y"])

    def greet(self, devices):
        barrier = pltpu.get_barrier_semaphore()
        for device in devices:
            pl.semaphore_signal(barrier, inc=1, device_id=device, device_id_type=MESH)
        pl.semaphore_wait(barrier, len(devices))


def remote(src, dst, send, recv, device):
    copy = pltpu.make_async_remote_copy(
        src_ref=src, dst_ref=dst, send_sem=send, recv_sem=recv, device_id=device, device_id_type=MESH
    )
    copy.start()
    return copy


class RingSum:
    def __init__(self, place, axis, part, relay, final, send, recv):
        self.me = getattr(place, axis)
        self.right, self.left = place.device(axis, 1), place.device(axis, 3)
        self.next, self.far, self.prev = (lax.rem(self.me + s, 4) for s in (1, 2, 3))
        self.part, self.relay, self.final, self.send, self.recv = part, relay, final, send, recv
        self.copies = []

    def copy(self, src, dst, device):
        i = len(self.copies)
        self.copies.append(remote(src, dst, self.send.at[i], self.recv.at[i], device))

    def start_far(self):
        self.copy(self.part(self.far, 0), self.relay.at[0], self.right)
        self.copy(self.part(self.far, 1), self.relay.at[1], self.left)

    def start_near(self):
        self.copy(self.part(self.next, 1), self.final.at[0, 1], self.right)
        self.copy(self.part(self.prev, 0), self.final.at[1, 0], self.left)

    def pass_on(self):
        self.copies[0].wait_recv()
        self.relay[0] += self.part(self.next, 0)[...]
        self.copy(self.relay.at[0], self.final.at[0, 0], self.right)
        self.copies[1].wait_recv()
        self.relay[1] += self.part(self.prev, 1)[...]
        self.copy(self.relay.at[1], self.final.at[1, 1], self.left)

    def finish(self):
        for copy in self.copies[2:]:
            copy.wait_recv()
        for h in (0, 1):
            yield self.part(self.me, h)[...] + self.final[0, h] + self.final[1, h]

    def drain(self):
        for copy in self.copies:
            copy.wait_send()


class RingShare(RingSum):
    def __init__(self, place, axis, part, send, recv):
        super().__init__(place, axis, part, None, None, send, recv)

    def start(self):
        for h, device in ((0, self.right), (1, self.left), (1, self.right), (0, self.left)):
            part = self.part(self.me, h)
            self.copy(part, part, device)

    def pass_on(self):
        self.copies[0].wait_recv()
        part = self.part(self.prev, 0)
        self.copy(part, part, self.right)
        self.copies[1].wait_recv()
        part = self.part(self.next, 1)
        self.copy(part, part, self.left)

    def finish(self):
        for copy in self.copies[2:]:
            copy.wait_recv()


class DirectSum:
    def __init__(self, place, axis, part, got, send, recv):
        self.me = getattr(place, axis)
        self.part, self.got, self.copies = part, got, []
        for step in (2, 1, 3):
            chunk = part(lax.rem(self.me + step, 4))
            i = step - 1
            self.copies.append(remote(chunk, got.at[i], send.at[i], recv.at[i], place.device(axis, step)))

    def finish(self):
        for copy in self.copies:
            copy.wait_recv()
        return self.part(self.me)[...] + self.got[0] + self.got[1] + self.got[2]

    def drain(self):
        for copy in self.copies:
            copy.wait_send()


class DirectShare(DirectSum):
    def __init__(self, place, axis, part, send, recv):
        self.copies = []
        mine = part(getattr(place, axis))
        for step in (2, 1, 3):
            i = step - 1
            self.copies.append(remote(mine, mine, send.at[i], recv.at[i], place.device(axis, step)))

    def finish(self):
        for copy in self.copies:
            copy.wait_recv()


PLANS = (("x", "y"), ("y", "x"))


def all_sum_steps(place, scale, value, out, relay1, final1, sum1, got2, sum2, got3, send, recv):
    portions = [(s, p) for s in range(2) for p in range(2)]

    def lane(s, p, stage):
        i = (s * 2 + p) * 5 + stage
        return send.at[i], recv.at[i]

    opposite = place.device("z", 2)
    first, second, across, third, fourth = {}, {}, {}, {}, {}
    for s in range(2):
        for p in range(2):
            first[s, p] = RingSum(
                place,
                PLANS[p][0],
                lambda k, h, s=s, p=p: value.at[s, p, k, h],
                relay1.at[s, p],
                final1.at[s, p],
                *lane(s, p, 0),
            )
            first[s, p].start_far()
        for p in range(2):
            first[s, p].start_near()
        yield
    for ring in first.values():
        ring.pass_on()
    yield
    for s, p in portions:
        for h, half in enumerate(first[s, p].finish()):
            sum1[s, p, h] = half
        second[s, p] = DirectSum(
            place,
            PLANS[p][1],
            lambda k, s=s, p=p: sum1.at[s, p, k // 2, lax.rem(k, 2)],
            got2.at[s, p],
            *lane(s, p, 1),
        )
    yield
    for s, p in portions:
        sum2[s, p] = second[s, p].finish()
        i = (s * 2 + p) * 5 + 2
        across[s, p] = remote(sum2.at[s, p], got3.at[s, p], send.at[i, 0], recv.at[i, 0], opposite)
    yield
    for s, p in portions:
        across[s, p].wait_recv()
        outer, inner = (getattr(place, axis) for axis in PLANS[p])
        out[s, p, outer, inner // 2, lax.rem(inner, 2)] = (sum2[s, p] + got3[s, p]) * scale
        third[s, p] = DirectShare(
            place,
            PLANS[p][1],
            lambda k, s=s, p=p, outer=outer: out.at[s, p, outer, k // 2, lax.rem(k, 2)],
            *lane(s, p, 3),
        )
    yield
    for s, p in portions:
        third[s, p].finish()
        fourth[s, p] = RingShare(
            place, PLANS[p][0], lambda k, h, s=s, p=p: out.at[s, p, k, h], *lane(s, p, 4)
        )
        fourth[s, p].start()
    yield
    for ring in fourth.values():
        ring.pass_on()
    for ring in fourth.values():
        ring.finish()
    for group in (first, second, third, fourth):
        for ring in group.values():
            ring.drain()
    for copy in across.values():
        copy.wait_send()
    yield


def all_sum_greet(place, core):
    others = [place.device(axis, step) for axis in "xy" for step in (1, 2, 3)]
    place.greet(others + [place.device("z", 2)] + ([place.device(core=1 - place.core)] if core else []))


precise = lax.Precision.HIGHEST
N, B = 1024, 128


def spread_row(tile, row):
    return jnp.broadcast_to(tile[row : row + 1, :], (8, B))


def spread_column(tile, column):
    return jnp.broadcast_to(tile[:, column : column + 1], (8, B))


def invert_pair(a, b, c):
    det = a * c - b * b
    r = 1.0 / det
    return c * r, -b * r, a * r, det


def factor_rows(a, b, c, det, row0, row1):
    s = lax.rsqrt(a)
    first = row0 * s
    return first, (row1 - (b * s) * first) * (lax.rsqrt(det) * (a * s))


def leaf_steps(block, store):
    sub = lax.broadcasted_iota(jnp.int32, (8, B), 0)
    lane = lax.broadcasted_iota(jnp.int32, (8, B), 1)
    a = [block[8 * g : 8 * g + 8, :] for g in range(16)]
    w = [jnp.where(lane == sub + 8 * g, 1.0, 0.0) for g in range(16)]
    four = range(4)
    d = {(l, m): spread_row(spread_column(a[0], m), l) for l in four for m in range(l + 1)}
    finished = None
    for step in range(32):
        g, r, j = step // 2, 4 * (step % 2), 4 * step
        p, q, s, det = invert_pair(d[0, 0], d[1, 0], d[1, 1])
        k = [[p * d[n, 0] + q * d[n, 1], q * d[n, 0] + s * d[n, 1]] for n in (2, 3)]
        s00 = d[2, 2] - (d[2, 0] * k[0][0] + d[2, 1] * k[0][1])
        s10 = d[3, 2] - (d[3, 0] * k[0][0] + d[3, 1] * k[0][1])
        s11 = d[3, 3] - (d[3, 0] * k[1][0] + d[3, 1] * k[1][1])
        u, v, t, det2 = invert_pair(s00, s10, s11)
        rows = [spread_row(a[g], r + n) for n in four]
        wrows = [spread_row(w[g], r + n) for n in four]
        old = d
        if step < 31:
            ng, nr = (step + 1) // 2, 4 * ((step + 1) % 2)
            tile = a[ng]
            near = [spread_column(tile, j + n) for n in four]
            far = [spread_column(tile, j + 4 + n) for n in four]
            gap = [[spread_row(near[n], nr + l) for n in four] for l in four]
            ha = [[p * gap[l][0] + q * gap[l][1], q * gap[l][0] + s * gap[l][1]] for l in four]
            gb = [[gap[l][n] - (k[n - 2][0] * gap[l][0] + k[n - 2][1] * gap[l][1]) for n in (2, 3)] for l in four]
            hb = [[u * gb[l][0] + v * gb[l][1], v * gb[l][0] + t * gb[l][1]] for l in four]
            d = {}
            for l in four:
                for m in range(l + 1):
                    before = spread_row(far[m], nr + l) - (gap[l][0] * ha[m][0] + gap[l][1] * ha[m][1])
                    d[l, m] = before - (gb[l][0] * hb[m][0] + gb[l][1] * hb[m][1])

        def solve(r0, r1, r2, r3):
            r2 = r2 - (k[0][0] * r0 + k[0][1] * r1)
            r3 = r3 - (k[1][0] * r0 + k[1][1] * r1)
            x2, x3 = u * r2 + v * r3, v * r2 + t * r3
            x0 = (p * r0 + q * r1) - (k[0][0] * x2 + k[1][0] * x3)
            x1 = (q * r0 + s * r1) - (k[0][1] * x2 + k[1][1] * x3)
            return (x0, x1, x2, x3), r2, r3

        x, _, _ = solve(*rows)
        xw, w2, w3 = solve(*wrows)
        ready = factor_rows(old[0, 0], old[1, 0], old[1, 1], det, wrows[0], wrows[1])
        ready += factor_rows(s00, s10, s11, det2, w2, w3)
        if r == 0:
            finished = ready[0]
        for n, row in enumerate(ready):
            if r + n:
                finished = jnp.where(sub == r + n, row, finished)
        if r == 4:
            store(g, finished)
        for tile in range(g if r == 0 else g + 1, 16):
            mult = [spread_column(a[tile], j + n) for n in four]
            if tile == g:
                mult = [jnp.where(sub >= 4, m, 0.0) for m in mult]
            a[tile] = a[tile] - ((mult[0] * x[0] + mult[1] * x[1]) + (mult[2] * x[2] + mult[3] * x[3]))
            w[tile] = w[tile] - ((mult[0] * xw[0] + mult[1] * xw[1]) + (mult[2] * xw[2] + mult[3] * xw[3]))
        yield step


def three_parts(value):
    high = value.astype(jnp.bfloat16)
    rest = value - high.astype(jnp.float32)
    middle = rest.astype(jnp.bfloat16)
    return high, middle, (rest - middle.astype(jnp.float32)).astype(jnp.bfloat16)


def inverse_kernel(packed_in, out, packed, whole, left, right, work, loads, stores):
    ahead = pltpu.make_async_copy(packed_in.at[0], packed.at[0], loads.at[0])
    ahead.start()
    rest = pltpu.make_async_copy(packed_in.at[1:], packed.at[1:], loads.at[1])
    rest.start()

    def store(g, tile):
        work[8 * g : 8 * g + 8, :] = tile

    def rows_of(i):
        return pl.ds(pl.multiple_of(i * B, B), B)

    ahead.wait()
    for _ in leaf_steps(packed[0], store):
        pass
    rest.wait()
    for i in range(8):
        for j in range(i + 1):
            block = packed[i * (i + 1) // 2 + j]
            whole[B * i : B * i + B, B * j : B * j + B] = block
            if j < i:
                whole[B * j : B * j + B, B * i : B * i + B] = block.T
    whole[N:, :] = jnp.zeros((B, N), jnp.float32)
    lane = lax.broadcasted_iota(jnp.int32, (B, B), 1)
    sub = lax.broadcasted_iota(jnp.int32, (B, B), 0)
    unit = jnp.where(lane == sub, 1.0, 0.0)

    def leave(k):
        return pltpu.make_async_copy(whole.at[rows_of(k)], out.at[rows_of(k)], stores.at[k])

    @pl.loop(0, 7)
    def _(k):
        here, below = rows_of(k), rows_of(k + 1)
        factor = work[...]
        first = dot(factor, whole[here, below], ((1,), (0,)))
        whole[below, below] -= dot(first, first, ((0,), (0,)))
        block = whole[below, below]
        whole[here, here] = unit

        def make_left(t):
            def job():
                there = rows_of(jnp.minimum(k + 1 + t, 8))
                high, middle, low = three_parts(dot(whole[there, here], factor, ((1,), (1,))))
                for n, part in enumerate((high, high, middle, middle, high, low)):
                    left[t * B : t * B + B, n * B : n * B + B] = part
                whole[there, here] = jnp.zeros((B, B), jnp.float32)

            return job

        def make_right(c):
            def job():
                columns = slice(256 * c, 256 * c + 256)
                panel = dot(factor, whole[here, columns], ((1,), (0,)))
                whole[here, columns] = panel
                high, middle, low = three_parts(panel)
                for n, part in enumerate((high, middle, high, middle, low, high)):
                    right[n * B : n * B + B, columns] = part

            return job

        def update(t, c):
            def job():
                columns = slice(256 * c, 256 * c + 256)
                there = rows_of(jnp.minimum(k + 1 + t, 8))
                term = jnp.dot(
                    left[t * B : t * B + B, :], right[:, columns], preferred_element_type=jnp.float32
                )
                if t == 0:
                    place = lax.broadcasted_iota(jnp.int32, (B, 256), 1) + 256 * c
                    term = jnp.where((place >= (k + 1) * B) & (place < (k + 2) * B), 0.0, term)
                whole[there, columns] -= term

            return job

        jobs = [make_right(c) for c in range(4)] + [make_left(t) for t in range(7)]
        jobs += [update(t, c) for t in range(7) for c in range(4)]
        done = 0
        for step in leaf_steps(block, store):
            upto = len(jobs) * (step + 1) // 32
            for job in jobs[done:upto]:
                job()
            done = upto
        whole[here, below] = jnp.zeros((B, B), jnp.float32)
        leave(k).start()

    whole[7 * B : N, 7 * B :] = unit
    whole[7 * B : N, :] = dot(work[...], whole[7 * B : N, :], ((1,), (0,)))
    leave(7).start()
    for k in range(8):
        leave(k).wait()


def factor_inverse(packed):
    return pl.pallas_call(
        inverse_kernel,
        out_shape=jax.ShapeDtypeStruct((N, N), jnp.float32),
        in_specs=[ANY],
        out_specs=ANY,
        scratch_shapes=[
            pltpu.VMEM((36, B, B), jnp.float32),
            pltpu.VMEM((N + B, N), jnp.float32),
            pltpu.VMEM((7 * B, 6 * B), jnp.bfloat16),
            pltpu.VMEM((6 * B, N), jnp.bfloat16),
            pltpu.VMEM((B, B), jnp.float32),
            pltpu.SemaphoreType.DMA((2,)),
            pltpu.SemaphoreType.DMA((8,)),
        ],
        compiler_params=pltpu.CompilerParams(vmem_limit_bytes=60 * 2**20),
    )(packed)


def dot(a, b, over, precision=precise):
    return lax.dot_general(a, b, (over, ((), ())), precision=precision, preferred_element_type=jnp.float32)


def make_all_sum_scratch():
    floats = lambda *lead: pltpu.VMEM((2, 2, *lead, 72, 128), jnp.float32)
    return [
        floats(2, 2),
        floats(2, 2, 2),
        floats(2, 2),
        floats(3),
        floats(),
        floats(),
        pltpu.SemaphoreType.DMA((20, 6)),
        pltpu.SemaphoreType.DMA((20, 6)),
    ]


CUT = (2, 2, 4, 2, 2, 72, 128)


def put_block(value, i, j, block):
    begin = (i * (i + 1) // 2 + j) * B
    row = begin
    while row < begin + B:
        piece, inside = divmod(row, 72)
        count = min(72 - inside, begin + B - row)
        s, p, k, h, l = piece // 32, piece // 16 % 2, piece // 4 % 4, piece // 2 % 2, piece % 2
        value[s, p, k, h, l, inside : inside + count, :] = block[row - begin : row - begin + count, :]
        row += count


def get_block(value, i, j):
    begin = (i * (i + 1) // 2 + j) * B
    row, parts = begin, []
    while row < begin + B:
        piece, inside = divmod(row, 72)
        count = min(72 - inside, begin + B - row)
        s, p, k, h, l = piece // 32, piece // 16 % 2, piece // 4 % 4, piece // 2 % 2, piece % 2
        parts.append(value[s, p, k, h, l, inside : inside + count, :])
        row += count
    return parts[0] if len(parts) == 1 else jnp.concatenate(parts, axis=0)


FAN = [(y, z) for y in range(4) for z in range(2)][1:]


def front_kernel(
    hidden_in, proj_in, covariance, centered_out, active_out,
    centered, active, hidden, proj, local_sum, row_sum, got_row, got_rest, value, outgoing, arrived,
    loads, core_send, core_recv, sum_send, sum_recv, *scratch,
):
    place = Place()
    rows, width = centered.shape
    deep = proj.shape[1]
    copies = []
    for i in range(4):
        copies.append(pltpu.make_async_copy(hidden_in.at[:, i * deep : i * deep + deep], hidden.at[i], loads.at[0, i]))
        copies.append(pltpu.make_async_copy(proj_in.at[i * deep : i * deep + deep], proj.at[i], loads.at[1, i]))
    for copy in copies:
        copy.start()
    line = [place.device("x", step) for step in (1, 2, 3)]

    def rest_of(step):
        z = lax.rem(place.z + 2 * step[1], 4)
        return (lax.rem(z, 2) * 2 + place.core, (z // 2) * 16 + place.x * 4 + lax.rem(place.y + step[0], 4))

    rest = [rest_of(step) for step in FAN]
    other = place.device(core=1 - place.core)
    barrier = pltpu.get_barrier_semaphore()
    for device in line + rest + [other]:
        pl.semaphore_signal(barrier, inc=1, device_id=device, device_id_type=MESH)
    for i in range(4):
        copies[2 * i].wait()
        copies[2 * i + 1].wait()
        rows_here = jnp.maximum(hidden[i], 0.0)
        for c in range(0, width, 256):
            product = jnp.dot(rows_here, proj[i, :, c : c + 256], preferred_element_type=jnp.float32)
            if i:
                product = product + centered[:, c : c + 256]
            centered[:, c : c + 256] = product
            if i == 3:
                total = jnp.sum(product, axis=0, keepdims=True)
                for q in (0, 128):
                    local_sum[(c + q) // 128 : (c + q) // 128 + 1, :] = total[:, q : q + 128]
                centered[:, c : c + 256] = product - total / rows
    pl.semaphore_wait(barrier, len(line + rest) + 1)
    along = [remote(local_sum, got_row.at[i], sum_send.at[i], sum_recv.at[i], line[i]) for i in range(3)]
    for i in range(8):
        wide = dot(centered[:, B * i : B * i + B], centered[:, : B * (i + 1)], ((0,), (0,)))
        for j in range(i + 1):
            put_block(value, i, j, wide[:, B * j : B * j + B])
        if i == 4:
            for copy in along:
                copy.wait_recv()
            row_sum[...] = local_sum[...] + got_row[0] + got_row[1] + got_row[2]
            along += [
                remote(row_sum, got_rest.at[n], sum_send.at[3 + n], sum_recv.at[3 + n], rest[n]) for n in range(7)
            ]
    for copy in along[3:]:
        copy.wait_recv()
    total = row_sum[...]
    for n in range(7):
        total = total + got_rest[n]
    count = rows * 32
    shift = local_sum[...] / rows - total / count
    upright = (shift * rows).T
    steps = all_sum_steps(place, 1.0 / count, value, covariance, *scratch)
    for i in range(8):
        column = jnp.broadcast_to(upright[:, i : i + 1], (B, B))
        for j in range(i + 1):
            put_block(value, i, j, get_block(value, i, j) + column * shift[j : j + 1, :])
        if i == 5:
            next(steps)
    next(steps)
    half = deep
    for part in range(2):
        kept = jnp.maximum(hidden[2 * part + 1 - place.core].astype(jnp.float32), 0.0)
        outgoing[:, part * half : part * half + half] = kept
    swap = remote(outgoing, arrived, core_send.at[0], core_recv.at[0], other)
    for i in range(8):
        centered[:, B * i : B * i + B] += shift[i : i + 1, :]
    results = [pltpu.make_async_copy(centered, centered_out, loads.at[0, 0])]
    results[0].start()

    def turn(q):
        part, inside = divmod(q * 256, half)
        mine = hidden[2 * part + place.core, :, inside : inside + 256].astype(jnp.float32)
        active[q * 256 : q * 256 + 256, :rows] = jnp.maximum(mine, 0.0).T.astype(active.dtype)

    def turn_arrived(q):
        active[q * 256 : q * 256 + 256, rows:] = arrived[:, q * 256 : q * 256 + 256].T.astype(active.dtype)

    work = [functools.partial(turn, q) for q in range(8)]
    for job in work[:4]:
        job()
    next(steps)
    for job in work[4:]:
        job()
    swap.wait_recv()
    later = [functools.partial(turn_arrived, q) for q in range(8)]
    for _ in steps:
        for job in later[:4]:
            job()
        later = later[4:]
    for job in later:
        job()
    results.append(pltpu.make_async_copy(active, active_out, loads.at[1, 0]))
    results[1].start()
    for copy in results:
        copy.wait()
    swap.wait_send()
    for copy in along:
        copy.wait_send()


def front(hidden, proj):
    rows, depth = hidden.shape
    width = proj.shape[1]
    f32, bf16 = jnp.float32, jnp.bfloat16
    return pl.pallas_call(
        front_kernel,
        out_shape=(
            jax.ShapeDtypeStruct(CUT, f32),
            jax.ShapeDtypeStruct((rows, width), f32),
            jax.ShapeDtypeStruct((depth // 2, 2 * rows), bf16),
        ),
        in_specs=[ANY, ANY],
        out_specs=(VMEM, ANY, ANY),
        scratch_shapes=[
            pltpu.VMEM((rows, width), f32),
            pltpu.VMEM((depth // 2, 2 * rows), bf16),
            pltpu.VMEM((4, rows, depth // 4), bf16),
            pltpu.VMEM((4, depth // 4, width), bf16),
            pltpu.VMEM((8, B), f32),
            pltpu.VMEM((8, B), f32),
            pltpu.VMEM((3, 8, B), f32),
            pltpu.VMEM((7, 8, B), f32),
            pltpu.VMEM(CUT, f32),
            pltpu.VMEM((rows, depth // 2), f32),
            pltpu.VMEM((rows, depth // 2), f32),
            pltpu.SemaphoreType.DMA((2, 4)),
            pltpu.SemaphoreType.DMA((1,)),
            pltpu.SemaphoreType.DMA((1,)),
            pltpu.SemaphoreType.DMA((10,)),
            pltpu.SemaphoreType.DMA((10,)),
            *make_all_sum_scratch(),
        ],
        compiler_params=pltpu.CompilerParams(
            collective_id=0, has_side_effects=True, vmem_limit_bytes=60 * 2**20
        ),
    )(hidden, proj)


ORDERS = (("x", "y", "z"), ("y", "z", "x"), ("z", "x", "y"))
WIDTHS = (384, 384, 256)


def three_terms(ref, value, block, columns, weight):
    high = value.astype(jnp.bfloat16)
    low = (value - high.astype(jnp.float32)).astype(jnp.bfloat16)
    for n, part in enumerate((high, low, high) if weight else (high, high, low)):
        if weight:
            start = block // 2 * 768 + n * 256 + block % 2 * B
            ref[start : start + value.shape[0], columns] = part
        else:
            ref[:, block * 768 + n * 256 : block * 768 + n * 256 + 256] = part


def back_kernel(
    centered_in, inverse_in, pairing, scale, proj_in, active_in, out, grad_hidden,
    centered, inverse, white, grad_white, there, value, packed, left, right, proj, active, grad_there, grad, staged,
    swap_send, swap_recv, core_send, core_recv, local, stream, drop, early, *scratch,
):
    sum_scratch, scratch = scratch[:8], scratch[8:]
    send, recv = scratch[-2:]
    place = Place()
    rows, width = white.shape
    count = rows * 32
    loads = []
    for i in range(4):
        part = slice(256 * i, 256 * i + 256)
        loads.append(pltpu.make_async_copy(centered_in.at[:, part], centered.at[:, part], early.at[0, i]))
        loads.append(pltpu.make_async_copy(inverse_in.at[part], inverse.at[part], early.at[1, i]))
    for copy in loads:
        copy.start()
    load_active = pltpu.make_async_copy(active_in, active, local.at[0])
    load_active.start()

    def load_proj(t):
        slot = lax.rem(t, 2)
        start = pl.multiple_of(t * 512, 512)
        return pltpu.make_async_copy(proj_in.at[pl.ds(start, 512)], proj.at[slot], stream.at[slot])

    load_proj(0).start()
    load_proj(1).start()
    other = place.device(core=1 - place.core)
    peers = [place.device(axis, step) for axis in "xyz" for step in (1, 2, 3)] + [other]
    barrier = pltpu.get_barrier_semaphore()
    for device in peers:
        pl.semaphore_signal(barrier, inc=1, device_id=device, device_id_type=MESH)

    swaps = []
    squares = jnp.zeros((rows, 1), jnp.float32)
    for i in range(4):
        columns = slice(256 * i, 256 * i + 256)
        loads[2 * i].wait()
        loads[2 * i + 1].wait()
        tile = dot(centered[:, : 256 * i + 256], inverse[columns, : 256 * i + 256], ((1,), (1,)))
        white[:, columns] = tile
        if i == 1:
            pl.semaphore_wait(barrier, len(peers))
        for n in {1: (0, 1), 2: (2,), 3: (3,)}.get(i, ()):
            part = slice(256 * n, 256 * n + 256)
            swaps.append(remote(white.at[:, part], there.at[:, part], swap_send.at[n], swap_recv.at[n], other))
        squares = squares + jnp.sum(tile * tile, axis=1, keepdims=True)
    over = 1.0 / jnp.sqrt(squares + 1e-06)
    lane = lax.broadcasted_iota(jnp.int32, (rows, rows), 1)
    chosen = jnp.where(pairing[...] == lane, 1.0, 0.0).astype(jnp.bfloat16)
    squares = jnp.zeros((rows, 1), jnp.float32)
    for i in range(4):
        swaps[i].wait_recv()
        tile = there[:, 256 * i : 256 * i + 256]
        squares = squares + jnp.sum(tile * tile, axis=1, keepdims=True)
    over_there = 1.0 / jnp.sqrt(squares + 1e-06)
    factor = 4.0 * scale[0, 0]
    along = jnp.zeros((rows, 1), jnp.float32)
    for i in range(4):
        columns = slice(256 * i, 256 * i + 256)
        partner = [
            jnp.dot(chosen, part, preferred_element_type=jnp.float32)
            for part in three_parts(there[:, columns] * over_there)
        ]
        normals = white[:, columns] * over
        change = factor * (normals - ((partner[2] + partner[1]) + partner[0]))
        grad_white[:, columns] = change
        along = along + jnp.sum(normals * change, axis=1, keepdims=True)
    totals = []
    for i in range(4):
        columns = slice(256 * i, 256 * i + 256)
        change = (grad_white[:, columns] - white[:, columns] * (over * along)) * over
        grad_white[:, columns] = change
        total = jnp.sum(change, axis=0, keepdims=True)
        totals += [total[:, :B], total[:, B:]]

    row = lax.broadcasted_iota(jnp.int32, (B, B), 0)
    lane = lax.broadcasted_iota(jnp.int32, (B, B), 1)
    steps = all_sum_steps(place, 1.0, value, packed, *sum_scratch)
    for i in range(8):
        wide = dot(grad_white[:, B * i : B * i + B], white[:, : B * (i + 1)], ((0,), (0,)), lax.Precision.HIGH)
        for j in range(i + 1):
            block = wide[:, B * j : B * j + B]
            if j == i:
                line = jnp.broadcast_to(totals[i], (B, B))
                first = jnp.broadcast_to(totals[i][:, :1], (B, B))
                block = jnp.where((row == 0) & (lane > 0), line, block)
                block = jnp.where((row == 1) & (lane == B - 1), first, block)
            put_block(value, i, j, block)
        if i == 5:
            next(steps)
    next(steps)
    for i in range(4):
        three_terms(left, white[:, 256 * i : 256 * i + 256], i, None, False)
    for swap in swaps:
        swap.wait_send()
    for _ in steps:
        pass

    for c in range(4):
        for q in (0, 1):
            j, at = 2 * c + q, slice(B * q, B * q + B)
            for i in range(8):
                if i > j:
                    block = get_block(packed, i, j)
                elif i < j:
                    block = get_block(packed, j, i).T
                else:
                    block = get_block(packed, i, i)
                    total = jnp.where(lane[:1] > 0, block[:1, :], block[1:2, B - 1 :])
                    grad_white[:, B * i : B * i + B] -= total / count
                    block = jnp.where(row >= lane, block, 0.0) + jnp.where(row > lane, block, 0.0).T
                three_terms(right, block, i, at, True)
        grad_white[:, 256 * c : 256 * c + 256] -= (
            jnp.dot(left[...], right[...], preferred_element_type=jnp.float32) / count
        )
    for i in range(4):
        three_terms(left, grad_white[:, 256 * i : 256 * i + 256], i, None, False)
    grads = []

    def gradient(c):
        columns = slice(256 * c, 256 * c + 256)
        for i in range(2 * c, 8):
            three_terms(right, inverse[B * i : B * i + B, columns], i, slice(None), True)
        tile = jnp.dot(left[:, 768 * c :], right[768 * c :, :], preferred_element_type=jnp.float32)
        white[:, columns] = tile
        grad[:rows, columns] = tile.astype(grad.dtype)
        grads.append(
            remote(white.at[:, columns], grad_there.at[:, columns], core_send.at[c], core_recv.at[c], other)
        )

    def gradient_there(c):
        columns = slice(256 * c, 256 * c + 256)
        grads[c].wait_recv()
        grad[rows:, columns] = grad_there[:, columns].astype(grad.dtype)

    parts, relays, finals, sums = [], [], [], []
    for p in range(3):
        parts.append(scratch[8 * p])
        relays.append(scratch[8 * p + 1 : 8 * p + 3])
        finals.append(scratch[8 * p + 3 : 8 * p + 6])
        sums.append(scratch[8 * p + 6 : 8 * p + 8])

    def multiply(p, k):
        begin = sum(WIDTHS[:p])
        high, low = k // 2, lax.rem(k, 2)
        if p == 0:
            left = active[:, :, k]
        elif p == 1:
            left = active[:, :, :, k]
        else:
            left = active[low, high]
        product = jnp.dot(
            left.reshape(512, 2 * rows), grad[:, begin : begin + WIDTHS[p]], preferred_element_type=jnp.float32
        )
        for n in range(16):
            block = product[32 * n : 32 * n + 32]
            if p == 0:
                parts[p][k, n % 4 // 2, n % 2, n // 4 % 2, n // 8] = block
            elif p == 1:
                parts[p][k, n // 4 % 2, n // 8, n % 4 // 2, n % 2] = block
            else:
                parts[p][k, n // 8, n // 4 % 2, n % 4 // 2, n % 2] = block

    def hidden_tile(t):
        slot = lax.rem(t, 2)
        load_proj(t).wait()
        product = lax.dot_general(
            grad[:rows, :], proj[slot], (((1,), (1,)), ((), ())), preferred_element_type=jnp.float32
        )

        def leave(t):
            columns = pl.ds(pl.multiple_of(t * 512, 512), 512)
            return pltpu.make_async_copy(staged.at[slot], grad_hidden.at[:, columns], drop.at[slot])

        @pl.when(t >= 2)
        def _():
            leave(t - 2).wait()

        staged[slot] = product.astype(grad_hidden.dtype)
        leave(t).start()

        @pl.when(t < 6)
        def _():
            load_proj(t + 2).start()

        @pl.when(t == 7)
        def _():
            leave(t).wait()
            pltpu.make_async_copy(
                staged.at[1 - slot], grad_hidden.at[:, pl.ds(6 * 512, 512)], drop.at[1 - slot]
            ).wait()

    first, second, third = {}, {}, {}

    def begin(p):
        i = p * 3
        first[p] = ring = RingSum(
            place, ORDERS[p][0], lambda k, h: parts[p].at[k, h], relays[p][0], finals[p][0], send.at[i], recv.at[i]
        )
        multiply(p, ring.far)
        ring.start_far()
        multiply(p, ring.next)
        multiply(p, ring.prev)
        ring.start_near()

    for c in (0, 1, 2):
        gradient(c)
    load_active.wait()
    gradient_there(0)
    gradient_there(1)
    begin(0)
    gradient(3)
    gradient_there(2)
    begin(1)
    gradient_there(3)
    begin(2)
    for p in range(3):
        multiply(p, first[p].me)
    pl.loop(0, 4)(hidden_tile)
    for p in range(3):
        first[p].pass_on()
    pl.loop(4, 8)(hidden_tile)
    for p in range(3):
        for h, half in enumerate(first[p].finish()):
            sums[p][0][h] = half
        i = p * 3 + 1
        second[p] = RingSum(
            place,
            ORDERS[p][1],
            lambda k, h, p=p: sums[p][0].at[k // 2, lax.rem(k, 2), h],
            relays[p][1],
            finals[p][1],
            send.at[i],
            recv.at[i],
        )
        second[p].start_far()
        second[p].start_near()
    for p in range(3):
        second[p].pass_on()
    for p in range(3):
        for h, half in enumerate(second[p].finish()):
            sums[p][1][h] = half
        i = p * 3 + 2
        third[p] = DirectSum(
            place,
            ORDERS[p][2],
            lambda k, p=p: sums[p][1].at[k // 2, lax.rem(k, 2)],
            finals[p][2],
            send.at[i],
            recv.at[i],
        )
    for p in range(3):
        start = sum(WIDTHS[:p])
        out[:, start : start + WIDTHS[p]] = third[p].finish().astype(out.dtype)
    for group in (first, second, third):
        for ring in group.values():
            ring.drain()
    for swap in grads:
        swap.wait_send()


def back(centered, inverse, pairing, scale, proj, active):
    rows, width = centered.shape
    depth = proj.shape[0]
    bf16, f32 = jnp.bfloat16, jnp.float32
    cut = (2, 2, 4, 4, 32, 2 * rows)
    scratch = [
        pltpu.VMEM((rows, width), f32),
        pltpu.VMEM((width, width), f32),
        pltpu.VMEM((rows, width), f32),
        pltpu.VMEM((rows, width), f32),
        pltpu.VMEM((rows, width), f32),
        pltpu.VMEM(CUT, f32),
        pltpu.VMEM(CUT, f32),
        pltpu.VMEM((rows, 3 * width), bf16),
        pltpu.VMEM((3 * width, 256), bf16),
        pltpu.VMEM((2, 512, width), bf16),
        pltpu.VMEM(cut, bf16),
        pltpu.VMEM((rows, width), f32),
        pltpu.VMEM((2 * rows, width), bf16),
        pltpu.VMEM((2, rows, 512), bf16),
        pltpu.SemaphoreType.DMA((4,)),
        pltpu.SemaphoreType.DMA((4,)),
        pltpu.SemaphoreType.DMA((4,)),
        pltpu.SemaphoreType.DMA((4,)),
        pltpu.SemaphoreType.DMA((1,)),
        pltpu.SemaphoreType.DMA((2,)),
        pltpu.SemaphoreType.DMA((2,)),
        pltpu.SemaphoreType.DMA((2, 4)),
        *make_all_sum_scratch(),
    ]
    for columns in WIDTHS:
        scratch += [
            pltpu.VMEM((*lead, 32, columns), f32)
            for lead in [
                (4, 2, 2, 2, 2),
                (2, 2, 2, 2),
                (2, 2),
                (2, 2, 2, 2, 2),
                (2, 2, 2),
                (3,),
                (2, 2, 2, 2),
                (2, 2),
            ]
        ]
    scratch += [pltpu.SemaphoreType.DMA((9, 6)), pltpu.SemaphoreType.DMA((9, 6))]
    return pl.pallas_call(
        back_kernel,
        out_shape=(jax.ShapeDtypeStruct((32, width), bf16), jax.ShapeDtypeStruct((rows, depth), bf16)),
        in_specs=[ANY, ANY, VMEM, pl.BlockSpec(memory_space=pltpu.SMEM), ANY, ANY],
        out_specs=(VMEM, ANY),
        scratch_shapes=scratch,
        compiler_params=pltpu.CompilerParams(
            collective_id=1, has_side_effects=True, vmem_limit_bytes=60 * 2**20
        ),
    )(centered, inverse, pairing, scale, proj, active.reshape(cut))


def local(hidden, w_proj, pairing, loss_scale):
    rows = hidden.shape[0]
    covariance, centered, active = front(hidden, w_proj)
    inverse = factor_inverse(covariance.reshape(36, B, B))
    partner = (pairing - lax.axis_index("dp") * rows).reshape(rows, 1)
    grad_weight, grad_active = back(centered, inverse, partner, loss_scale.reshape(1, 1), w_proj, active)
    return (jnp.where(hidden > 0, grad_active, 0), grad_weight)


def solution(mesh):
    return jax.shard_map(
        local,
        mesh=mesh,
        in_specs=(P(("grp", "dp"), None), P(), P(("grp", "dp")), P()),
        out_specs=(P(("grp", "dp"), None), P(("grp", "dp"), None)),
        check_vma=False,
    )
```

```python
import functools

import jax
import jax.numpy as jnp
from jax import lax
from jax.experimental import pallas as pl
from jax.experimental.pallas import tpu as pltpu
from jax.sharding import PartitionSpec as P

MESH = pl.DeviceIdType.MESH
VMEM = pl.BlockSpec(memory_space=pltpu.VMEM)
ANY = pl.BlockSpec(memory_space=pl.ANY)


class Place:
    def __init__(self):
        grp, dp = lax.axis_index("grp"), lax.axis_index("dp")
        self.core = lax.rem(grp, 2)
        self.z = (dp // 16) * 2 + grp // 2
        self.x = lax.rem(dp // 4, 4)
        self.y = lax.rem(dp, 4)

    def device(self, axis=None, step=0, core=None):
        where = {"x": self.x, "y": self.y, "z": self.z}
        if axis is not None:
            where[axis] = lax.rem(where[axis] + step, 4)
        core = self.core if core is None else core
        z = where["z"]
        return (lax.rem(z, 2) * 2 + core, (z // 2) * 16 + where["x"] * 4 + where["y"])

    def greet(self, devices):
        barrier = pltpu.get_barrier_semaphore()
        for device in devices:
            pl.semaphore_signal(barrier, inc=1, device_id=device, device_id_type=MESH)
        pl.semaphore_wait(barrier, len(devices))


def remote(src, dst, send, recv, device):
    copy = pltpu.make_async_remote_copy(
        src_ref=src, dst_ref=dst, send_sem=send, recv_sem=recv, device_id=device, device_id_type=MESH
    )
    copy.start()
    return copy


class RingSum:
    def __init__(self, place, axis, part, relay, final, send, recv):
        self.me = getattr(place, axis)
        self.right, self.left = place.device(axis, 1), place.device(axis, 3)
        self.next, self.far, self.prev = (lax.rem(self.me + s, 4) for s in (1, 2, 3))
        self.part, self.relay, self.final, self.send, self.recv = part, relay, final, send, recv
        self.copies = []

    def copy(self, src, dst, device):
        i = len(self.copies)
        self.copies.append(remote(src, dst, self.send.at[i], self.recv.at[i], device))

    def start_far(self):
        self.copy(self.part(self.far, 0), self.relay.at[0], self.right)
        self.copy(self.part(self.far, 1), self.relay.at[1], self.left)

    def start_near(self):
        self.copy(self.part(self.next, 1), self.final.at[0, 1], self.right)
        self.copy(self.part(self.prev, 0), self.final.at[1, 0], self.left)

    def pass_on(self):
        self.copies[0].wait_recv()
        self.relay[0] += self.part(self.next, 0)[...]
        self.copy(self.relay.at[0], self.final.at[0, 0], self.right)
        self.copies[1].wait_recv()
        self.relay[1] += self.part(self.prev, 1)[...]
        self.copy(self.relay.at[1], self.final.at[1, 1], self.left)

    def finish(self):
        for copy in self.copies[2:]:
            copy.wait_recv()
        for h in (0, 1):
            yield self.part(self.me, h)[...] + self.final[0, h] + self.final[1, h]

    def drain(self):
        for copy in self.copies:
            copy.wait_send()


class RingShare(RingSum):
    def __init__(self, place, axis, part, send, recv):
        super().__init__(place, axis, part, None, None, send, recv)

    def start(self):
        for h, device in ((0, self.right), (1, self.left), (1, self.right), (0, self.left)):
            part = self.part(self.me, h)
            self.copy(part, part, device)

    def pass_on(self):
        self.copies[0].wait_recv()
        part = self.part(self.prev, 0)
        self.copy(part, part, self.right)
        self.copies[1].wait_recv()
        part = self.part(self.next, 1)
        self.copy(part, part, self.left)

    def finish(self):
        for copy in self.copies[2:]:
            copy.wait_recv()


class DirectSum:
    def __init__(self, place, axis, part, got, send, recv):
        self.me = getattr(place, axis)
        self.part, self.got, self.copies = part, got, []
        for step in (2, 1, 3):
            chunk = part(lax.rem(self.me + step, 4))
            i = step - 1
            self.copies.append(remote(chunk, got.at[i], send.at[i], recv.at[i], place.device(axis, step)))

    def finish(self):
        for copy in self.copies:
            copy.wait_recv()
        return self.part(self.me)[...] + self.got[0] + self.got[1] + self.got[2]

    def drain(self):
        for copy in self.copies:
            copy.wait_send()


class DirectShare(DirectSum):
    def __init__(self, place, axis, part, send, recv):
        self.copies = []
        mine = part(getattr(place, axis))
        for step in (2, 1, 3):
            i = step - 1
            self.copies.append(remote(mine, mine, send.at[i], recv.at[i], place.device(axis, step)))

    def finish(self):
        for copy in self.copies:
            copy.wait_recv()


PLANS = (("x", "y"), ("y", "x"))


def all_sum_steps(place, scale, value, out, relay1, final1, sum1, got2, sum2, got3, send, recv):
    portions = [(s, p) for s in range(2) for p in range(2)]

    def lane(s, p, stage):
        i = (s * 2 + p) * 5 + stage
        return send.at[i], recv.at[i]

    opposite = place.device("z", 2)
    first, second, across, third, fourth = {}, {}, {}, {}, {}
    for s in range(2):
        for p in range(2):
            first[s, p] = RingSum(
                place,
                PLANS[p][0],
                lambda k, h, s=s, p=p: value.at[s, p, k, h],
                relay1.at[s, p],
                final1.at[s, p],
                *lane(s, p, 0),
            )
            first[s, p].start_far()
        for p in range(2):
            first[s, p].start_near()
        yield
    for ring in first.values():
        ring.pass_on()
    yield
    for s, p in portions:
        for h, half in enumerate(first[s, p].finish()):
            sum1[s, p, h] = half
        second[s, p] = DirectSum(
            place,
            PLANS[p][1],
            lambda k, s=s, p=p: sum1.at[s, p, k // 2, lax.rem(k, 2)],
            got2.at[s, p],
            *lane(s, p, 1),
        )
    yield
    for s, p in portions:
        sum2[s, p] = second[s, p].finish()
        i = (s * 2 + p) * 5 + 2
        across[s, p] = remote(sum2.at[s, p], got3.at[s, p], send.at[i, 0], recv.at[i, 0], opposite)
    yield
    for s, p in portions:
        across[s, p].wait_recv()
        outer, inner = (getattr(place, axis) for axis in PLANS[p])
        out[s, p, outer, inner // 2, lax.rem(inner, 2)] = (sum2[s, p] + got3[s, p]) * scale
        third[s, p] = DirectShare(
            place,
            PLANS[p][1],
            lambda k, s=s, p=p, outer=outer: out.at[s, p, outer, k // 2, lax.rem(k, 2)],
            *lane(s, p, 3),
        )
    yield
    for s, p in portions:
        third[s, p].finish()
        fourth[s, p] = RingShare(
            place, PLANS[p][0], lambda k, h, s=s, p=p: out.at[s, p, k, h], *lane(s, p, 4)
        )
        fourth[s, p].start()
    yield
    for ring in fourth.values():
        ring.pass_on()
    for ring in fourth.values():
        ring.finish()
    for group in (first, second, third, fourth):
        for ring in group.values():
            ring.drain()
    for copy in across.values():
        copy.wait_send()
    yield


FAN = [(y, z) for y in range(4) for z in range(2)][1:]


class SmallSum:
    def __init__(self, place, source, middle, got_row, got_rest, send, recv):
        self.source, self.middle, self.got_row, self.got_rest = source, middle, got_row, got_rest
        self.send, self.recv, self.rest = send, recv, self.fan(place)
        self.copies = [
            remote(source, got_row.at[i], send.at[i], recv.at[i], place.device("x", i + 1)) for i in range(3)
        ]

    @staticmethod
    def fan(place):
        devices = []
        for y, z in FAN:
            far = lax.rem(place.z + 2 * z, 4)
            devices.append(
                (lax.rem(far, 2) * 2 + place.core, (far // 2) * 16 + place.x * 4 + lax.rem(place.y + y, 4))
            )
        return devices

    def pass_on(self):
        for copy in self.copies:
            copy.wait_recv()
        self.middle[...] = self.source[...] + self.got_row[0] + self.got_row[1] + self.got_row[2]
        for n in range(7):
            i = 3 + n
            self.copies.append(
                remote(self.middle, self.got_rest.at[n], self.send.at[i], self.recv.at[i], self.rest[n])
            )

    def finish(self):
        for copy in self.copies[3:]:
            copy.wait_recv()
        total = self.middle[...]
        for n in range(7):
            total = total + self.got_rest[n]
        return total

    def drain(self):
        for copy in self.copies:
            copy.wait_send()


precise = lax.Precision.HIGHEST
N, B = 1024, 128


def spread_row(tile, row):
    return jnp.broadcast_to(tile[row : row + 1, :], (8, B))


def spread_column(tile, column):
    return jnp.broadcast_to(tile[:, column : column + 1], (8, B))


def invert_pair(a, b, c):
    det = a * c - b * b
    r = 1.0 / det
    return c * r, -b * r, a * r, det


def factor_rows(a, b, c, det, row0, row1):
    s = lax.rsqrt(a)
    first = row0 * s
    return first, (row1 - (b * s) * first) * (lax.rsqrt(det) * (a * s))


def leaf_steps(block, store):
    sub = lax.broadcasted_iota(jnp.int32, (8, B), 0)
    lane = lax.broadcasted_iota(jnp.int32, (8, B), 1)
    a = [block[8 * g : 8 * g + 8, :] for g in range(16)]
    w = [jnp.where(lane == sub + 8 * g, 1.0, 0.0) for g in range(16)]
    four = range(4)
    d = {(l, m): spread_row(spread_column(a[0], m), l) for l in four for m in range(l + 1)}
    finished = None
    for step in range(32):
        g, r, j = step // 2, 4 * (step % 2), 4 * step
        p, q, s, det = invert_pair(d[0, 0], d[1, 0], d[1, 1])
        k = [[p * d[n, 0] + q * d[n, 1], q * d[n, 0] + s * d[n, 1]] for n in (2, 3)]
        s00 = d[2, 2] - (d[2, 0] * k[0][0] + d[2, 1] * k[0][1])
        s10 = d[3, 2] - (d[3, 0] * k[0][0] + d[3, 1] * k[0][1])
        s11 = d[3, 3] - (d[3, 0] * k[1][0] + d[3, 1] * k[1][1])
        u, v, t, det2 = invert_pair(s00, s10, s11)
        rows = [spread_row(a[g], r + n) for n in four]
        wrows = [spread_row(w[g], r + n) for n in four]
        old = d
        if step < 31:
            ng, nr = (step + 1) // 2, 4 * ((step + 1) % 2)
            tile = a[ng]
            near = [spread_column(tile, j + n) for n in four]
            far = [spread_column(tile, j + 4 + n) for n in four]
            gap = [[spread_row(near[n], nr + l) for n in four] for l in four]
            ha = [[p * gap[l][0] + q * gap[l][1], q * gap[l][0] + s * gap[l][1]] for l in four]
            gb = [[gap[l][n] - (k[n - 2][0] * gap[l][0] + k[n - 2][1] * gap[l][1]) for n in (2, 3)] for l in four]
            hb = [[u * gb[l][0] + v * gb[l][1], v * gb[l][0] + t * gb[l][1]] for l in four]
            d = {}
            for l in four:
                for m in range(l + 1):
                    before = spread_row(far[m], nr + l) - (gap[l][0] * ha[m][0] + gap[l][1] * ha[m][1])
                    d[l, m] = before - (gb[l][0] * hb[m][0] + gb[l][1] * hb[m][1])

        def solve(r0, r1, r2, r3):
            r2 = r2 - (k[0][0] * r0 + k[0][1] * r1)
            r3 = r3 - (k[1][0] * r0 + k[1][1] * r1)
            x2, x3 = u * r2 + v * r3, v * r2 + t * r3
            x0 = (p * r0 + q * r1) - (k[0][0] * x2 + k[1][0] * x3)
            x1 = (q * r0 + s * r1) - (k[0][1] * x2 + k[1][1] * x3)
            return (x0, x1, x2, x3), r2, r3

        x, _, _ = solve(*rows)
        xw, w2, w3 = solve(*wrows)
        ready = factor_rows(old[0, 0], old[1, 0], old[1, 1], det, wrows[0], wrows[1])
        ready += factor_rows(s00, s10, s11, det2, w2, w3)
        if r == 0:
            finished = ready[0]
        for n, row in enumerate(ready):
            if r + n:
                finished = jnp.where(sub == r + n, row, finished)
        if r == 4:
            store(g, finished)
        for tile in range(g if r == 0 else g + 1, 16):
            mult = [spread_column(a[tile], j + n) for n in four]
            if tile == g:
                mult = [jnp.where(sub >= 4, m, 0.0) for m in mult]
            a[tile] = a[tile] - ((mult[0] * x[0] + mult[1] * x[1]) + (mult[2] * x[2] + mult[3] * x[3]))
            w[tile] = w[tile] - ((mult[0] * xw[0] + mult[1] * xw[1]) + (mult[2] * xw[2] + mult[3] * xw[3]))
        yield step


def three_parts(value):
    high = value.astype(jnp.bfloat16)
    rest = value - high.astype(jnp.float32)
    middle = rest.astype(jnp.bfloat16)
    return high, middle, (rest - middle.astype(jnp.float32)).astype(jnp.bfloat16)


def diagonal_block(block, diagonals, i):
    row = lax.broadcasted_iota(jnp.int32, (B, B), 0)
    lane = lax.broadcasted_iota(jnp.int32, (B, B), 1)
    if i % 2:
        strict = jnp.where(lane > row, block, 0.0)
        middle = jnp.broadcast_to(diagonals[i // 2 : i // 2 + 1, :], (B, B))
    else:
        strict = jnp.where(row > lane, block, 0.0)
        middle = block
    return strict + strict.T + jnp.where(row == lane, middle, 0.0)


def inverse_kernel(packed_in, diagonals, out, packed, whole, left, right, work, loads, stores):
    ahead = pltpu.make_async_copy(packed_in.at[:2], packed.at[:2], loads.at[0])
    ahead.start()
    rest = pltpu.make_async_copy(packed_in.at[2:], packed.at[2:], loads.at[1])
    rest.start()

    def store(g, tile):
        work[8 * g : 8 * g + 8, :] = tile

    def rows_of(i):
        return pl.ds(pl.multiple_of(i * B, B), B)

    ahead.wait()
    for _ in leaf_steps(diagonal_block(packed[SLOTS[0]], None, 0), store):
        pass
    rest.wait()
    for i in range(8):
        for j in range(i):
            block = packed[SLOTS[i, j]]
            whole[B * i : B * i + B, B * j : B * j + B] = block
            whole[B * j : B * j + B, B * i : B * i + B] = block.T
        whole[B * i : B * i + B, B * i : B * i + B] = diagonal_block(packed[SLOTS[i // 2]], diagonals, i)
    whole[N:, :] = jnp.zeros((B, N), jnp.float32)
    lane = lax.broadcasted_iota(jnp.int32, (B, B), 1)
    sub = lax.broadcasted_iota(jnp.int32, (B, B), 0)
    unit = jnp.where(lane == sub, 1.0, 0.0)

    def leave(k):
        return pltpu.make_async_copy(whole.at[rows_of(k)], out.at[rows_of(k)], stores.at[k])

    @pl.loop(0, 7)
    def _(k):
        here, below = rows_of(k), rows_of(k + 1)
        factor = work[...]
        first = dot(factor, whole[here, below], ((1,), (0,)))
        whole[below, below] -= dot(first, first, ((0,), (0,)))
        block = whole[below, below]
        whole[here, here] = unit

        def make_left(t):
            def job():
                there = rows_of(jnp.minimum(k + 1 + t, 8))
                high, middle, low = three_parts(dot(whole[there, here], factor, ((1,), (1,))))
                for n, part in enumerate((high, high, middle, middle, high, low)):
                    left[t * B : t * B + B, n * B : n * B + B] = part
                whole[there, here] = jnp.zeros((B, B), jnp.float32)

            return job

        def make_right(c):
            def job():
                columns = slice(256 * c, 256 * c + 256)
                panel = dot(factor, whole[here, columns], ((1,), (0,)))
                whole[here, columns] = panel
                high, middle, low = three_parts(panel)
                for n, part in enumerate((high, middle, high, middle, low, high)):
                    right[n * B : n * B + B, columns] = part

            return job

        def update(t, c):
            def job():
                columns = slice(256 * c, 256 * c + 256)
                there = rows_of(jnp.minimum(k + 1 + t, 8))
                term = jnp.dot(
                    left[t * B : t * B + B, :], right[:, columns], preferred_element_type=jnp.float32
                )
                if t == 0:
                    place = lax.broadcasted_iota(jnp.int32, (B, 256), 1) + 256 * c
                    term = jnp.where((place >= (k + 1) * B) & (place < (k + 2) * B), 0.0, term)
                whole[there, columns] -= term

            return job

        jobs = [make_right(c) for c in range(4)] + [make_left(t) for t in range(7)]
        jobs += [update(t, c) for t in range(7) for c in range(4)]
        done = 0
        for step in leaf_steps(block, store):
            upto = len(jobs) * (step + 1) // 32
            for job in jobs[done:upto]:
                job()
            done = upto
        whole[here, below] = jnp.zeros((B, B), jnp.float32)
        leave(k).start()

    whole[7 * B : N, 7 * B :] = unit
    whole[7 * B : N, :] = dot(work[...], whole[7 * B : N, :], ((1,), (0,)))
    leave(7).start()
    for k in range(8):
        leave(k).wait()


def factor_inverse(packed, diagonals):
    return pl.pallas_call(
        inverse_kernel,
        out_shape=jax.ShapeDtypeStruct((N, N), jnp.float32),
        in_specs=[ANY, VMEM],
        out_specs=ANY,
        scratch_shapes=[
            pltpu.VMEM((32, B, B), jnp.float32),
            pltpu.VMEM((N + B, N), jnp.float32),
            pltpu.VMEM((7 * B, 6 * B), jnp.bfloat16),
            pltpu.VMEM((6 * B, N), jnp.bfloat16),
            pltpu.VMEM((B, B), jnp.float32),
            pltpu.SemaphoreType.DMA((2,)),
            pltpu.SemaphoreType.DMA((8,)),
        ],
        compiler_params=pltpu.CompilerParams(vmem_limit_bytes=60 * 2**20),
    )(packed, diagonals)


def dot(a, b, over, precision=precise):
    return lax.dot_general(a, b, (over, ((), ())), precision=precision, preferred_element_type=jnp.float32)


def make_all_sum_scratch():
    floats = lambda *lead: pltpu.VMEM((2, 2, *lead, 64, 128), jnp.float32)
    return [
        floats(2, 2),
        floats(2, 2, 2),
        floats(2, 2),
        floats(3),
        floats(),
        floats(),
        pltpu.SemaphoreType.DMA((20, 6)),
        pltpu.SemaphoreType.DMA((20, 6)),
    ]


CUT = (2, 2, 4, 2, 2, 64, 128)


SLOTS = {}
for _i in range(8):
    for _j in range(_i):
        SLOTS[_i, _j] = len(SLOTS)
    if _i % 2:
        SLOTS[_i // 2] = len(SLOTS)


def put_block(value, slot, block):
    for half in range(2):
        n = 2 * SLOTS[slot] + half
        value[n // 32, n // 16 % 2, n // 4 % 4, n // 2 % 2, n % 2] = block[64 * half : 64 * half + 64, :]


def get_block(value, slot):
    parts = []
    for half in range(2):
        n = 2 * SLOTS[slot] + half
        parts.append(value[n // 32, n // 16 % 2, n // 4 % 4, n // 2 % 2, n % 2])
    return jnp.concatenate(parts, axis=0)


def small_scratch():
    floats = lambda *lead: pltpu.VMEM((*lead, 16, B), jnp.float32)
    return [floats(), floats(), floats(3), floats(7), pltpu.SemaphoreType.DMA((10,)), pltpu.SemaphoreType.DMA((10,))]


def front_kernel(
    hidden_in, proj_in, covariance, extra_out, centered_out, active_out,
    centered, active, hidden, proj, local_sum, row_sum, got_row, got_rest, odd, extra, *more_scratch,
):
    small, more_scratch = more_scratch[:5], more_scratch[5:]
    front_steps(
        hidden_in, proj_in, covariance, extra_out, centered_out, active_out, centered, active, hidden, proj,
        local_sum, row_sum, got_row, got_rest, odd, extra, small, *more_scratch,
    )


def front_steps(
    hidden_in, proj_in, covariance, extra_out, centered_out, active_out,
    centered, active, hidden, proj, local_sum, row_sum, got_row, got_rest, odd, extra, small, value, outgoing, arrived,
    loads, core_send, core_recv, sum_send, sum_recv, *scratch,
):
    place = Place()
    rows, width = centered.shape
    deep = proj.shape[1]
    copies = []
    for i in range(4):
        copies.append(pltpu.make_async_copy(hidden_in.at[:, i * deep : i * deep + deep], hidden.at[i], loads.at[0, i]))
        copies.append(pltpu.make_async_copy(proj_in.at[i * deep : i * deep + deep], proj.at[i], loads.at[1, i]))
    for copy in copies[:4]:
        copy.start()
    line = [place.device("x", step) for step in (1, 2, 3)]
    rest = SmallSum.fan(place)
    other = place.device(core=1 - place.core)
    barrier = pltpu.get_barrier_semaphore()
    for device in line + rest + [other]:
        pl.semaphore_signal(barrier, inc=1, device_id=device, device_id_type=MESH)
    for i in range(4):
        copies[2 * i].wait()
        copies[2 * i + 1].wait()
        for copy in copies[2 * i + 4 : 2 * i + 6]:
            copy.start()
        rows_here = jnp.maximum(hidden[i], 0.0)
        for c in range(0, width, 256):
            product = jnp.dot(rows_here, proj[i, :, c : c + 256], preferred_element_type=jnp.float32)
            if i:
                product = product + centered[:, c : c + 256]
            centered[:, c : c + 256] = product
            if i == 3:
                total = jnp.sum(product, axis=0, keepdims=True)
                for q in (0, 128):
                    local_sum[(c + q) // 128 : (c + q) // 128 + 1, :] = total[:, q : q + 128]
                centered[:, c : c + 256] = product - total / rows
    pl.semaphore_wait(barrier, len(line + rest) + 1)
    mean = SmallSum(place, local_sum, row_sum, got_row, got_rest, sum_send, sum_recv)
    for i in range(8):
        wide = dot(centered[:, B * i : B * i + B], centered[:, : B * (i + 1)], ((0,), (0,)))
        for j in range(i):
            put_block(value, (i, j), wide[:, B * j : B * j + B])
        if i % 2:
            odd[i // 2] = wide[:, B * i :]
        else:
            put_block(value, i // 2, wide[:, B * i :])
        if i == 4:
            mean.pass_on()
    total = mean.finish()
    count = rows * 32
    shift = local_sum[...] / rows - total / count
    upright = (shift * rows).T
    steps = all_sum_steps(place, 1.0 / count, value, covariance, *scratch)
    row = lax.broadcasted_iota(jnp.int32, (B, B), 0)
    lane = lax.broadcasted_iota(jnp.int32, (B, B), 1)
    extra[...] = jnp.zeros_like(extra)
    for i in range(8):
        column = jnp.broadcast_to(upright[:, i : i + 1], (B, B))
        for j in range(i):
            put_block(value, (i, j), get_block(value, (i, j)) + column * shift[j : j + 1, :])
        if i % 2:
            even = get_block(value, i // 2) + before
            block = odd[i // 2] + column * shift[i : i + 1, :]
            put_block(value, i // 2, jnp.where(row >= lane, even, block))
            extra[i // 2 : i // 2 + 1, :] = jnp.sum(jnp.where(row == lane, block, 0.0), axis=0, keepdims=True)
        before = column * shift[i : i + 1, :]
        if i == 5:
            next(steps)
    next(steps)
    diagonals = SmallSum(place, extra, *small)
    half = deep
    for part in range(2):
        kept = jnp.maximum(hidden[2 * part + 1 - place.core].astype(jnp.float32), 0.0)
        outgoing[:, part * half : part * half + half] = kept
    swap = remote(outgoing, arrived, core_send.at[0], core_recv.at[0], other)
    for i in range(8):
        centered[:, B * i : B * i + B] += shift[i : i + 1, :]
    results = [pltpu.make_async_copy(centered, centered_out, loads.at[0, 0])]
    results[0].start()

    def turn(q):
        part, inside = divmod(q * 256, half)
        mine = hidden[2 * part + place.core, :, inside : inside + 256].astype(jnp.float32)
        active[q * 256 : q * 256 + 256, :rows] = jnp.maximum(mine, 0.0).T.astype(active.dtype)

    def turn_arrived(q):
        active[q * 256 : q * 256 + 256, rows:] = arrived[:, q * 256 : q * 256 + 256].T.astype(active.dtype)

    work = [functools.partial(turn, q) for q in range(8)]
    for job in work[:4]:
        job()
    next(steps)
    for job in work[4:]:
        job()
    diagonals.pass_on()
    swap.wait_recv()
    later = [functools.partial(turn_arrived, q) for q in range(8)]
    for _ in steps:
        for job in later[:4]:
            job()
        later = later[4:]
    for job in later:
        job()
    results.append(pltpu.make_async_copy(active, active_out, loads.at[1, 0]))
    results[1].start()
    for copy in results:
        copy.wait()
    extra_out[...] = diagonals.finish() * (1.0 / count)
    swap.wait_send()
    mean.drain()
    diagonals.drain()


def front(hidden, proj):
    rows, depth = hidden.shape
    width = proj.shape[1]
    f32, bf16 = jnp.float32, jnp.bfloat16
    return pl.pallas_call(
        front_kernel,
        out_shape=(
            jax.ShapeDtypeStruct(CUT, f32),
            jax.ShapeDtypeStruct((16, B), f32),
            jax.ShapeDtypeStruct((rows, width), f32),
            jax.ShapeDtypeStruct((depth // 2, 2 * rows), bf16),
        ),
        in_specs=[ANY, ANY],
        out_specs=(VMEM, VMEM, ANY, ANY),
        scratch_shapes=[
            pltpu.VMEM((rows, width), f32),
            pltpu.VMEM((depth // 2, 2 * rows), bf16),
            pltpu.VMEM((4, rows, depth // 4), bf16),
            pltpu.VMEM((4, depth // 4, width), bf16),
            pltpu.VMEM((8, B), f32),
            pltpu.VMEM((8, B), f32),
            pltpu.VMEM((3, 8, B), f32),
            pltpu.VMEM((7, 8, B), f32),
            pltpu.VMEM((4, B, B), f32),
            *small_scratch(),
            pltpu.VMEM(CUT, f32),
            pltpu.VMEM((rows, depth // 2), f32),
            pltpu.VMEM((rows, depth // 2), f32),
            pltpu.SemaphoreType.DMA((2, 4)),
            pltpu.SemaphoreType.DMA((1,)),
            pltpu.SemaphoreType.DMA((1,)),
            pltpu.SemaphoreType.DMA((10,)),
            pltpu.SemaphoreType.DMA((10,)),
            *make_all_sum_scratch(),
        ],
        compiler_params=pltpu.CompilerParams(
            collective_id=0, has_side_effects=True, vmem_limit_bytes=60 * 2**20
        ),
    )(hidden, proj)


ORDERS = (("x", "y", "z"), ("y", "z", "x"), ("z", "x", "y"))
WIDTHS = (384, 384, 256)


def three_terms(ref, value, block, columns, weight):
    high = value.astype(jnp.bfloat16)
    low = (value - high.astype(jnp.float32)).astype(jnp.bfloat16)
    for n, part in enumerate((high, low, high) if weight else (high, high, low)):
        if weight:
            start = block // 2 * 768 + n * 256 + block % 2 * B
            ref[start : start + value.shape[0], columns] = part
        else:
            ref[:, block * 768 + n * 256 : block * 768 + n * 256 + 256] = part


def back_kernel(
    centered_in, inverse_in, pairing, scale, proj_in, active_in, out, grad_hidden,
    centered, inverse, white, grad_white, there, value, packed, left, right, proj, active, grad_there, grad, staged,
    swap_send, swap_recv, core_send, core_recv, local, stream, drop, early, extra, *scratch,
):
    small, sum_scratch, scratch = scratch[:5], scratch[5:13], scratch[13:]
    send, recv = scratch[-2:]
    place = Place()
    rows, width = white.shape
    count = rows * 32
    loads = []
    for i in range(4):
        part = slice(256 * i, 256 * i + 256)
        loads.append(pltpu.make_async_copy(centered_in.at[:, part], centered.at[:, part], early.at[0, i]))
        loads.append(pltpu.make_async_copy(inverse_in.at[part], inverse.at[part], early.at[1, i]))
    for copy in loads[:4]:
        copy.start()
    load_active = pltpu.make_async_copy(active_in, active, local.at[0])

    def load_proj(t):
        slot = lax.rem(t, 2)
        start = pl.multiple_of(t * 512, 512)
        return pltpu.make_async_copy(proj_in.at[pl.ds(start, 512)], proj.at[slot], stream.at[slot])

    other = place.device(core=1 - place.core)
    peers = [place.device(axis, step) for axis in "xyz" for step in (1, 2, 3)] + [other]
    peers += [device for device, (y, z) in zip(SmallSum.fan(place), FAN) if y and z]
    barrier = pltpu.get_barrier_semaphore()
    for device in peers:
        pl.semaphore_signal(barrier, inc=1, device_id=device, device_id_type=MESH)

    swaps = []
    squares = jnp.zeros((rows, 1), jnp.float32)
    for i in range(4):
        columns = slice(256 * i, 256 * i + 256)
        loads[2 * i].wait()
        loads[2 * i + 1].wait()
        for copy in loads[2 * i + 4 : 2 * i + 6]:
            copy.start()
        tile = dot(centered[:, : 256 * i + 256], inverse[columns, : 256 * i + 256], ((1,), (1,)))
        white[:, columns] = tile
        if i == 1:
            pl.semaphore_wait(barrier, len(peers))
        for n in {1: (0, 1), 2: (2,), 3: (3,)}.get(i, ()):
            part = slice(256 * n, 256 * n + 256)
            swaps.append(remote(white.at[:, part], there.at[:, part], swap_send.at[n], swap_recv.at[n], other))
        squares = squares + jnp.sum(tile * tile, axis=1, keepdims=True)
    load_active.start()
    load_proj(0).start()
    load_proj(1).start()
    over = 1.0 / jnp.sqrt(squares + 1e-06)
    lane = lax.broadcasted_iota(jnp.int32, (rows, rows), 1)
    chosen = jnp.where(pairing[...] == lane, 1.0, 0.0).astype(jnp.bfloat16)
    squares = jnp.zeros((rows, 1), jnp.float32)
    for i in range(4):
        swaps[i].wait_recv()
        tile = there[:, 256 * i : 256 * i + 256]
        squares = squares + jnp.sum(tile * tile, axis=1, keepdims=True)
    over_there = 1.0 / jnp.sqrt(squares + 1e-06)
    factor = 4.0 * scale[0, 0]
    along = jnp.zeros((rows, 1), jnp.float32)
    for i in range(4):
        columns = slice(256 * i, 256 * i + 256)
        partner = [
            jnp.dot(chosen, part, preferred_element_type=jnp.float32)
            for part in three_parts(there[:, columns] * over_there)
        ]
        normals = white[:, columns] * over
        change = factor * (normals - ((partner[2] + partner[1]) + partner[0]))
        grad_white[:, columns] = change
        along = along + jnp.sum(normals * change, axis=1, keepdims=True)
    totals = []
    for i in range(4):
        columns = slice(256 * i, 256 * i + 256)
        change = (grad_white[:, columns] - white[:, columns] * (over * along)) * over
        grad_white[:, columns] = change
        total = jnp.sum(change, axis=0, keepdims=True)
        totals += [total[:, :B], total[:, B:]]

    row = lax.broadcasted_iota(jnp.int32, (B, B), 0)
    lane = lax.broadcasted_iota(jnp.int32, (B, B), 1)
    steps = all_sum_steps(place, 1.0, value, packed, *sum_scratch)
    extra[...] = jnp.zeros_like(extra)
    for i in range(8):
        wide = dot(grad_white[:, B * i : B * i + B], white[:, : B * (i + 1)], ((0,), (0,)), lax.Precision.HIGH)
        for j in range(i):
            put_block(value, (i, j), wide[:, B * j : B * j + B])
        block = wide[:, B * i :]
        extra[8 + i : 9 + i, :] = totals[i]
        if i % 2:
            put_block(value, i // 2, jnp.where(row >= lane, even, block.T))
            extra[i // 2 : i // 2 + 1, :] = jnp.sum(jnp.where(row == lane, block, 0.0), axis=0, keepdims=True)
        even = block
        if i == 5:
            next(steps)
    next(steps)
    extras = SmallSum(place, extra, *small)
    next(steps)
    extras.pass_on()
    for i in range(4):
        three_terms(left, white[:, 256 * i : 256 * i + 256], i, None, False)
    for swap in swaps:
        swap.wait_send()
    for _ in steps:
        pass
    extra_total = extras.finish()
    extras.drain()

    for c in range(4):
        for q in (0, 1):
            j, at = 2 * c + q, slice(B * q, B * q + B)
            for i in range(8):
                if i > j:
                    block = get_block(packed, (i, j))
                elif i < j:
                    block = get_block(packed, (j, i)).T
                else:
                    grad_white[:, B * i : B * i + B] -= extra_total[8 + i : 9 + i, :] / count
                    block = diagonal_block(get_block(packed, i // 2), extra_total, i)
                three_terms(right, block, i, at, True)
        grad_white[:, 256 * c : 256 * c + 256] -= (
            jnp.dot(left[...], right[...], preferred_element_type=jnp.float32) / count
        )
    for i in range(4):
        three_terms(left, grad_white[:, 256 * i : 256 * i + 256], i, None, False)
    grads = []

    def gradient(c):
        columns = slice(256 * c, 256 * c + 256)
        for i in range(2 * c, 8):
            three_terms(right, inverse[B * i : B * i + B, columns], i, slice(None), True)
        tile = jnp.dot(left[:, 768 * c :], right[768 * c :, :], preferred_element_type=jnp.float32)
        white[:, columns] = tile
        grad[:rows, columns] = tile.astype(grad.dtype)
        grads.append(
            remote(white.at[:, columns], grad_there.at[:, columns], core_send.at[c], core_recv.at[c], other)
        )

    def gradient_there(c):
        columns = slice(256 * c, 256 * c + 256)
        grads[c].wait_recv()
        grad[rows:, columns] = grad_there[:, columns].astype(grad.dtype)

    parts, relays, finals, sums = [], [], [], []
    for p in range(3):
        parts.append(scratch[8 * p])
        relays.append(scratch[8 * p + 1 : 8 * p + 3])
        finals.append(scratch[8 * p + 3 : 8 * p + 6])
        sums.append(scratch[8 * p + 6 : 8 * p + 8])

    def multiply(p, k):
        begin = sum(WIDTHS[:p])
        high, low = k // 2, lax.rem(k, 2)
        if p == 0:
            left = active[:, :, k]
        elif p == 1:
            left = active[:, :, :, k]
        else:
            left = active[low, high]
        product = jnp.dot(
            left.reshape(512, 2 * rows), grad[:, begin : begin + WIDTHS[p]], preferred_element_type=jnp.float32
        )
        for n in range(16):
            block = product[32 * n : 32 * n + 32]
            if p == 0:
                parts[p][k, n % 4 // 2, n % 2, n // 4 % 2, n // 8] = block
            elif p == 1:
                parts[p][k, n // 4 % 2, n // 8, n % 4 // 2, n % 2] = block
            else:
                parts[p][k, n // 8, n // 4 % 2, n % 4 // 2, n % 2] = block

    def hidden_tile(t):
        slot = lax.rem(t, 2)
        load_proj(t).wait()
        product = lax.dot_general(
            grad[:rows, :], proj[slot], (((1,), (1,)), ((), ())), preferred_element_type=jnp.float32
        )

        def leave(t):
            columns = pl.ds(pl.multiple_of(t * 512, 512), 512)
            return pltpu.make_async_copy(staged.at[slot], grad_hidden.at[:, columns], drop.at[slot])

        @pl.when(t >= 2)
        def _():
            leave(t - 2).wait()

        staged[slot] = product.astype(grad_hidden.dtype)
        leave(t).start()

        @pl.when(t < 6)
        def _():
            load_proj(t + 2).start()

        @pl.when(t == 7)
        def _():
            leave(t).wait()
            pltpu.make_async_copy(
                staged.at[1 - slot], grad_hidden.at[:, pl.ds(6 * 512, 512)], drop.at[1 - slot]
            ).wait()

    first, second, third = {}, {}, {}

    def begin(p):
        i = p * 3
        first[p] = ring = RingSum(
            place, ORDERS[p][0], lambda k, h: parts[p].at[k, h], relays[p][0], finals[p][0], send.at[i], recv.at[i]
        )
        multiply(p, ring.far)
        ring.start_far()
        multiply(p, ring.next)
        multiply(p, ring.prev)
        ring.start_near()

    for c in (0, 1, 2):
        gradient(c)
    load_active.wait()
    gradient_there(0)
    gradient_there(1)
    begin(0)
    gradient(3)
    gradient_there(2)
    begin(1)
    gradient_there(3)
    begin(2)
    for p in range(3):
        multiply(p, first[p].me)
    pl.loop(0, 4)(hidden_tile)
    for p in range(3):
        first[p].pass_on()
    pl.loop(4, 8)(hidden_tile)
    for p in range(3):
        for h, half in enumerate(first[p].finish()):
            sums[p][0][h] = half
        i = p * 3 + 1
        second[p] = RingSum(
            place,
            ORDERS[p][1],
            lambda k, h, p=p: sums[p][0].at[k // 2, lax.rem(k, 2), h],
            relays[p][1],
            finals[p][1],
            send.at[i],
            recv.at[i],
        )
        second[p].start_far()
        second[p].start_near()
    for p in range(3):
        second[p].pass_on()
    for p in range(3):
        for h, half in enumerate(second[p].finish()):
            sums[p][1][h] = half
        i = p * 3 + 2
        third[p] = DirectSum(
            place,
            ORDERS[p][2],
            lambda k, p=p: sums[p][1].at[k // 2, lax.rem(k, 2)],
            finals[p][2],
            send.at[i],
            recv.at[i],
        )
    for p in range(3):
        start = sum(WIDTHS[:p])
        out[:, start : start + WIDTHS[p]] = third[p].finish().astype(out.dtype)
    for group in (first, second, third):
        for ring in group.values():
            ring.drain()
    for swap in grads:
        swap.wait_send()


def back(centered, inverse, pairing, scale, proj, active):
    rows, width = centered.shape
    depth = proj.shape[0]
    bf16, f32 = jnp.bfloat16, jnp.float32
    cut = (2, 2, 4, 4, 32, 2 * rows)
    scratch = [
        pltpu.VMEM((rows, width), f32),
        pltpu.VMEM((width, width), f32),
        pltpu.VMEM((rows, width), f32),
        pltpu.VMEM((rows, width), f32),
        pltpu.VMEM((rows, width), f32),
        pltpu.VMEM(CUT, f32),
        pltpu.VMEM(CUT, f32),
        pltpu.VMEM((rows, 3 * width), bf16),
        pltpu.VMEM((3 * width, 256), bf16),
        pltpu.VMEM((2, 512, width), bf16),
        pltpu.VMEM(cut, bf16),
        pltpu.VMEM((rows, width), f32),
        pltpu.VMEM((2 * rows, width), bf16),
        pltpu.VMEM((2, rows, 512), bf16),
        pltpu.SemaphoreType.DMA((4,)),
        pltpu.SemaphoreType.DMA((4,)),
        pltpu.SemaphoreType.DMA((4,)),
        pltpu.SemaphoreType.DMA((4,)),
        pltpu.SemaphoreType.DMA((1,)),
        pltpu.SemaphoreType.DMA((2,)),
        pltpu.SemaphoreType.DMA((2,)),
        pltpu.SemaphoreType.DMA((2, 4)),
        *small_scratch(),
        *make_all_sum_scratch(),
    ]
    for columns in WIDTHS:
        scratch += [
            pltpu.VMEM((*lead, 32, columns), f32)
            for lead in [
                (4, 2, 2, 2, 2),
                (2, 2, 2, 2),
                (2, 2),
                (2, 2, 2, 2, 2),
                (2, 2, 2),
                (3,),
                (2, 2, 2, 2),
                (2, 2),
            ]
        ]
    scratch += [pltpu.SemaphoreType.DMA((9, 6)), pltpu.SemaphoreType.DMA((9, 6))]
    return pl.pallas_call(
        back_kernel,
        out_shape=(jax.ShapeDtypeStruct((32, width), bf16), jax.ShapeDtypeStruct((rows, depth), bf16)),
        in_specs=[ANY, ANY, VMEM, pl.BlockSpec(memory_space=pltpu.SMEM), ANY, ANY],
        out_specs=(VMEM, ANY),
        scratch_shapes=scratch,
        compiler_params=pltpu.CompilerParams(
            collective_id=1, has_side_effects=True, vmem_limit_bytes=60 * 2**20
        ),
    )(centered, inverse, pairing, scale, proj, active.reshape(cut))


def local(hidden, w_proj, pairing, loss_scale):
    rows = hidden.shape[0]
    covariance, diagonals, centered, active = front(hidden, w_proj)
    inverse = factor_inverse(covariance.reshape(32, B, B), diagonals)
    partner = (pairing - lax.axis_index("dp") * rows).reshape(rows, 1)
    grad_weight, grad_active = back(centered, inverse, partner, loss_scale.reshape(1, 1), w_proj, active)
    return (jnp.where(hidden > 0, grad_active, 0), grad_weight)


def solution(mesh):
    return jax.shard_map(
        local,
        mesh=mesh,
        in_specs=(P(("grp", "dp"), None), P(), P(("grp", "dp")), P()),
        out_specs=(P(("grp", "dp"), None), P(("grp", "dp"), None)),
        check_vma=False,
    )
```

```python
import functools

import jax
import jax.numpy as jnp
from jax import lax
from jax.experimental import pallas as pl
from jax.experimental.pallas import tpu as pltpu
from jax.sharding import PartitionSpec as P

MESH = pl.DeviceIdType.MESH
VMEM = pl.BlockSpec(memory_space=pltpu.VMEM)
ANY = pl.BlockSpec(memory_space=pl.ANY)


class Place:
    def __init__(self):
        grp, dp = lax.axis_index("grp"), lax.axis_index("dp")
        self.core = lax.rem(grp, 2)
        self.z = (dp // 16) * 2 + grp // 2
        self.x = lax.rem(dp // 4, 4)
        self.y = lax.rem(dp, 4)

    def device(self, axis=None, step=0, core=None):
        where = {"x": self.x, "y": self.y, "z": self.z}
        if axis is not None:
            where[axis] = lax.rem(where[axis] + step, 4)
        core = self.core if core is None else core
        z = where["z"]
        return (lax.rem(z, 2) * 2 + core, (z // 2) * 16 + where["x"] * 4 + where["y"])

    def greet(self, devices):
        barrier = pltpu.get_barrier_semaphore()
        for device in devices:
            pl.semaphore_signal(barrier, inc=1, device_id=device, device_id_type=MESH)
        pl.semaphore_wait(barrier, len(devices))


def remote(src, dst, send, recv, device):
    copy = pltpu.make_async_remote_copy(
        src_ref=src, dst_ref=dst, send_sem=send, recv_sem=recv, device_id=device, device_id_type=MESH
    )
    copy.start()
    return copy


class RingSum:
    def __init__(self, place, axis, part, relay, final, send, recv):
        self.me = getattr(place, axis)
        self.right, self.left = place.device(axis, 1), place.device(axis, 3)
        self.next, self.far, self.prev = (lax.rem(self.me + s, 4) for s in (1, 2, 3))
        self.part, self.relay, self.final, self.send, self.recv = part, relay, final, send, recv
        self.copies = []

    def copy(self, src, dst, device):
        i = len(self.copies)
        self.copies.append(remote(src, dst, self.send.at[i], self.recv.at[i], device))

    def start_far(self):
        self.copy(self.part(self.far, 0), self.relay.at[0], self.right)
        self.copy(self.part(self.far, 1), self.relay.at[1], self.left)

    def start_near(self):
        self.copy(self.part(self.next, 1), self.final.at[0, 1], self.right)
        self.copy(self.part(self.prev, 0), self.final.at[1, 0], self.left)

    def pass_on(self):
        self.copies[0].wait_recv()
        self.relay[0] += self.part(self.next, 0)[...]
        self.copy(self.relay.at[0], self.final.at[0, 0], self.right)
        self.copies[1].wait_recv()
        self.relay[1] += self.part(self.prev, 1)[...]
        self.copy(self.relay.at[1], self.final.at[1, 1], self.left)

    def finish(self):
        for copy in self.copies[2:]:
            copy.wait_recv()
        for h in (0, 1):
            yield self.part(self.me, h)[...] + self.final[0, h] + self.final[1, h]

    def drain(self):
        for copy in self.copies:
            copy.wait_send()


class RingShare(RingSum):
    def __init__(self, place, axis, part, send, recv):
        super().__init__(place, axis, part, None, None, send, recv)

    def start(self):
        for h, device in ((0, self.right), (1, self.left), (1, self.right), (0, self.left)):
            part = self.part(self.me, h)
            self.copy(part, part, device)

    def pass_on(self):
        self.copies[0].wait_recv()
        part = self.part(self.prev, 0)
        self.copy(part, part, self.right)
        self.copies[1].wait_recv()
        part = self.part(self.next, 1)
        self.copy(part, part, self.left)

    def finish(self):
        for copy in self.copies[2:]:
            copy.wait_recv()


class DirectSum:
    def __init__(self, place, axis, part, got, send, recv):
        self.me = getattr(place, axis)
        self.part, self.got, self.copies = part, got, []
        for step in (2, 1, 3):
            chunk = part(lax.rem(self.me + step, 4))
            i = step - 1
            self.copies.append(remote(chunk, got.at[i], send.at[i], recv.at[i], place.device(axis, step)))

    def finish(self):
        for copy in self.copies:
            copy.wait_recv()
        return self.part(self.me)[...] + self.got[0] + self.got[1] + self.got[2]

    def drain(self):
        for copy in self.copies:
            copy.wait_send()


class DirectShare(DirectSum):
    def __init__(self, place, axis, part, send, recv):
        self.copies = []
        mine = part(getattr(place, axis))
        for step in (2, 1, 3):
            i = step - 1
            self.copies.append(remote(mine, mine, send.at[i], recv.at[i], place.device(axis, step)))

    def finish(self):
        for copy in self.copies:
            copy.wait_recv()


PLANS = (("x", "y"), ("y", "x"))


def all_sum_steps(place, scale, value, out, relay1, final1, sum1, got2, sum2, got3, send, recv):
    portions = [(s, p) for s in range(2) for p in range(2)]

    def lane(s, p, stage):
        i = (s * 2 + p) * 5 + stage
        return send.at[i], recv.at[i]

    opposite = place.device("z", 2)
    first, second, across, third, fourth = {}, {}, {}, {}, {}
    for s in range(2):
        for p in range(2):
            first[s, p] = RingSum(
                place,
                PLANS[p][0],
                lambda k, h, s=s, p=p: value.at[s, p, k, h],
                relay1.at[s, p],
                final1.at[s, p],
                *lane(s, p, 0),
            )
            first[s, p].start_far()
        for p in range(2):
            first[s, p].start_near()
        yield
    for ring in first.values():
        ring.pass_on()
    yield
    for s, p in portions:
        for h, half in enumerate(first[s, p].finish()):
            sum1[s, p, h] = half
        second[s, p] = DirectSum(
            place,
            PLANS[p][1],
            lambda k, s=s, p=p: sum1.at[s, p, k // 2, lax.rem(k, 2)],
            got2.at[s, p],
            *lane(s, p, 1),
        )
    yield
    for s, p in portions:
        sum2[s, p] = second[s, p].finish()
        i = (s * 2 + p) * 5 + 2
        across[s, p] = remote(sum2.at[s, p], got3.at[s, p], send.at[i, 0], recv.at[i, 0], opposite)
    yield
    for s, p in portions:
        across[s, p].wait_recv()
        outer, inner = (getattr(place, axis) for axis in PLANS[p])
        out[s, p, outer, inner // 2, lax.rem(inner, 2)] = (sum2[s, p] + got3[s, p]) * scale
        third[s, p] = DirectShare(
            place,
            PLANS[p][1],
            lambda k, s=s, p=p, outer=outer: out.at[s, p, outer, k // 2, lax.rem(k, 2)],
            *lane(s, p, 3),
        )
    yield
    for s, p in portions:
        third[s, p].finish()
        fourth[s, p] = RingShare(
            place, PLANS[p][0], lambda k, h, s=s, p=p: out.at[s, p, k, h], *lane(s, p, 4)
        )
        fourth[s, p].start()
    yield
    for ring in fourth.values():
        ring.pass_on()
    for ring in fourth.values():
        ring.finish()
    for group in (first, second, third, fourth):
        for ring in group.values():
            ring.drain()
    for copy in across.values():
        copy.wait_send()
    yield


FAN = [(y, z) for y in range(4) for z in range(2)][1:]


class SmallSum:
    def __init__(self, place, source, middle, got_row, got_rest, send, recv):
        self.source, self.middle, self.got_row, self.got_rest = source, middle, got_row, got_rest
        self.send, self.recv, self.rest = send, recv, self.fan(place)
        self.copies = [
            remote(source, got_row.at[i], send.at[i], recv.at[i], place.device("x", i + 1)) for i in range(3)
        ]

    @staticmethod
    def fan(place):
        devices = []
        for y, z in FAN:
            far = lax.rem(place.z + 2 * z, 4)
            devices.append(
                (lax.rem(far, 2) * 2 + place.core, (far // 2) * 16 + place.x * 4 + lax.rem(place.y + y, 4))
            )
        return devices

    def pass_on(self):
        for copy in self.copies:
            copy.wait_recv()
        self.middle[...] = self.source[...] + self.got_row[0] + self.got_row[1] + self.got_row[2]
        for n in range(7):
            i = 3 + n
            self.copies.append(
                remote(self.middle, self.got_rest.at[n], self.send.at[i], self.recv.at[i], self.rest[n])
            )

    def finish(self):
        for copy in self.copies[3:]:
            copy.wait_recv()
        total = self.middle[...]
        for n in range(7):
            total = total + self.got_rest[n]
        return total

    def drain(self):
        for copy in self.copies:
            copy.wait_send()


precise = lax.Precision.HIGHEST
N, B = 1024, 128


def spread_row(tile, row):
    return jnp.broadcast_to(tile[row : row + 1, :], (8, B))


def spread_column(tile, column):
    return jnp.broadcast_to(tile[:, column : column + 1], (8, B))


def invert_pair(a, b, c):
    det = a * c - b * b
    r = 1.0 / det
    return c * r, -b * r, a * r, det


def factor_rows(a, b, c, det, row0, row1):
    s = lax.rsqrt(a)
    first = row0 * s
    return first, (row1 - (b * s) * first) * (lax.rsqrt(det) * (a * s))


def leaf_steps(block, store):
    sub = lax.broadcasted_iota(jnp.int32, (8, B), 0)
    lane = lax.broadcasted_iota(jnp.int32, (8, B), 1)
    a = [block[8 * g : 8 * g + 8, :] for g in range(16)]
    w = [jnp.where(lane == sub + 8 * g, 1.0, 0.0) for g in range(16)]
    four = range(4)
    d = {(l, m): spread_row(spread_column(a[0], m), l) for l in four for m in range(l + 1)}
    finished = None
    for step in range(32):
        g, r, j = step // 2, 4 * (step % 2), 4 * step
        p, q, s, det = invert_pair(d[0, 0], d[1, 0], d[1, 1])
        k = [[p * d[n, 0] + q * d[n, 1], q * d[n, 0] + s * d[n, 1]] for n in (2, 3)]
        s00 = d[2, 2] - (d[2, 0] * k[0][0] + d[2, 1] * k[0][1])
        s10 = d[3, 2] - (d[3, 0] * k[0][0] + d[3, 1] * k[0][1])
        s11 = d[3, 3] - (d[3, 0] * k[1][0] + d[3, 1] * k[1][1])
        u, v, t, det2 = invert_pair(s00, s10, s11)
        rows = [spread_row(a[g], r + n) for n in four]
        wrows = [spread_row(w[g], r + n) for n in four]
        old = d
        if step < 31:
            ng, nr = (step + 1) // 2, 4 * ((step + 1) % 2)
            tile = a[ng]
            near = [spread_column(tile, j + n) for n in four]
            far = [spread_column(tile, j + 4 + n) for n in four]
            gap = [[spread_row(near[n], nr + l) for n in four] for l in four]
            ha = [[p * gap[l][0] + q * gap[l][1], q * gap[l][0] + s * gap[l][1]] for l in four]
            gb = [[gap[l][n] - (k[n - 2][0] * gap[l][0] + k[n - 2][1] * gap[l][1]) for n in (2, 3)] for l in four]
            hb = [[u * gb[l][0] + v * gb[l][1], v * gb[l][0] + t * gb[l][1]] for l in four]
            d = {}
            for l in four:
                for m in range(l + 1):
                    before = spread_row(far[m], nr + l) - (gap[l][0] * ha[m][0] + gap[l][1] * ha[m][1])
                    d[l, m] = before - (gb[l][0] * hb[m][0] + gb[l][1] * hb[m][1])

        def solve(r0, r1, r2, r3):
            r2 = r2 - (k[0][0] * r0 + k[0][1] * r1)
            r3 = r3 - (k[1][0] * r0 + k[1][1] * r1)
            x2, x3 = u * r2 + v * r3, v * r2 + t * r3
            x0 = (p * r0 + q * r1) - (k[0][0] * x2 + k[1][0] * x3)
            x1 = (q * r0 + s * r1) - (k[0][1] * x2 + k[1][1] * x3)
            return (x0, x1, x2, x3), r2, r3

        x, _, _ = solve(*rows)
        xw, w2, w3 = solve(*wrows)
        ready = factor_rows(old[0, 0], old[1, 0], old[1, 1], det, wrows[0], wrows[1])
        ready += factor_rows(s00, s10, s11, det2, w2, w3)
        if r == 0:
            finished = ready[0]
        for n, row in enumerate(ready):
            if r + n:
                finished = jnp.where(sub == r + n, row, finished)
        if r == 4:
            store(g, finished)
        for tile in range(g if r == 0 else g + 1, 16):
            mult = [spread_column(a[tile], j + n) for n in four]
            if tile == g:
                mult = [jnp.where(sub >= 4, m, 0.0) for m in mult]
            a[tile] = a[tile] - ((mult[0] * x[0] + mult[1] * x[1]) + (mult[2] * x[2] + mult[3] * x[3]))
            w[tile] = w[tile] - ((mult[0] * xw[0] + mult[1] * xw[1]) + (mult[2] * xw[2] + mult[3] * xw[3]))
        yield step


def three_parts(value):
    high = value.astype(jnp.bfloat16)
    rest = value - high.astype(jnp.float32)
    middle = rest.astype(jnp.bfloat16)
    return high, middle, (rest - middle.astype(jnp.float32)).astype(jnp.bfloat16)


def diagonal_block(block, diagonals, i):
    row = lax.broadcasted_iota(jnp.int32, (B, B), 0)
    lane = lax.broadcasted_iota(jnp.int32, (B, B), 1)
    if i % 2:
        strict = jnp.where(lane > row, block, 0.0)
        middle = jnp.broadcast_to(diagonals[i // 2 : i // 2 + 1, :], (B, B))
    else:
        strict = jnp.where(row > lane, block, 0.0)
        middle = block
    return strict + strict.T + jnp.where(row == lane, middle, 0.0)


def inverse_kernel(packed_in, diagonals, out, packed, whole, left, right, work, loads, stores):
    ahead = pltpu.make_async_copy(packed_in.at[:2], packed.at[:2], loads.at[0])
    ahead.start()
    rest = pltpu.make_async_copy(packed_in.at[2:], packed.at[2:], loads.at[1])
    rest.start()

    def store(g, tile):
        work[8 * g : 8 * g + 8, :] = tile

    def rows_of(i):
        return pl.ds(pl.multiple_of(i * B, B), B)

    ahead.wait()
    for _ in leaf_steps(diagonal_block(packed[SLOTS[0]], None, 0), store):
        pass
    rest.wait()
    for i in range(8):
        for j in range(i):
            block = packed[SLOTS[i, j]]
            whole[B * i : B * i + B, B * j : B * j + B] = block
            whole[B * j : B * j + B, B * i : B * i + B] = block.T
        whole[B * i : B * i + B, B * i : B * i + B] = diagonal_block(packed[SLOTS[i // 2]], diagonals, i)
    whole[N:, :] = jnp.zeros((B, N), jnp.float32)
    lane = lax.broadcasted_iota(jnp.int32, (B, B), 1)
    sub = lax.broadcasted_iota(jnp.int32, (B, B), 0)
    unit = jnp.where(lane == sub, 1.0, 0.0)

    def leave(k):
        return pltpu.make_async_copy(whole.at[rows_of(k)], out.at[rows_of(k)], stores.at[k])

    @pl.loop(0, 7)
    def _(k):
        here, below = rows_of(k), rows_of(k + 1)
        factor = work[...]
        first = dot(factor, whole[here, below], ((1,), (0,)))
        whole[below, below] -= dot(first, first, ((0,), (0,)))
        block = whole[below, below]
        whole[here, here] = unit

        def make_left(t):
            def job():
                there = rows_of(jnp.minimum(k + 1 + t, 8))
                high, middle, low = three_parts(dot(whole[there, here], factor, ((1,), (1,))))
                for n, part in enumerate((high, high, middle, middle, high, low)):
                    left[t * B : t * B + B, n * B : n * B + B] = part
                whole[there, here] = jnp.zeros((B, B), jnp.float32)

            return job

        def make_right(c):
            def job():
                columns = slice(256 * c, 256 * c + 256)
                panel = dot(factor, whole[here, columns], ((1,), (0,)))
                whole[here, columns] = panel
                high, middle, low = three_parts(panel)
                for n, part in enumerate((high, middle, high, middle, low, high)):
                    right[n * B : n * B + B, columns] = part

            return job

        def update(t, c):
            def job():
                columns = slice(256 * c, 256 * c + 256)
                there = rows_of(jnp.minimum(k + 1 + t, 8))
                term = jnp.dot(
                    left[t * B : t * B + B, :], right[:, columns], preferred_element_type=jnp.float32
                )
                if t == 0:
                    place = lax.broadcasted_iota(jnp.int32, (B, 256), 1) + 256 * c
                    term = jnp.where((place >= (k + 1) * B) & (place < (k + 2) * B), 0.0, term)
                whole[there, columns] -= term

            return job

        jobs = [make_right(c) for c in range(4)] + [make_left(t) for t in range(7)]
        jobs += [update(t, c) for t in range(7) for c in range(4)]
        done = 0
        for step in leaf_steps(block, store):
            upto = len(jobs) * (step + 1) // 32
            for job in jobs[done:upto]:
                job()
            done = upto
        whole[here, below] = jnp.zeros((B, B), jnp.float32)
        leave(k).start()

    whole[7 * B : N, 7 * B :] = unit
    whole[7 * B : N, :] = dot(work[...], whole[7 * B : N, :], ((1,), (0,)))
    leave(7).start()
    for k in range(8):
        leave(k).wait()


def factor_inverse(packed, diagonals):
    return pl.pallas_call(
        inverse_kernel,
        out_shape=jax.ShapeDtypeStruct((N, N), jnp.float32),
        in_specs=[ANY, VMEM],
        out_specs=ANY,
        scratch_shapes=[
            pltpu.VMEM((32, B, B), jnp.float32),
            pltpu.VMEM((N + B, N), jnp.float32),
            pltpu.VMEM((7 * B, 6 * B), jnp.bfloat16),
            pltpu.VMEM((6 * B, N), jnp.bfloat16),
            pltpu.VMEM((B, B), jnp.float32),
            pltpu.SemaphoreType.DMA((2,)),
            pltpu.SemaphoreType.DMA((8,)),
        ],
        compiler_params=pltpu.CompilerParams(vmem_limit_bytes=60 * 2**20),
    )(packed, diagonals)


def dot(a, b, over, precision=precise):
    return lax.dot_general(a, b, (over, ((), ())), precision=precision, preferred_element_type=jnp.float32)


def make_all_sum_scratch():
    floats = lambda *lead: pltpu.VMEM((2, 2, *lead, 64, 128), jnp.float32)
    return [
        floats(2, 2),
        floats(2, 2, 2),
        floats(2, 2),
        floats(3),
        floats(),
        floats(),
        pltpu.SemaphoreType.DMA((20, 6)),
        pltpu.SemaphoreType.DMA((20, 6)),
    ]


CUT = (2, 2, 4, 2, 2, 64, 128)


SLOTS = {}
for _i in range(8):
    for _j in range(_i):
        SLOTS[_i, _j] = len(SLOTS)
    if _i % 2:
        SLOTS[_i // 2] = len(SLOTS)


def put_block(value, slot, block):
    for half in range(2):
        n = 2 * SLOTS[slot] + half
        value[n // 32, n // 16 % 2, n // 4 % 4, n // 2 % 2, n % 2] = block[64 * half : 64 * half + 64, :]


def get_block(value, slot):
    parts = []
    for half in range(2):
        n = 2 * SLOTS[slot] + half
        parts.append(value[n // 32, n // 16 % 2, n // 4 % 4, n // 2 % 2, n % 2])
    return jnp.concatenate(parts, axis=0)


def small_scratch():
    floats = lambda *lead: pltpu.VMEM((*lead, 16, B), jnp.float32)
    return [floats(), floats(), floats(3), floats(7), pltpu.SemaphoreType.DMA((10,)), pltpu.SemaphoreType.DMA((10,))]


def front_kernel(
    hidden_in, proj_in, covariance, extra_out, centered_out, active_out,
    centered, active, hidden, proj, local_sum, row_sum, got_row, got_rest, odd, extra, *more_scratch,
):
    small, more_scratch = more_scratch[:5], more_scratch[5:]
    front_steps(
        hidden_in, proj_in, covariance, extra_out, centered_out, active_out, centered, active, hidden, proj,
        local_sum, row_sum, got_row, got_rest, odd, extra, small, *more_scratch,
    )


def front_steps(
    hidden_in, proj_in, covariance, extra_out, centered_out, active_out,
    centered, active, hidden, proj, local_sum, row_sum, got_row, got_rest, odd, extra, small, value, outgoing, arrived,
    loads, core_send, core_recv, sum_send, sum_recv, *scratch,
):
    place = Place()
    rows, width = centered.shape
    deep = proj.shape[1]
    copies = []
    for i in range(4):
        copies.append(pltpu.make_async_copy(hidden_in.at[:, i * deep : i * deep + deep], hidden.at[i], loads.at[0, i]))
        copies.append(pltpu.make_async_copy(proj_in.at[i * deep : i * deep + deep], proj.at[i], loads.at[1, i]))
    for copy in copies[:4]:
        copy.start()
    line = [place.device("x", step) for step in (1, 2, 3)]
    rest = SmallSum.fan(place)
    other = place.device(core=1 - place.core)
    barrier = pltpu.get_barrier_semaphore()
    for device in line + rest + [other]:
        pl.semaphore_signal(barrier, inc=1, device_id=device, device_id_type=MESH)
    for i in range(4):
        copies[2 * i].wait()
        copies[2 * i + 1].wait()
        for copy in copies[2 * i + 4 : 2 * i + 6]:
            copy.start()
        rows_here = jnp.maximum(hidden[i], 0.0)
        for c in range(0, width, 256):
            product = jnp.dot(rows_here, proj[i, :, c : c + 256], preferred_element_type=jnp.float32)
            if i:
                product = product + centered[:, c : c + 256]
            centered[:, c : c + 256] = product
            if i == 3:
                total = jnp.sum(product, axis=0, keepdims=True)
                for q in (0, 128):
                    local_sum[(c + q) // 128 : (c + q) // 128 + 1, :] = total[:, q : q + 128]
                centered[:, c : c + 256] = product - total / rows
    pl.semaphore_wait(barrier, len(line + rest) + 1)
    mean = SmallSum(place, local_sum, row_sum, got_row, got_rest, sum_send, sum_recv)
    for i in range(8):
        wide = dot(centered[:, B * i : B * i + B], centered[:, : B * (i + 1)], ((0,), (0,)))
        for j in range(i):
            put_block(value, (i, j), wide[:, B * j : B * j + B])
        if i % 2:
            odd[i // 2] = wide[:, B * i :]
        else:
            put_block(value, i // 2, wide[:, B * i :])
        if i == 4:
            mean.pass_on()
    total = mean.finish()
    count = rows * 32
    shift = local_sum[...] / rows - total / count
    upright = (shift * rows).T
    steps = all_sum_steps(place, 1.0 / count, value, covariance, *scratch)
    row = lax.broadcasted_iota(jnp.int32, (B, B), 0)
    lane = lax.broadcasted_iota(jnp.int32, (B, B), 1)
    extra[...] = jnp.zeros_like(extra)
    for i in range(8):
        column = jnp.broadcast_to(upright[:, i : i + 1], (B, B))
        for j in range(i):
            put_block(value, (i, j), get_block(value, (i, j)) + column * shift[j : j + 1, :])
        if i % 2:
            even = get_block(value, i // 2) + before
            block = odd[i // 2] + column * shift[i : i + 1, :]
            put_block(value, i // 2, jnp.where(row >= lane, even, block))
            extra[i // 2 : i // 2 + 1, :] = jnp.sum(jnp.where(row == lane, block, 0.0), axis=0, keepdims=True)
        before = column * shift[i : i + 1, :]
        if i == 5:
            next(steps)
    next(steps)
    diagonals = SmallSum(place, extra, *small)
    half = deep
    for part in range(2):
        kept = jnp.maximum(hidden[2 * part + 1 - place.core].astype(jnp.float32), 0.0)
        outgoing[:, part * half : part * half + half] = kept
    swap = remote(outgoing, arrived, core_send.at[0], core_recv.at[0], other)
    for i in range(8):
        centered[:, B * i : B * i + B] += shift[i : i + 1, :]
    results = [pltpu.make_async_copy(centered, centered_out, loads.at[0, 0])]
    results[0].start()

    def turn(q):
        part, inside = divmod(q * 256, half)
        mine = hidden[2 * part + place.core, :, inside : inside + 256].astype(jnp.float32)
        active[q * 256 : q * 256 + 256, :rows] = jnp.maximum(mine, 0.0).T.astype(active.dtype)

    def turn_arrived(q):
        active[q * 256 : q * 256 + 256, rows:] = arrived[:, q * 256 : q * 256 + 256].T.astype(active.dtype)

    work = [functools.partial(turn, q) for q in range(8)]
    for job in work[:4]:
        job()
    next(steps)
    for job in work[4:]:
        job()
    diagonals.pass_on()
    swap.wait_recv()
    later = [functools.partial(turn_arrived, q) for q in range(8)]
    for _ in steps:
        for job in later[:4]:
            job()
        later = later[4:]
    for job in later:
        job()
    results.append(pltpu.make_async_copy(active, active_out, loads.at[1, 0]))
    results[1].start()
    for copy in results:
        copy.wait()
    extra_out[...] = diagonals.finish() * (1.0 / count)
    swap.wait_send()
    mean.drain()
    diagonals.drain()


def front(hidden, proj):
    rows, depth = hidden.shape
    width = proj.shape[1]
    f32, bf16 = jnp.float32, jnp.bfloat16
    return pl.pallas_call(
        front_kernel,
        out_shape=(
            jax.ShapeDtypeStruct(CUT, f32),
            jax.ShapeDtypeStruct((16, B), f32),
            jax.ShapeDtypeStruct((rows, width), f32),
            jax.ShapeDtypeStruct((depth // 2, 2 * rows), bf16),
        ),
        in_specs=[ANY, ANY],
        out_specs=(VMEM, VMEM, ANY, ANY),
        scratch_shapes=[
            pltpu.VMEM((rows, width), f32),
            pltpu.VMEM((depth // 2, 2 * rows), bf16),
            pltpu.VMEM((4, rows, depth // 4), bf16),
            pltpu.VMEM((4, depth // 4, width), bf16),
            pltpu.VMEM((8, B), f32),
            pltpu.VMEM((8, B), f32),
            pltpu.VMEM((3, 8, B), f32),
            pltpu.VMEM((7, 8, B), f32),
            pltpu.VMEM((4, B, B), f32),
            *small_scratch(),
            pltpu.VMEM(CUT, f32),
            pltpu.VMEM((rows, depth // 2), f32),
            pltpu.VMEM((rows, depth // 2), f32),
            pltpu.SemaphoreType.DMA((2, 4)),
            pltpu.SemaphoreType.DMA((1,)),
            pltpu.SemaphoreType.DMA((1,)),
            pltpu.SemaphoreType.DMA((10,)),
            pltpu.SemaphoreType.DMA((10,)),
            *make_all_sum_scratch(),
        ],
        compiler_params=pltpu.CompilerParams(
            collective_id=0, has_side_effects=True, vmem_limit_bytes=60 * 2**20
        ),
    )(hidden, proj)


ORDERS = (("x", "y", "z"), ("y", "z", "x"), ("z", "x", "y"))
WIDTHS = (384, 384, 256)


def three_terms(ref, value, block, columns, weight):
    high = value.astype(jnp.bfloat16)
    low = (value - high.astype(jnp.float32)).astype(jnp.bfloat16)
    for n, part in enumerate((high, low, high) if weight else (high, high, low)):
        if weight:
            start = block // 2 * 768 + n * 256 + block % 2 * B
            ref[start : start + value.shape[0], columns] = part
        else:
            ref[:, block * 768 + n * 256 : block * 768 + n * 256 + 256] = part


def back_kernel(
    centered_in, inverse_in, pairing, scale, proj_in, active_in, out, grad_hidden,
    centered, inverse, white, grad_white, there, value, packed, left, right, proj, active, grad_there, grad, staged,
    swap_send, swap_recv, core_send, core_recv, local, stream, drop, early, extra, *scratch,
):
    small, sum_scratch, scratch = scratch[:5], scratch[5:13], scratch[13:]
    send, recv = scratch[-2:]
    place = Place()
    rows, width = white.shape
    count = rows * 32
    loads = []
    for i in range(4):
        part = slice(256 * i, 256 * i + 256)
        loads.append(pltpu.make_async_copy(centered_in.at[:, part], centered.at[:, part], early.at[0, i]))
        loads.append(pltpu.make_async_copy(inverse_in.at[part], inverse.at[part], early.at[1, i]))
    for copy in loads[:4]:
        copy.start()
    load_active = pltpu.make_async_copy(active_in, active, local.at[0])

    def load_proj(t):
        slot = lax.rem(t, 2)
        start = pl.multiple_of(t * 512, 512)
        return pltpu.make_async_copy(proj_in.at[pl.ds(start, 512)], proj.at[slot], stream.at[slot])

    other = place.device(core=1 - place.core)
    peers = [place.device(axis, step) for axis in "xyz" for step in (1, 2, 3)] + [other]
    peers += [device for device, (y, z) in zip(SmallSum.fan(place), FAN) if y and z]
    barrier = pltpu.get_barrier_semaphore()
    for device in peers:
        pl.semaphore_signal(barrier, inc=1, device_id=device, device_id_type=MESH)

    swaps = []
    squares = jnp.zeros((rows, 1), jnp.float32)
    for i in range(4):
        columns = slice(256 * i, 256 * i + 256)
        loads[2 * i].wait()
        loads[2 * i + 1].wait()
        for copy in loads[2 * i + 4 : 2 * i + 6]:
            copy.start()
        tile = dot(centered[:, : 256 * i + 256], inverse[columns, : 256 * i + 256], ((1,), (1,)))
        white[:, columns] = tile
        if i == 1:
            pl.semaphore_wait(barrier, len(peers))
        for n in {1: (0, 1), 2: (2,), 3: (3,)}.get(i, ()):
            part = slice(256 * n, 256 * n + 256)
            swaps.append(remote(white.at[:, part], there.at[:, part], swap_send.at[n], swap_recv.at[n], other))
        squares = squares + jnp.sum(tile * tile, axis=1, keepdims=True)
    load_active.start()
    load_proj(0).start()
    load_proj(1).start()
    over = 1.0 / jnp.sqrt(squares + 1e-06)
    lane = lax.broadcasted_iota(jnp.int32, (rows, rows), 1)
    chosen = jnp.where(pairing[...] == lane, 1.0, 0.0).astype(jnp.bfloat16)
    squares = jnp.zeros((rows, 1), jnp.float32)
    for i in range(4):
        swaps[i].wait_recv()
        tile = there[:, 256 * i : 256 * i + 256]
        squares = squares + jnp.sum(tile * tile, axis=1, keepdims=True)
    over_there = 1.0 / jnp.sqrt(squares + 1e-06)
    factor = 4.0 * scale[0, 0]
    along = jnp.zeros((rows, 1), jnp.float32)
    for i in range(4):
        columns = slice(256 * i, 256 * i + 256)
        partner = [
            jnp.dot(chosen, part, preferred_element_type=jnp.float32)
            for part in three_parts(there[:, columns] * over_there)
        ]
        normals = white[:, columns] * over
        change = factor * (normals - ((partner[2] + partner[1]) + partner[0]))
        grad_white[:, columns] = change
        along = along + jnp.sum(normals * change, axis=1, keepdims=True)
    totals = []
    for i in range(4):
        columns = slice(256 * i, 256 * i + 256)
        change = (grad_white[:, columns] - white[:, columns] * (over * along)) * over
        grad_white[:, columns] = change
        total = jnp.sum(change, axis=0, keepdims=True)
        totals += [total[:, :B], total[:, B:]]

    row = lax.broadcasted_iota(jnp.int32, (B, B), 0)
    lane = lax.broadcasted_iota(jnp.int32, (B, B), 1)
    steps = all_sum_steps(place, 1.0, value, packed, *sum_scratch)
    extra[...] = jnp.zeros_like(extra)
    for i in range(8):
        wide = dot(grad_white[:, B * i : B * i + B], white[:, : B * (i + 1)], ((0,), (0,)), lax.Precision.HIGH)
        for j in range(i):
            put_block(value, (i, j), wide[:, B * j : B * j + B])
        block = wide[:, B * i :]
        extra[8 + i : 9 + i, :] = totals[i]
        if i % 2:
            put_block(value, i // 2, jnp.where(row >= lane, even, block.T))
            extra[i // 2 : i // 2 + 1, :] = jnp.sum(jnp.where(row == lane, block, 0.0), axis=0, keepdims=True)
        even = block
        if i == 5:
            next(steps)
    next(steps)
    extras = SmallSum(place, extra, *small)
    next(steps)
    extras.pass_on()
    for i in range(4):
        three_terms(left, white[:, 256 * i : 256 * i + 256], i, None, False)
    for swap in swaps:
        swap.wait_send()
    for _ in steps:
        pass
    extra_total = extras.finish()
    extras.drain()

    for c in range(4):
        for q in (0, 1):
            j, at = 2 * c + q, slice(B * q, B * q + B)
            for i in range(8):
                if i > j:
                    block = get_block(packed, (i, j))
                elif i < j:
                    block = get_block(packed, (j, i)).T
                else:
                    grad_white[:, B * i : B * i + B] -= extra_total[8 + i : 9 + i, :] / count
                    block = diagonal_block(get_block(packed, i // 2), extra_total, i)
                three_terms(right, block, i, at, True)
        grad_white[:, 256 * c : 256 * c + 256] -= (
            jnp.dot(left[...], right[...], preferred_element_type=jnp.float32) / count
        )
    for i in range(4):
        three_terms(left, grad_white[:, 256 * i : 256 * i + 256], i, None, False)
    grads = []

    def gradient(c):
        columns = slice(256 * c, 256 * c + 256)
        for i in range(2 * c, 8):
            three_terms(right, inverse[B * i : B * i + B, columns], i, slice(None), True)
        tile = jnp.dot(left[:, 768 * c :], right[768 * c :, :], preferred_element_type=jnp.float32)
        white[:, columns] = tile
        grad[:rows, columns] = tile.astype(grad.dtype)
        grads.append(
            remote(white.at[:, columns], grad_there.at[:, columns], core_send.at[c], core_recv.at[c], other)
        )

    def gradient_there(c):
        columns = slice(256 * c, 256 * c + 256)
        grads[c].wait_recv()
        grad[rows:, columns] = grad_there[:, columns].astype(grad.dtype)

    parts, relays, finals, sums = [], [], [], []
    for p in range(3):
        parts.append(scratch[8 * p])
        relays.append(scratch[8 * p + 1 : 8 * p + 3])
        finals.append(scratch[8 * p + 3 : 8 * p + 6])
        sums.append(scratch[8 * p + 6 : 8 * p + 8])

    def multiply(p, k):
        begin = sum(WIDTHS[:p])
        high, low = k // 2, lax.rem(k, 2)
        if p == 0:
            left = active[:, :, k]
        elif p == 1:
            left = active[:, :, :, k]
        else:
            left = active[low, high]
        product = jnp.dot(
            left.reshape(512, 2 * rows), grad[:, begin : begin + WIDTHS[p]], preferred_element_type=jnp.float32
        )
        for n in range(16):
            block = product[32 * n : 32 * n + 32]
            if p == 0:
                parts[p][k, n % 4 // 2, n % 2, n // 4 % 2, n // 8] = block
            elif p == 1:
                parts[p][k, n // 4 % 2, n // 8, n % 4 // 2, n % 2] = block
            else:
                parts[p][k, n // 8, n // 4 % 2, n % 4 // 2, n % 2] = block

    def hidden_tile(t):
        slot = lax.rem(t, 2)
        load_proj(t).wait()
        product = lax.dot_general(
            grad[:rows, :], proj[slot], (((1,), (1,)), ((), ())), preferred_element_type=jnp.float32
        )

        def leave(t):
            columns = pl.ds(pl.multiple_of(t * 512, 512), 512)
            return pltpu.make_async_copy(staged.at[slot], grad_hidden.at[:, columns], drop.at[slot])

        @pl.when(t >= 2)
        def _():
            leave(t - 2).wait()

        staged[slot] = product.astype(grad_hidden.dtype)
        leave(t).start()

        @pl.when(t < 6)
        def _():
            load_proj(t + 2).start()

        @pl.when(t == 7)
        def _():
            leave(t).wait()
            pltpu.make_async_copy(
                staged.at[1 - slot], grad_hidden.at[:, pl.ds(6 * 512, 512)], drop.at[1 - slot]
            ).wait()

    first, second, third = {}, {}, {}

    def begin(p):
        i = p * 3
        first[p] = ring = RingSum(
            place, ORDERS[p][0], lambda k, h: parts[p].at[k, h], relays[p][0], finals[p][0], send.at[i], recv.at[i]
        )
        multiply(p, ring.far)
        ring.start_far()
        multiply(p, ring.next)
        multiply(p, ring.prev)
        ring.start_near()

    for c in (0, 1, 2):
        gradient(c)
    load_active.wait()
    gradient_there(0)
    gradient_there(1)
    begin(0)
    gradient(3)
    gradient_there(2)
    begin(1)
    gradient_there(3)
    begin(2)
    for p in range(3):
        multiply(p, first[p].me)
    pl.loop(0, 2)(hidden_tile)
    for p in range(3):
        first[p].pass_on()
    pl.loop(2, 8)(hidden_tile)
    for p in range(3):
        for h, half in enumerate(first[p].finish()):
            sums[p][0][h] = half
        i = p * 3 + 1
        second[p] = RingSum(
            place,
            ORDERS[p][1],
            lambda k, h, p=p: sums[p][0].at[k // 2, lax.rem(k, 2), h],
            relays[p][1],
            finals[p][1],
            send.at[i],
            recv.at[i],
        )
        second[p].start_far()
        second[p].start_near()
    for p in range(3):
        second[p].pass_on()
    for p in range(3):
        for h, half in enumerate(second[p].finish()):
            sums[p][1][h] = half
        i = p * 3 + 2
        third[p] = DirectSum(
            place,
            ORDERS[p][2],
            lambda k, p=p: sums[p][1].at[k // 2, lax.rem(k, 2)],
            finals[p][2],
            send.at[i],
            recv.at[i],
        )
    for p in range(3):
        start = sum(WIDTHS[:p])
        out[:, start : start + WIDTHS[p]] = third[p].finish().astype(out.dtype)
    for group in (first, second, third):
        for ring in group.values():
            ring.drain()
    for swap in grads:
        swap.wait_send()


def back(centered, inverse, pairing, scale, proj, active):
    rows, width = centered.shape
    depth = proj.shape[0]
    bf16, f32 = jnp.bfloat16, jnp.float32
    cut = (2, 2, 4, 4, 32, 2 * rows)
    scratch = [
        pltpu.VMEM((rows, width), f32),
        pltpu.VMEM((width, width), f32),
        pltpu.VMEM((rows, width), f32),
        pltpu.VMEM((rows, width), f32),
        pltpu.VMEM((rows, width), f32),
        pltpu.VMEM(CUT, f32),
        pltpu.VMEM(CUT, f32),
        pltpu.VMEM((rows, 3 * width), bf16),
        pltpu.VMEM((3 * width, 256), bf16),
        pltpu.VMEM((2, 512, width), bf16),
        pltpu.VMEM(cut, bf16),
        pltpu.VMEM((rows, width), f32),
        pltpu.VMEM((2 * rows, width), bf16),
        pltpu.VMEM((2, rows, 512), bf16),
        pltpu.SemaphoreType.DMA((4,)),
        pltpu.SemaphoreType.DMA((4,)),
        pltpu.SemaphoreType.DMA((4,)),
        pltpu.SemaphoreType.DMA((4,)),
        pltpu.SemaphoreType.DMA((1,)),
        pltpu.SemaphoreType.DMA((2,)),
        pltpu.SemaphoreType.DMA((2,)),
        pltpu.SemaphoreType.DMA((2, 4)),
        *small_scratch(),
        *make_all_sum_scratch(),
    ]
    for columns in WIDTHS:
        scratch += [
            pltpu.VMEM((*lead, 32, columns), f32)
            for lead in [
                (4, 2, 2, 2, 2),
                (2, 2, 2, 2),
                (2, 2),
                (2, 2, 2, 2, 2),
                (2, 2, 2),
                (3,),
                (2, 2, 2, 2),
                (2, 2),
            ]
        ]
    scratch += [pltpu.SemaphoreType.DMA((9, 6)), pltpu.SemaphoreType.DMA((9, 6))]
    return pl.pallas_call(
        back_kernel,
        out_shape=(jax.ShapeDtypeStruct((32, width), bf16), jax.ShapeDtypeStruct((rows, depth), bf16)),
        in_specs=[ANY, ANY, VMEM, pl.BlockSpec(memory_space=pltpu.SMEM), ANY, ANY],
        out_specs=(VMEM, ANY),
        scratch_shapes=scratch,
        compiler_params=pltpu.CompilerParams(
            collective_id=1, has_side_effects=True, vmem_limit_bytes=60 * 2**20
        ),
    )(centered, inverse, pairing, scale, proj, active.reshape(cut))


def local(hidden, w_proj, pairing, loss_scale):
    rows = hidden.shape[0]
    covariance, diagonals, centered, active = front(hidden, w_proj)
    inverse = factor_inverse(covariance.reshape(32, B, B), diagonals)
    partner = (pairing - lax.axis_index("dp") * rows).reshape(rows, 1)
    grad_weight, grad_active = back(centered, inverse, partner, loss_scale.reshape(1, 1), w_proj, active)
    return (jnp.where(hidden > 0, grad_active, 0), grad_weight)


def solution(mesh):
    return jax.shard_map(
        local,
        mesh=mesh,
        in_specs=(P(("grp", "dp"), None), P(), P(("grp", "dp")), P()),
        out_specs=(P(("grp", "dp"), None), P(("grp", "dp"), None)),
        check_vma=False,
    )
```
